32 devices in a mesh: wide: 8 (over y, x, core), narrow: 4 (over z).
Axes of the slice: x: 2, y: 2, z: 4, core: 2. Of those that a mesh axis runs over, the one named last changes fastest.
Arguments:
- tokens: bfloat16 [32, 256, 2048], P(('wide', 'narrow')), may hold values from -6 to 6
- doc_lengths: int32 [32, 4], P(('wide', 'narrow')), may hold values from 1 to 128, 256 in all within a row
- gain_attn: bfloat16 [2048], P(('wide', 'narrow')), may hold values from 0.25 to 1.75
- w_query: bfloat16 [2048, 2048], P(('wide', 'narrow')), may hold values from -0.125 to 0.125
- w_key: bfloat16 [2048, 2048], P(('wide', 'narrow')), may hold values from -0.125 to 0.125
- w_value: bfloat16 [2048, 2048], P(('wide', 'narrow')), may hold values from -0.125 to 0.125
- w_beta: bfloat16 [2048, 16], P(('wide', 'narrow')), may hold values from -0.125 to 0.125
- conv_query: bfloat16 [4, 2048], P(None, ('wide', 'narrow')), may hold values from -3 to 3
- conv_key: bfloat16 [4, 2048], P(None, ('wide', 'narrow')), may hold values from -3 to 3
- conv_value: bfloat16 [4, 2048], P(None, ('wide', 'narrow')), may hold values from -3 to 3
- gain_head: bfloat16 [128], replicated, may hold values from 0.25 to 1.75
- w_out: bfloat16 [2048, 2048], P(('wide', 'narrow')), may hold values from -0.125 to 0.125
- gain_ffn: bfloat16 [2048], P(('wide', 'narrow')), may hold values from 0.25 to 1.75
- w_gate: bfloat16 [2048, 5632], P(('wide', 'narrow')), may hold values from -0.125 to 0.125
- w_up: bfloat16 [2048, 5632], P(('wide', 'narrow')), may hold values from -0.125 to 0.125
- w_down: bfloat16 [5632, 2048], P(('wide', 'narrow')), may hold values from -0.078125 to 0.078125
- cotangent: bfloat16 [32, 256, 2048], P(('wide', 'narrow')), may hold values from -6 to 6
Outputs:
- output: bfloat16 [32, 256, 2048], P(('wide', 'narrow'))
- grad_input: bfloat16 [32, 256, 2048], P(('wide', 'narrow'))
- grad_gain_attn: float32 [2048], P(('wide', 'narrow'))
- grad_w_query: float32 [2048, 2048], P(('wide', 'narrow'))
- grad_w_key: float32 [2048, 2048], P(('wide', 'narrow'))
- grad_w_value: float32 [2048, 2048], P(('wide', 'narrow'))
- grad_w_beta: float32 [2048, 16], P(('wide', 'narrow'))
- grad_conv_query: float32 [4, 2048], P(None, ('wide', 'narrow'))
- grad_conv_key: float32 [4, 2048], P(None, ('wide', 'narrow'))
- grad_conv_value: float32 [4, 2048], P(None, ('wide', 'narrow'))
- grad_gain_head: float32 [128], replicated
- grad_w_out: float32 [2048, 2048], P(('wide', 'narrow'))
- grad_gain_ffn: float32 [2048], P(('wide', 'narrow'))
- grad_w_gate: float32 [2048, 5632], P(('wide', 'narrow'))
- grad_w_up: float32 [2048, 5632], P(('wide', 'narrow'))
- grad_w_down: float32 [5632, 2048], P(('wide', 'narrow'))
The draws below stay inside these ranges and needn't reach their ends.
Inputs may be any that keep to these rules, and one draw needn't show every extreme that they name: `doc_lengths`: each row holds the lengths of 4 documents that fill the sequence, the longest exactly 128.
All inputs are finite; a program needn't handle non-finite values.
Results may differ from the reference program's by a relative error of at most 0.012.
The reference program's roundings to bfloat16 on the way count: a program that leaves them out, or rounds other values in their place, can miss the bound.
Values may be sent and summed in bfloat16 or wider, within the bound.
No kernel may reach another device: no remote copies, remote signals or barrier semaphores. Data moves between devices by JAX's collectives and lax.ppermute only.
A program may use at most 448 MiB of HBM per device.

```python
import math
import jax
import jax.numpy as jnp
import numpy as np
from jax import lax

D = 2048
HEADS = 16
DK = 128
FF = 5632
CONV = 4
SPAN = 64
NDOCS = 4
SEQ = 256
BATCH = 32


def spiked(values, rng, source, target, parts, factor):
    owner, partner = [(jnp.arange(values.shape[position]) // (values.shape[position] // parts)).reshape([-1 if axis == position else 1 for axis in range(values.ndim)]) for position in (source, target)]
    chosen = jax.random.permutation(rng, parts)[partner]
    strong = (owner == chosen) | (owner == (partner + parts // 2) % parts)
    return jnp.where(strong, factor * values, values)


def level_of(rng, dims, shards, smallest, high):
    def one(dim, blocks):
        draws = jax.random.uniform(jax.random.fold_in(jax.random.fold_in(rng, 6), dim), (blocks,), jnp.float32, smallest / len(shards), high / len(shards))
        return jnp.repeat(jnp.exp(draws), dims[dim] // blocks).reshape((-1,) + (1,) * (len(dims) - dim - 1))

    level = one(*shards[0])
    for cut in shards[1:]:
        level = level * one(*cut)
    return level


def split_up(number_of, total, bound, slope):
    loads = [(1 << 20) // math.isqrt(standing ** slope) + 1 for standing in range(2, number_of + 1)]
    rest, counts = total - bound - (number_of - 1), [1] * (number_of - 1)
    while rest > 0:
        candidates = [i for i in range(number_of - 1) if counts[i] < bound]
        whole, remaining = sum([loads[i] for i in candidates]), rest
        for i in candidates:
            addition = min(bound - counts[i], max(1, remaining * loads[i] // whole), rest)
            counts[i] = counts[i] + addition
            rest = rest - addition
    return np.array([bound] + counts)


def ragged(rng, amount, total, most, slope):
    if amount == 2:
        one = jax.random.randint(rng, (), max(1, total - most), min(most, total - 1) + 1)
        return jnp.stack([one, total - one])
    sizes = jnp.asarray(split_up(amount, total, most, slope), jnp.int32)
    couples = (amount - 1) // 2
    donor, taker = sizes[1:1 + 2 * couples:2], sizes[2:2 + 2 * couples:2]
    room = jnp.minimum(donor - 1, most - taker)
    passed = jax.random.randint(jax.random.fold_in(rng, 1), (couples,), 0, 1 << 20) % (room + 1)
    sizes = sizes.at[1:1 + 2 * couples:2].set(donor - passed).at[2:2 + 2 * couples:2].set(taker + passed)
    return sizes[jax.random.permutation(jax.random.fold_in(rng, 2), amount)]


def bell_draw(stream_key, dims, scale, most, pieces=(), kind=jnp.bfloat16):
    drawn = scale * jax.random.normal(stream_key, dims, jnp.float32)
    if pieces:
        drawn = drawn * level_of(stream_key, dims, pieces, -0.22, 0.18)
    return jnp.clip(drawn, -most, most).astype(kind)


def noise_with(key, dims, scale, reach, cuts, heavy, kind=jnp.bfloat16):
    drawn = scale * jax.random.normal(key, dims, jnp.float32)
    if cuts:
        drawn = drawn * level_of(key, dims, cuts, -0.22, 0.18)
    return jnp.clip(spiked(drawn, jax.random.fold_in(key, 3), *heavy), -reach, reach).astype(kind)


def setup_inputs(seed: int = 0) -> dict:
    seeds = jax.random.split(jax.random.key(seed), 18)
    return {
        "tokens": noise_with(seeds[0], (BATCH, SEQ, D), 1.0, 6.0, ((0, 32),), (0, 2, 32, 2.75)),
        "doc_lengths": jax.vmap(lambda own: ragged(own, NDOCS, SEQ, SEQ // 2, 0))(jax.random.split(seeds[1], BATCH)).reshape((BATCH, NDOCS)).astype(jnp.int32),
        "gain_attn": jnp.clip(1.0 + 0.15 * jax.random.normal(seeds[2], (D,), jnp.float32), 0.25, 1.75).astype(jnp.bfloat16),
        "w_query": bell_draw(seeds[3], (D, D), D ** -0.5, 0.125, ((0, 32),)),
        "w_key": bell_draw(seeds[4], (D, D), D ** -0.5, 0.125, ((0, 32),)),
        "w_value": bell_draw(seeds[5], (D, D), D ** -0.5, 0.125, ((0, 32),)),
        "w_beta": bell_draw(seeds[6], (D, HEADS), D ** -0.5, 0.125, ((0, 32),)),
        "conv_query": bell_draw(seeds[7], (CONV, D), CONV ** -0.5, 3.0, ((1, 32),)),
        "conv_key": bell_draw(seeds[8], (CONV, D), CONV ** -0.5, 3.0, ((1, 32),)),
        "conv_value": bell_draw(seeds[9], (CONV, D), CONV ** -0.5, 3.0, ((1, 32),)),
        "gain_head": jnp.clip(1.0 + 0.15 * jax.random.normal(seeds[10], (DK,), jnp.float32), 0.25, 1.75).astype(jnp.bfloat16),
        "w_out": bell_draw(seeds[11], (D, D), D ** -0.5, 0.125, ((0, 32),)),
        "gain_ffn": jnp.clip(1.0 + 0.15 * jax.random.normal(seeds[12], (D,), jnp.float32), 0.25, 1.75).astype(jnp.bfloat16),
        "w_gate": bell_draw(seeds[13], (D, FF), D ** -0.5, 0.125, ((0, 32),)),
        "w_up": bell_draw(seeds[14], (D, FF), D ** -0.5, 0.125, ((0, 32),)),
        "w_down": bell_draw(seeds[15], (FF, D), FF ** -0.5, 0.078125, ((0, 32),)),
        "cotangent": noise_with(seeds[16], (BATCH, SEQ, D), 1.0, 6.0, ((0, 32),), (0, 2, 32, 2.75)),
    }


PRECISION_LEVEL = lax.Precision.HIGHEST

@jax.custom_vjp
def low(v):
    return lax.optimization_barrier(v.astype(jnp.bfloat16)).astype(jnp.float32)

@jax.custom_vjp
def low_back(v):
    return v

def low_keep(v):
    return (low(v), None)

def low_pass(kept, grad):
    return (grad,)

def back_keep(v):
    return (v, None)

def back_low(kept, grad):
    return (low(grad),)
low.defvjp(low_keep, low_pass)
low_back.defvjp(back_keep, back_low)

def multiply(left, right):
    return jnp.dot(left.astype(jnp.float32), right.astype(jnp.float32), precision=PRECISION_LEVEL, preferred_element_type=jnp.float32)

def scale_rows(values, gain):
    return values * lax.rsqrt(lax.optimization_barrier(jnp.mean(values * values, axis=-1, keepdims=True)) + 1e-06) * gain

def head_norm(output, gain):
    normed = output * lax.rsqrt(lax.optimization_barrier(jnp.mean(output * output, axis=-1, keepdims=True)) + 1e-05) * gain
    return normed.reshape(normed.shape[:-2] + (normed.shape[-2] * normed.shape[-1],))

def doc_ids(lengths, length):
    ends = jnp.cumsum(lengths.astype(jnp.int32))
    places = jnp.arange(length, dtype=jnp.int32)
    return lax.optimization_barrier(jnp.sum((places[:, None] >= ends[None, :-1]).astype(jnp.int32), axis=1)).astype(jnp.int32)

def short_conv(projected, weight, docs):
    total = projected * weight[0]
    for offset in range(1, weight.shape[0]):
        moved = jnp.concatenate([jnp.zeros((offset, projected.shape[1]), projected.dtype), projected[:-offset]], axis=0)
        moved_doc = jnp.concatenate([jnp.full((offset,), -1, jnp.int32), docs[:-offset]])
        keeping_factor = (moved_doc == docs).astype(projected.dtype)
        total = total + moved * weight[offset] * keeping_factor[:, None]
    return total

def prepare(query_proj, key_proj, value_proj, beta_logit, conv_q, conv_k, conv_v, docs):
    heads = beta_logit.shape[-1]
    length = query_proj.shape[0]

    def unit(values):
        values = values.reshape(length, heads, -1)
        return values * lax.rsqrt(lax.optimization_barrier(jnp.sum(values * values, axis=-1, keepdims=True)) + 1e-06)
    query = unit(jax.nn.silu(short_conv(query_proj, conv_q, docs)))
    key = unit(jax.nn.silu(short_conv(key_proj, conv_k, docs)))
    value = jax.nn.silu(short_conv(value_proj, conv_v, docs)).reshape(length, heads, -1)
    return (query, key, value, jax.nn.sigmoid(beta_logit))

def core(query, key, value, beta, docs):
    length, heads, width = query.shape
    count = length // SPAN

    def blocks(values):
        return values.reshape(count, SPAN, heads, -1).transpose(0, 2, 1, 3)
    beta_blocks = beta.reshape(count, SPAN, heads).transpose(0, 2, 1)
    doc_blocks = docs.reshape(count, SPAN)
    before = jnp.concatenate([jnp.full((1,), -1, jnp.int32), doc_blocks[:-1, -1]])
    identity = jnp.eye(SPAN, dtype=query.dtype)
    strict = jnp.tril(jnp.ones((SPAN, SPAN), query.dtype), -1)
    causal = jnp.tril(jnp.ones((SPAN, SPAN), query.dtype))

    def step(running_state, inputs):
        current_query, current_key, value_now, beta_now, doc_now, doc_before = inputs
        same = (doc_now[:, None] == doc_now[None, :]).astype(query.dtype)
        inner = jnp.einsum('hik,hjk->hij', current_key, current_key, precision=PRECISION_LEVEL)
        lower = identity + beta_now[:, :, None] * inner * (same * strict)
        stacked = beta_now[:, :, None] * jnp.concatenate([current_key, value_now], axis=-1)
        solved = jax.scipy.linalg.solve_triangular(lower, stacked, lower=True, unit_diagonal=True)
        weighted_keys = solved[..., :width]
        weighted_values = solved[..., width:]
        carried_over = (doc_now == doc_before).astype(query.dtype)[None, :, None]
        ending_position = (doc_now == doc_now[-1]).astype(query.dtype)[None, :, None]
        keeping_factor = (doc_now[-1] == doc_before).astype(query.dtype)
        fixed_value = weighted_values - carried_over * jnp.einsum('tlf,tfy->tly', weighted_keys, running_state, precision=PRECISION_LEVEL)
        scores = jnp.einsum('hik,hjk->hij', current_query, current_key, precision=PRECISION_LEVEL) * (same * causal)
        output = carried_over * jnp.einsum('tlf,tfy->tly', current_query, running_state, precision=PRECISION_LEVEL)
        output = output + jnp.einsum('hij,hjv->hiv', scores, fixed_value, precision=PRECISION_LEVEL)
        running_state = keeping_factor * running_state + jnp.einsum('ewd,ewy->edy', current_key * ending_position, fixed_value, precision=PRECISION_LEVEL)
        return (running_state, output)
    initial = jnp.zeros((heads, width, value.shape[-1]), query.dtype)
    final, outputs = lax.scan(jax.checkpoint(step), initial, (blocks(query), blocks(key), blocks(value), beta_blocks, doc_blocks, before))
    return outputs.transpose(0, 2, 1, 3).reshape(length, heads, -1)

def layer(params, inputs, docs):
    gain_one, query_w, key_w, value_w, beta_w, conv_q, conv_k, conv_v, gain_mid, out_w, gain_two, gate_w, up_w, down_w = params
    count, length, width = inputs.shape
    rows_in = inputs.reshape(count * length, width)
    activated = low(scale_rows(rows_in, gain_one))
    query_proj = low_back(multiply(activated, query_w)).reshape(count, length, width)
    key_proj = low_back(multiply(activated, key_w)).reshape(count, length, width)
    value_proj = low_back(multiply(activated, value_w)).reshape(count, length, width)
    beta_logit = low_back(multiply(activated, beta_w)).reshape(count, length, -1)
    query, key, value, beta = jax.vmap(prepare, in_axes=(0, 0, 0, 0, None, None, None, 0))(query_proj, key_proj, value_proj, beta_logit, conv_q, conv_k, conv_v, docs)
    mixed = jax.vmap(core)(low(query), low(key), low(value), beta, docs)
    head_low = low(head_norm(mixed, gain_mid)).reshape(count * length, width)
    middle = rows_in + low_back(multiply(head_low, out_w))
    second = low(scale_rows(middle, gain_two))
    gate_pre = low_back(multiply(second, gate_w))
    up_pre = low_back(multiply(second, up_w))
    hidden = low(jax.nn.silu(gate_pre) * up_pre)
    return (middle + multiply(hidden, down_w)).reshape(count, length, width)

def reference(tokens, doc_lengths, gain_attn, w_query, w_key, w_value, w_beta, conv_query, conv_key, conv_value, gain_head, w_out, gain_ffn, w_gate, w_up, w_down, cotangent):
    params = tuple((weight.astype(jnp.float32) for weight in (gain_attn, w_query, w_key, w_value, w_beta, conv_query, conv_key, conv_value, gain_head, w_out, gain_ffn, w_gate, w_up, w_down)))
    docs = jax.vmap(lambda lengths: doc_ids(lengths, SEQ))(doc_lengths)
    groups = tokens.shape[0] // 8
    inputs = tokens.astype(jnp.float32).reshape(groups, 8, SEQ, D)
    doc_groups = docs.reshape(groups, 8, SEQ)
    grad_groups = cotangent.astype(jnp.float32).reshape(groups, 8, SEQ, D)

    def visit(totals, item):
        group_in, group_docs, group_grad = item
        result, pull = jax.vjp(lambda weights, values: layer(weights, values, group_docs), params, group_in)
        grad_params, grad_values = pull(group_grad)
        totals = tuple((total + part for total, part in zip(totals, grad_params)))
        return (totals, (result, grad_values))
    initial = tuple((jnp.zeros_like(weight) for weight in params))
    totals, (results, grad_values) = lax.scan(visit, initial, (inputs, doc_groups, grad_groups))
    output = results.reshape(tokens.shape).astype(jnp.bfloat16)
    grad_input = grad_values.reshape(tokens.shape).astype(jnp.bfloat16)
    return (output, grad_input, totals[0], totals[1], totals[2], totals[3], totals[4], totals[5], totals[6], totals[7], totals[8], totals[9], totals[10], totals[11], totals[12], totals[13])
```

```python
from functools import partial

import jax
import jax.numpy as jnp
from jax import lax
from jax.experimental import pallas as pl
from jax.experimental.pallas import tpu as pltpu
from jax.sharding import Mesh
from jax.sharding import PartitionSpec as P

F32 = jnp.float32
BF16 = jnp.bfloat16
DK = 128
GROUP = 8
TP = ("y", "x", "c")
REST = ("far", "narrow")
ALL = ("far", "y", "x", "c", "narrow")
SWAP = [(0, 1), (1, 0)]

NN = (((1,), (0,)), ((), ()))
NT = (((1,), (1,)), ((), ()))
TN = (((0,), (0,)), ((), ()))


def dot(left, right, dims=NN):
    return lax.dot_general(left, right, dims, preferred_element_type=F32)


def halves(value):
    high = value.astype(BF16)
    return high, (value - high.astype(F32)).astype(BF16)


def fine(left, right, dims=NN):
    left_high, left_low = halves(left)
    right_high, right_low = halves(right)
    return dot(left_high, right_high, dims) + (dot(left_high, right_low, dims) + dot(left_low, right_high, dims))


def semi(left, right, dims=NN):
    left_high, left_low = halves(left)
    return dot(left_high, right, dims) + dot(left_low, right, dims)


def plain(left, right, dims=NN):
    return dot(left.astype(BF16), right.astype(BF16), dims)


def documents(ends_ref, seq, shape, axis):
    place = lax.broadcasted_iota(jnp.int32, shape, axis)
    doc = jnp.zeros(shape, jnp.int32)
    first = jnp.zeros(shape, jnp.int32)
    for j in range(ends_ref.shape[1]):
        end = ends_ref[seq, j]
        past = place >= end
        doc = doc + past.astype(jnp.int32)
        first = jnp.where(past, end, first)
    return doc, place - first


def inverse(lower, size):
    row = lax.broadcasted_iota(jnp.int32, (size, size), 0)
    col = lax.broadcasted_iota(jnp.int32, (size, size), 1)
    eye = (row == col).astype(F32)
    half = 1
    result = None
    while half < size:
        pair = jnp.logical_and(row // (2 * half) == col // (2 * half), row // half != col // half)
        part = jnp.where(pair, lower, 0.0)
        result = eye - part if result is None else result - fine(result, fine(part, result))
        half *= 2
    return result


def conv(values, taps, keeps):
    total = values * taps[0]
    for j in range(1, len(taps)):
        total = total + jnp.where(keeps[j], pltpu.roll(values, j, 0), 0.0) * taps[j]
    return total


def mixer_forward(ends_ref, act_ref, wqkv_ref, wbeta_ref, taps_ref, gain_ref, wout_ref, y_ref, p_ref, bl_ref, t_ref, u_ref, o_ref, on_ref):
    seq = pl.program_id(0)
    rows = act_ref.shape[1]
    width = wout_ref.shape[0]
    heads = width // DK
    half = rows // 2
    act = act_ref[0]
    proj = dot(act, wqkv_ref[...])
    p_ref[0] = proj
    logit = dot(act, wbeta_ref[...], NT)
    bl_ref[0] = logit
    beta_all = jax.nn.sigmoid(logit)
    doc_row, pos = documents(ends_ref, seq, (rows, DK), 0)
    doc_r, _ = documents(ends_ref, seq, (rows, rows), 0)
    doc_c, _ = documents(ends_ref, seq, (rows, rows), 1)
    row = lax.broadcasted_iota(jnp.int32, (rows, rows), 0)
    col = lax.broadcasted_iota(jnp.int32, (rows, rows), 1)
    same = doc_r == doc_c
    strict = jnp.logical_and(same, row > col)
    causal = jnp.logical_and(same, row >= col)
    keeps = [pos >= j for j in range(taps_ref.shape[0])]
    gain = gain_ref[...]

    def part(kind, head):
        first = kind * width + head * DK
        taps = [taps_ref[j : j + 1, first : first + DK] for j in range(taps_ref.shape[0])]
        c = conv(proj[:, first : first + DK], taps, keeps)
        return c * jax.nn.sigmoid(c)

    def unit(u):
        return u * lax.rsqrt(jnp.sum(u * u, axis=-1, keepdims=True) + 1e-06)

    ons = []
    for head in range(heads):
        q = unit(part(0, head)).astype(BF16)
        k = unit(part(1, head)).astype(BF16)
        v = part(2, head).astype(BF16)
        beta = beta_all[:, head : head + 1]
        inner = dot(k, k, NT)
        scores = dot(q, k, NT)
        lower = jnp.where(strict, inner, 0.0) * beta
        top = inverse(lower[:half, :half], half)
        low = inverse(lower[half:, half:], half)
        cross = -fine(low, fine(lower[half:, :half], top))
        t_ref[0, head, :half, :half] = top
        t_ref[0, head, :half, half:] = jnp.zeros((half, half), F32)
        t_ref[0, head, half:, :half] = cross
        t_ref[0, head, half:, half:] = low
        target = v.astype(F32) * beta
        u_top = fine(top, target[:half])
        u_low = fine(cross, target[:half]) + fine(low, target[half:])
        u = jnp.concatenate([u_top, u_low], axis=0)
        u_ref[0, head] = u
        o = fine(jnp.where(causal, scores, 0.0), u)
        o_ref[0, head] = o
        on = o * lax.rsqrt(jnp.mean(o * o, axis=-1, keepdims=True) + 1e-05) * gain
        ons.append(on.astype(BF16))
    on = jnp.concatenate(ons, axis=1)
    on_ref[0] = on
    y_ref[0] = dot(on, wout_ref[...]).astype(BF16)


def mixer_backward(ends_ref, dy_ref, p_ref, bl_ref, t_ref, u_ref, o_ref, wqkv_ref, wbeta_ref, taps_ref, gain_ref, wout_ref, dact_ref, dqkv_ref, dbl_ref, dtaps_ref, dgain_ref):
    seq = pl.program_id(0)
    rows = dy_ref.shape[1]
    width = wout_ref.shape[0]
    heads = width // DK
    count = taps_ref.shape[0]

    @pl.when(seq == 0)
    def _():
        dtaps_ref[...] = jnp.zeros_like(dtaps_ref)
        dgain_ref[...] = jnp.zeros_like(dgain_ref)

    don_all = dot(dy_ref[0], wout_ref[...], NT)
    beta_all = jax.nn.sigmoid(bl_ref[0])
    doc_row, pos = documents(ends_ref, seq, (rows, DK), 0)
    doc_r, _ = documents(ends_ref, seq, (rows, rows), 0)
    doc_c, _ = documents(ends_ref, seq, (rows, rows), 1)
    row = lax.broadcasted_iota(jnp.int32, (rows, rows), 0)
    col = lax.broadcasted_iota(jnp.int32, (rows, rows), 1)
    same = doc_r == doc_c
    strict = jnp.logical_and(same, row > col)
    causal = jnp.logical_and(same, row >= col)
    keeps = [pos >= j for j in range(count)]
    gain = gain_ref[...]
    lane = lax.broadcasted_iota(jnp.int32, (rows, DK), 1)
    dbl_total = jnp.zeros((rows, DK), F32)

    def taps_of(first):
        return [taps_ref[j : j + 1, first : first + DK] for j in range(count)]

    def conv_back(first, dc):
        p = p_ref[0, :, first : first + DK]
        taps = taps_of(first)
        dp = dc * taps[0]
        dtaps_ref[0:1, first : first + DK] += jnp.sum(dc * p, axis=0, keepdims=True)
        for j in range(1, count):
            kept = jnp.where(keeps[j], dc, 0.0)
            dp = dp + pltpu.roll(kept, rows - j, 0) * taps[j]
            dtaps_ref[j : j + 1, first : first + DK] += jnp.sum(kept * pltpu.roll(p, j, 0), axis=0, keepdims=True)
        return dp

    def parts(first):
        c = conv(p_ref[0, :, first : first + DK], taps_of(first), keeps)
        sigma = jax.nn.sigmoid(c)
        return c * sigma, sigma * (1.0 + c * (1.0 - sigma))

    def unit_back(u, norm, grad):
        return norm * grad - u * (norm * norm * norm * jnp.sum(u * grad, axis=-1, keepdims=True))

    grads = [None] * (3 * heads)
    for head in range(heads):
        firsts = [kind * width + head * DK for kind in range(3)]
        uq, slope_q = parts(firsts[0])
        uk, slope_k = parts(firsts[1])
        uv, slope_v = parts(firsts[2])
        norm_q = lax.rsqrt(jnp.sum(uq * uq, axis=-1, keepdims=True) + 1e-06)
        norm_k = lax.rsqrt(jnp.sum(uk * uk, axis=-1, keepdims=True) + 1e-06)
        q = (uq * norm_q).astype(BF16)
        k = (uk * norm_k).astype(BF16)
        v = uv.astype(BF16).astype(F32)
        beta = beta_all[:, head : head + 1]
        o = o_ref[0, head]
        don = don_all[:, head * DK : (head + 1) * DK]
        r = lax.rsqrt(jnp.mean(o * o, axis=-1, keepdims=True) + 1e-05)
        scaled = don * gain
        dgain_ref[...] += jnp.sum(don * o * r, axis=0, keepdims=True)
        do = r * scaled - o * (r * r * r * jnp.mean(o * scaled, axis=-1, keepdims=True))
        u = u_ref[0, head]
        inner = dot(k, k, NT)
        scores = jnp.where(causal, dot(q, k, NT), 0.0)
        du = fine(scores, do, TN)
        dscores = jnp.where(causal, fine(do, u, NT), 0.0)
        dq = semi(dscores, k)
        dk = semi(dscores, q, TN)
        w = fine(t_ref[0, head], du, TN)
        dv = beta * w
        dlower = jnp.where(strict, fine(w, u, NT), 0.0)
        dbeta = jnp.sum(w * v, axis=-1, keepdims=True) - jnp.sum(dlower * inner, axis=-1, keepdims=True)
        dinner = dlower * beta
        dk = dk - semi(dinner, k) - semi(dinner, k, TN)
        dbl_total = jnp.where(lane == head, dbeta * beta * (1.0 - beta), dbl_total)
        grads[head] = conv_back(firsts[0], unit_back(uq, norm_q, dq) * slope_q).astype(BF16)
        grads[heads + head] = conv_back(firsts[1], unit_back(uk, norm_k, dk) * slope_k).astype(BF16)
        grads[2 * heads + head] = conv_back(firsts[2], dv * slope_v).astype(BF16)
    dqkv = jnp.concatenate(grads, axis=1)
    dqkv_ref[0] = dqkv
    dbl = dbl_total.astype(BF16)
    dbl_ref[0] = dbl
    dact_ref[0] = (dot(dqkv, wqkv_ref[...], NT) + dot(dbl, wbeta_ref[...])).astype(BF16)


def feed_forward(act_ref, dy_ref, wg_ref, wu_ref, wd_ref, out_ref, dact_ref, hid_ref, dgt_ref, dup_ref):
    act = act_ref[...]
    gt = dot(act, wg_ref[...])
    up = dot(act, wu_ref[...])
    sigma = jax.nn.sigmoid(gt)
    swish = gt * sigma
    hid = (swish * up).astype(BF16)
    hid_ref[...] = hid
    out_ref[...] = dot(hid, wd_ref[...]).astype(BF16)
    dhid = dot(dy_ref[...], wd_ref[...], NT)
    dgt = (dhid * up * sigma * (1.0 + gt * (1.0 - sigma))).astype(BF16)
    dup = (dhid * swish).astype(BF16)
    dgt_ref[...] = dgt
    dup_ref[...] = dup
    dact_ref[...] = (dot(dgt, wg_ref[...], NT) + dot(dup, wu_ref[...], NT)).astype(BF16)


def whole(shape):
    return pl.BlockSpec(shape, lambda i: (0,) * len(shape), pipeline_mode=pl.Buffered(1))


def each(shape):
    return pl.BlockSpec((1,) + shape, lambda i: (i,) + (0,) * len(shape))


PARAMS = pltpu.CompilerParams(vmem_limit_bytes=60 * 1024 * 1024, dimension_semantics=("arbitrary",))


def gather_group(own):
    half = own.shape[0] // 2
    by_x = lax.ppermute(own, "x", SWAP)
    by_y = lax.ppermute(own, "y", SWAP)
    far_a = lax.ppermute(by_x[:half], "y", SWAP)
    far_b = lax.ppermute(by_y[half:], "x", SWAP)
    far = jnp.concatenate([far_a, far_b])
    near = [own, by_x, by_y, far]
    return jnp.stack(near + [lax.ppermute(piece, "c", SWAP) for piece in near])


def joined(left, right):
    return left.astype(F32) + right.astype(F32)


def sum_group(parts):
    _, rows, columns = parts.shape
    half = rows // 2
    parts = parts.reshape(2, 4, rows, columns)
    other = lax.ppermute(parts[1], "c", SWAP)
    both = joined(parts[0], other).astype(BF16)
    a = both[:, :half].reshape(2, 2, half, columns)
    b = both[:, half:].reshape(2, 2, rows - half, columns)
    a = joined(a[:, 0], lax.ppermute(a[:, 1], "x", SWAP)).astype(BF16)
    b = joined(b[0], lax.ppermute(b[1], "y", SWAP)).astype(BF16)
    a = joined(a[0], lax.ppermute(a[1], "y", SWAP))
    b = joined(b[0], lax.ppermute(b[1], "x", SWAP))
    return jnp.concatenate([a, b])


def spread_columns(weight):
    rows, columns = weight.shape
    slices = weight.reshape(rows, GROUP, columns // GROUP).transpose(1, 0, 2)
    mine = lax.all_to_all(slices, TP, 0, 0, tiled=True)
    return gather_rest(mine)


def gather_rest(mine):
    far, narrow = lax.axis_size("far"), lax.axis_size("narrow")
    _, rows, columns = mine.shape
    full = lax.all_gather(mine, REST, axis=0)
    full = full.reshape(far, narrow, GROUP, rows, columns).transpose(0, 2, 1, 3, 4)
    return full.reshape(-1, columns)


def sum_rest(grad):
    far, narrow = lax.axis_size("far"), lax.axis_size("narrow")
    columns = grad.shape[1]
    grad = grad.reshape(far, GROUP, narrow, -1, columns).transpose(0, 2, 1, 3, 4)
    grad = lax.psum_scatter(grad.reshape(-1, columns), REST, scatter_dimension=0, tiled=True)
    return grad.reshape(GROUP, -1, columns)


def spread_rows(weight, group=GROUP):
    if lax.axis_size("far") == 1:
        return lax.all_gather(weight, "narrow", axis=0, tiled=True)
    full = lax.all_gather(weight, ALL, axis=0, tiled=True)
    rows = full.shape[0] // group
    return lax.dynamic_slice_in_dim(full, lax.axis_index(TP) * rows, rows, 0)


def sum_rows(grad, group=GROUP):
    if lax.axis_size("far") == 1:
        return lax.psum_scatter(grad, "narrow", scatter_dimension=0, tiled=True).astype(F32)
    rows, columns = grad.shape
    full = jnp.where((jnp.arange(group) == lax.axis_index(TP))[:, None, None], grad[None], 0)
    return lax.psum_scatter(full.reshape(-1, columns), ALL, scatter_dimension=0, tiled=True).astype(F32)


def collect_columns(mine):
    slices = lax.all_to_all(mine, TP, 0, 0, tiled=True)
    return slices.transpose(1, 0, 2).reshape(slices.shape[1], -1).astype(F32)


def local(tokens, doc_lengths, gain_attn, w_query, w_key, w_value, w_beta, conv_query, conv_key, conv_value, gain_head, w_out, gain_ffn, w_gate, w_up, w_down, cotangent):
    x_low = tokens[0]
    x = x_low.astype(F32)
    dy_low = cotangent[0]
    length, width = x.shape
    heads = w_beta.shape[1]
    mine = heads // GROUP
    cols = mine * DK
    taps_count = conv_query.shape[0]
    y_at, x_at, c_at = lax.axis_index("y"), lax.axis_index("x"), lax.axis_index("c")
    me = (y_at * 2 + x_at) * 2 + c_at

    small = jnp.concatenate([gain_attn[None], gain_ffn[None], conv_query, conv_key, conv_value, w_beta.T])
    small = lax.all_gather(small, ALL, axis=0)
    small = small.transpose(1, 0, 2).reshape(small.shape[1], width)
    gain_one = small[0].astype(F32)
    gain_two = small[1].astype(F32)
    taps = small[2 : 2 + 3 * taps_count].reshape(3, taps_count, GROUP, cols)
    taps = lax.dynamic_index_in_dim(taps, me, 2, keepdims=False)
    taps = taps.transpose(1, 0, 2).reshape(taps_count, 3 * cols).astype(F32)
    wbeta = lax.dynamic_slice_in_dim(small[2 + 3 * taps_count :], me * mine, mine, 0)
    wbeta = jnp.pad(wbeta, ((0, DK - mine), (0, 0)))
    gain_h = gain_head.astype(F32)[None]

    lengths = lax.all_gather(doc_lengths[0], TP, axis=0)
    order = [((y_at ^ dy) * 2 + (x_at ^ dx)) * 2 + (c_at ^ dc) for dc in (0, 1) for dy in (0, 1) for dx in (0, 1)]
    ends = jnp.cumsum(jnp.take(lengths, jnp.stack(order), axis=0), axis=1)[:, :-1]

    qkv_rows = jnp.concatenate([w.reshape(-1, GROUP, cols) for w in (w_query, w_key, w_value)], axis=2)
    wqkv = spread_columns(qkv_rows.reshape(qkv_rows.shape[0], -1))
    wout = spread_rows(w_out)
    wgate = spread_columns(w_gate)
    wup = spread_columns(w_up)
    wdown = spread_rows(w_down)

    x_all = gather_group(x_low)
    x_wide = x_all.astype(F32)
    act = (x_wide * lax.rsqrt(jnp.mean(x_wide * x_wide, axis=-1, keepdims=True) + 1e-06) * gain_one).astype(BF16)

    specs = [pl.BlockSpec(memory_space=pltpu.SMEM), each((length, width)), whole((width, 3 * cols)), whole((DK, width)), whole((taps_count, 3 * cols)), whole((1, DK)), whole((cols, width))]
    kept = [((length, 3 * cols), F32), ((length, DK), F32), ((mine, length, length), F32), ((mine, length, DK), F32), ((mine, length, DK), F32)]
    outs = [((length, width), BF16)] + kept + [((length, cols), BF16)]
    y_parts, p, bl, t, u, o, on = pl.pallas_call(
        mixer_forward,
        grid=(GROUP,),
        in_specs=specs,
        out_specs=[each(shape) for shape, _ in outs],
        out_shape=[jax.ShapeDtypeStruct((GROUP,) + shape, kind) for shape, kind in outs],
        compiler_params=PARAMS,
        cost_estimate=pl.CostEstimate(flops=20_000_000_000, bytes_accessed=60_000_000, transcendentals=0),
        name="mixer_forward",
    )(ends, act, wqkv, wbeta, taps, gain_h, wout)

    h1 = x + sum_group(y_parts)
    r2 = lax.rsqrt(jnp.mean(h1 * h1, axis=-1, keepdims=True) + 1e-06)
    act2 = (h1 * r2 * gain_two).astype(BF16)
    dy_all = gather_group(dy_low).reshape(-1, width)
    act2_all = gather_group(act2).reshape(-1, width)
    hidden = wdown.shape[0]
    block = 2 * length

    def rows_of(columns):
        return pl.BlockSpec((block, columns), lambda i: (i, 0))

    total = GROUP * length
    out_parts, dact2_parts, hid, dgt, dup = pl.pallas_call(
        feed_forward,
        grid=(total // block,),
        in_specs=[rows_of(width), rows_of(width), whole((width, hidden)), whole((width, hidden)), whole((hidden, width))],
        out_specs=[rows_of(width), rows_of(width), rows_of(hidden), rows_of(hidden), rows_of(hidden)],
        out_shape=[jax.ShapeDtypeStruct((total, columns), BF16) for columns in (width, width, hidden, hidden, hidden)],
        compiler_params=PARAMS,
        cost_estimate=pl.CostEstimate(flops=36_000_000_000, bytes_accessed=60_000_000, transcendentals=0),
        name="feed_forward",
    )(act2_all, dy_all, wgate, wup, wdown)

    grad_second = sum_group(dact2_parts.reshape(GROUP, length, width))
    scaled = grad_second * gain_two
    dh1 = dy_low.astype(F32) + r2 * scaled - h1 * (r2 * r2 * r2 * jnp.mean(h1 * scaled, axis=-1, keepdims=True))
    grad_gain_ffn = jnp.sum(grad_second * h1 * r2, axis=0)
    dy1 = dh1.astype(BF16)
    dy1_all = gather_group(dy1)

    grad_gate = sum_rest(dot(act2_all, dgt, TN).astype(BF16))
    grad_up = sum_rest(dot(act2_all, dup, TN).astype(BF16))
    grad_down = sum_rows(dot(hid, dy_all, TN).astype(BF16))
    result = (h1 + sum_group(out_parts.reshape(GROUP, length, width))).astype(BF16)

    specs = [pl.BlockSpec(memory_space=pltpu.SMEM), each((length, width))] + [each(shape) for shape, _ in kept]
    specs += [whole((width, 3 * cols)), whole((DK, width)), whole((taps_count, 3 * cols)), whole((1, DK)), whole((cols, width))]
    outs = [((length, width), BF16), ((length, 3 * cols), BF16), ((length, DK), BF16)]
    dact_parts, dqkv, dbl, dtaps, dgain = pl.pallas_call(
        mixer_backward,
        grid=(GROUP,),
        in_specs=specs,
        out_specs=[each(shape) for shape, _ in outs] + [pl.BlockSpec((taps_count, 3 * cols), lambda i: (0, 0)), pl.BlockSpec((1, DK), lambda i: (0, 0))],
        out_shape=[jax.ShapeDtypeStruct((GROUP,) + shape, kind) for shape, kind in outs]
        + [jax.ShapeDtypeStruct((taps_count, 3 * cols), F32), jax.ShapeDtypeStruct((1, DK), F32)],
        compiler_params=PARAMS,
        cost_estimate=pl.CostEstimate(flops=40_000_000_000, bytes_accessed=60_000_000, transcendentals=0),
        name="mixer_backward",
    )(ends, dy1_all, p, bl, t, u, o, wqkv, wbeta, taps, gain_h, wout)

    act_rows = act.reshape(total, width)
    dqkv = dqkv.reshape(total, 3 * cols)
    grad_out = sum_rows(dot(on.reshape(total, cols), dy1_all.reshape(total, width), TN).astype(BF16))
    grad_qkv = sum_rest(dot(act_rows, dqkv, TN).astype(BF16))
    grad_wbeta = dot(dbl.reshape(total, DK), act_rows, TN)[:mine]

    grad_act = sum_group(dact_parts)
    r1 = lax.rsqrt(jnp.mean(x * x, axis=-1, keepdims=True) + 1e-06)
    scaled = grad_act * gain_one
    grad_input = (dh1 + r1 * scaled - x * (r1 * r1 * r1 * jnp.mean(x * scaled, axis=-1, keepdims=True))).astype(BF16)
    grad_gain_attn = jnp.sum(grad_act * x * r1, axis=0)

    dtaps = dtaps.reshape(taps_count, 3, 1, cols).transpose(1, 0, 2, 3).reshape(3 * taps_count, 1, cols)
    dtaps = jnp.where((jnp.arange(GROUP) == me)[None, :, None], dtaps, 0.0).reshape(3 * taps_count, width)
    dbeta = jnp.where((jnp.arange(GROUP) == me)[:, None, None], grad_wbeta[None], 0.0).reshape(heads, width)
    smalls = jnp.concatenate([grad_gain_attn[None], grad_gain_ffn[None], dtaps, dbeta])
    smalls = smalls.reshape(smalls.shape[0], lax.axis_size(ALL), -1).transpose(1, 0, 2)
    smalls = lax.psum_scatter(smalls, ALL, scatter_dimension=0, tiled=False)
    grad_gain_head = lax.psum(dgain[0], ALL)

    third = collect_columns(grad_qkv).reshape(-1, GROUP, 3, cols)
    return (
        result[None],
        grad_input[None],
        smalls[0],
        third[:, :, 0].reshape(-1, width),
        third[:, :, 1].reshape(-1, width),
        third[:, :, 2].reshape(-1, width),
        smalls[2 + 3 * taps_count :].T,
        smalls[2 : 2 + taps_count],
        smalls[2 + taps_count : 2 + 2 * taps_count],
        smalls[2 + 2 * taps_count : 2 + 3 * taps_count],
        grad_gain_head,
        grad_out,
        smalls[1],
        collect_columns(grad_gate),
        collect_columns(grad_up),
        grad_down,
    )


def solution(mesh):
    wide, narrow = mesh.shape["wide"], mesh.shape["narrow"]
    inner = Mesh(mesh.devices.reshape(wide // GROUP, 2, 2, 2, narrow), ALL)
    rows = P(ALL, None)
    columns = P(None, ALL)
    vector = P(ALL)
    cube = P(ALL, None, None)
    return jax.shard_map(
        local,
        mesh=inner,
        in_specs=(cube, rows, vector, rows, rows, rows, rows, columns, columns, columns, P(), rows, vector, rows, rows, rows, cube),
        out_specs=(cube, cube, vector, rows, rows, rows, rows, columns, columns, columns, P(), rows, vector, rows, rows, rows),
        check_vma=False,
    )
```

```python
from functools import partial

import jax
import jax.numpy as jnp
from jax import lax
from jax.experimental import pallas as pl
from jax.experimental.pallas import tpu as pltpu
from jax.sharding import Mesh
from jax.sharding import PartitionSpec as P

F32 = jnp.float32
BF16 = jnp.bfloat16
DK = 128
GROUP = 8
SLICES = ("y", "x", "c")
REST = ("far", "narrow")
ALL = ("far", "y", "x", "c", "narrow")
SWAP = [(0, 1), (1, 0)]
NEAR = [(0, 1), (1, 0), (2, 3), (3, 2)]
SKIP = [(0, 2), (2, 0), (1, 3), (3, 1)]
MIDDLE = [(1, 2), (2, 1)]
ACROSS = [(0, 3), (3, 0), (1, 2), (2, 1)]

NN = (((1,), (0,)), ((), ()))
NT = (((1,), (1,)), ((), ()))
TN = (((0,), (0,)), ((), ()))


def dot(left, right, dims=NN):
    return lax.dot_general(left, right, dims, preferred_element_type=F32)


def halves(value):
    high = value.astype(BF16)
    return high, (value - high.astype(F32)).astype(BF16)


def fine(left, right, dims=NN):
    left_high, left_low = halves(left)
    right_high, right_low = halves(right)
    return dot(left_high, right_high, dims) + (dot(left_high, right_low, dims) + dot(left_low, right_high, dims))


def semi(left, right, dims=NN):
    left_high, left_low = halves(left)
    return dot(left_high, right, dims) + dot(left_low, right, dims)


def plain(left, right, dims=NN):
    return dot(left.astype(BF16), right.astype(BF16), dims)


def documents(ends_ref, seq, shape, axis):
    place = lax.broadcasted_iota(jnp.int32, shape, axis)
    doc = jnp.zeros(shape, jnp.int32)
    first = jnp.zeros(shape, jnp.int32)
    for j in range(ends_ref.shape[1]):
        end = ends_ref[seq, j]
        past = place >= end
        doc = doc + past.astype(jnp.int32)
        first = jnp.where(past, end, first)
    return doc, place - first


def inverses(lowers, size):
    row = lax.broadcasted_iota(jnp.int32, (size, size), 0)
    col = lax.broadcasted_iota(jnp.int32, (size, size), 1)
    apart = row ^ col
    eye = (row == col).astype(F32)
    results = [eye - jnp.where(apart == 1, lower, 0.0) for lower in lowers]
    half = 2
    while half < size:
        pair = jnp.logical_and(apart >= half, apart < 2 * half)
        parts = [jnp.where(pair, lower, 0.0) for lower in lowers]
        middles = [fine(part, result) for part, result in zip(parts, results)]
        results = [result - fine(result, middle) for middle, result in zip(middles, results)]
        half *= 2
    return results


def conv(values, taps, keeps):
    total = values * taps[0]
    for j in range(1, len(taps)):
        total = total + jnp.where(keeps[j], pltpu.roll(values, j, 0), 0.0) * taps[j]
    return total


def load(refs, held, sems, where_ref):
    copies = [pltpu.make_async_copy(ref, held.at[:, where_ref[n]], sems.at[n]) for n, ref in enumerate(refs)]
    for copy in copies:
        copy.start()
    return copies


def load_side(ref, side, held, sems):
    copies = [pltpu.make_async_copy(ref.at[side, n], held.at[:, n], sems.at[n]) for n in range(4)]
    for copy in copies:
        copy.start()
    return copies


def wait_all(groups):
    for copies in groups:
        for copy in copies:
            copy.wait()


def flat(value):
    return value.reshape(-1, value.shape[-1])


def chosen(*refs):
    value = refs[0][...]
    for n, ref in enumerate(refs[1:], 1):
        value = jnp.where(pl.program_id(0) == n, ref[...], value)
    return value


def hand_out(step, refs, value):
    own_ref, by_x_ref, by_y_ref, x_low_ref, y_top_ref = refs
    half = value.shape[0] // 2

    @pl.when(step == 0)
    def _():
        own_ref[...] = value

    @pl.when(step == 1)
    def _():
        by_x_ref[0] = value[:half]
        x_low_ref[...] = value[half:]

    @pl.when(step == 2)
    def _():
        y_top_ref[...] = value[:half]
        by_y_ref[0] = value[half:]

    @pl.when(step == 3)
    def _():
        by_x_ref[1] = value[:half]
        by_y_ref[1] = value[half:]


def masks(ends_ref, seq, rows, taps):
    _, pos = documents(ends_ref, seq, (rows, DK), 0)
    doc_r, _ = documents(ends_ref, seq, (rows, rows), 0)
    doc_c, _ = documents(ends_ref, seq, (rows, rows), 1)
    row = lax.broadcasted_iota(jnp.int32, (rows, rows), 0)
    col = lax.broadcasted_iota(jnp.int32, (rows, rows), 1)
    same = doc_r == doc_c
    return [pos >= j for j in range(taps)], jnp.logical_and(same, row > col), jnp.logical_and(same, row >= col)


def mixer_forward(ends_ref, where_ref, x0_ref, x1_ref, x2_ref, x3_ref, gain_one_ref, wbeta_ref, taps_ref, gain_ref, *rest):
    w_refs = rest[:4], rest[4:8]
    out_refs, rest = rest[8:13], rest[13:]
    act_ref, p_ref, bl_ref, t_ref, u_ref, o_ref, on_ref, w0, w1, sems = rest
    held = (w0, w1)
    seq = pl.program_id(0)

    @pl.when(seq == 0)
    def _():
        wait_all([load(w_refs[side], held[side], sems.at[side], where_ref) for side in (0, 1)])

    rows = x0_ref.shape[0]
    cols = on_ref.shape[2] // 2
    heads = cols // DK
    half = rows // 2
    count = taps_ref.shape[0]
    x = chosen(x0_ref, x1_ref, x2_ref, x3_ref).astype(F32)
    act = (x * lax.rsqrt(jnp.mean(x * x, axis=-1, keepdims=True) + 1e-06) * gain_one_ref[...]).astype(BF16)
    act_ref[0] = act
    projs = []
    for side in (0, 1):
        proj = dot(act, flat(held[side][:, :, :, : 3 * cols]))
        p_ref[0, :, side * 3 * cols : (side + 1) * 3 * cols] = proj
        projs.append(proj)
    logit = dot(act, wbeta_ref[...], NT)
    bl_ref[0] = logit
    beta_all = jax.nn.sigmoid(logit)
    keeps, strict, causal = masks(ends_ref, seq, rows, count)
    gain = gain_ref[...]
    every = range(2 * heads)

    def part(kind, head):
        side, first = head // heads, kind * cols + (head % heads) * DK
        at = side * 3 * cols + first
        taps = [taps_ref[j : j + 1, at : at + DK] for j in range(count)]
        c = conv(projs[side][:, first : first + DK], taps, keeps)
        return c * jax.nn.sigmoid(c)

    def unit(u):
        return u * lax.rsqrt(jnp.sum(u * u, axis=-1, keepdims=True) + 1e-06)

    qs = [unit(part(0, head)).astype(BF16) for head in every]
    ks = [unit(part(1, head)).astype(BF16) for head in every]
    lowers = [jnp.where(strict, dot(ks[head], ks[head], NT), 0.0) * beta_all[:, head : head + 1] for head in every]
    blocks = inverses([block for lower in lowers for block in (lower[:half, :half], lower[half:, half:])], half)
    ons = []
    for head in every:
        v = part(2, head).astype(BF16)
        beta = beta_all[:, head : head + 1]
        top, low = blocks[2 * head], blocks[2 * head + 1]
        cross = -fine(low, fine(lowers[head][half:, :half], top))
        t_ref[0, head, :half, :half] = top
        t_ref[0, head, :half, half:] = jnp.zeros((half, half), F32)
        t_ref[0, head, half:, :half] = cross
        t_ref[0, head, half:, half:] = low
        target = v.astype(F32) * beta
        u_top = fine(top, target[:half])
        u_low = fine(cross, target[:half]) + fine(low, target[half:])
        u = jnp.concatenate([u_top, u_low], axis=0)
        u_ref[0, head] = u
        o = fine(jnp.where(causal, dot(qs[head], ks[head], NT), 0.0), u)
        o_ref[0, head] = o
        on = o * lax.rsqrt(jnp.mean(o * o, axis=-1, keepdims=True) + 1e-05) * gain
        ons.append(on.astype(BF16))
    on = jnp.concatenate(ons, axis=1)
    on_ref[0] = on
    y = []
    for block in range(w0.shape[0]):
        parts = [dot(on[:, side * cols : (side + 1) * cols], flat(held[side][block, :, :, 3 * cols :])) for side in (0, 1)]
        y.append((parts[0] + parts[1]).astype(BF16))
    hand_out(seq, out_refs, jnp.concatenate(y, axis=1))


def mixer_backward(ends_ref, where_ref, dy0_ref, dy1_ref, dy2_ref, dy3_ref, p_ref, bl_ref, t_ref, u_ref, o_ref, wbeta_ref, taps_ref, gain_ref, *rest):
    w_refs = rest[:4], rest[4:8]
    out_refs, rest = rest[8:13], rest[13:]
    dqkv_ref, dbl_ref, dtaps_ref, dgain_ref, w0, w1, sems = rest
    held = (w0, w1)
    seq = pl.program_id(0)
    rows = dy0_ref.shape[0]
    cols = p_ref.shape[2] // 6
    heads = cols // DK
    count = taps_ref.shape[0]

    @pl.when(seq == 0)
    def _():
        groups = [load(w_refs[side], held[side], sems.at[side], where_ref) for side in (0, 1)]
        dtaps_ref[...] = jnp.zeros_like(dtaps_ref)
        dgain_ref[...] = jnp.zeros_like(dgain_ref)
        wait_all(groups)

    dy = chosen(dy0_ref, dy1_ref, dy2_ref, dy3_ref)
    dons = []
    for side in (0, 1):
        don = 0.0
        for block in range(w0.shape[0]):
            weight = flat(held[side][block, :, :, 3 * cols :])
            don = don + dot(dy[:, block * weight.shape[1] : (block + 1) * weight.shape[1]], weight, NT)
        dons.append(don)
    beta_all = jax.nn.sigmoid(bl_ref[0])
    keeps, strict, causal = masks(ends_ref, seq, rows, count)
    gain = gain_ref[...]
    lane = lax.broadcasted_iota(jnp.int32, (rows, DK), 1)
    dbl_total = jnp.zeros((rows, DK), F32)

    def taps_of(first):
        return [taps_ref[j : j + 1, first : first + DK] for j in range(count)]

    def conv_back(first, dc):
        p = p_ref[0, :, first : first + DK]
        taps = taps_of(first)
        dp = dc * taps[0]
        dtaps_ref[0:1, first : first + DK] += jnp.sum(dc * p, axis=0, keepdims=True)
        for j in range(1, count):
            kept = jnp.where(keeps[j], dc, 0.0)
            dp = dp + pltpu.roll(kept, rows - j, 0) * taps[j]
            dtaps_ref[j : j + 1, first : first + DK] += jnp.sum(kept * pltpu.roll(p, j, 0), axis=0, keepdims=True)
        return dp

    def parts(first):
        c = conv(p_ref[0, :, first : first + DK], taps_of(first), keeps)
        sigma = jax.nn.sigmoid(c)
        return c * sigma, sigma * (1.0 + c * (1.0 - sigma))

    def unit_back(u, norm, grad):
        return norm * grad - u * (norm * norm * norm * jnp.sum(u * grad, axis=-1, keepdims=True))

    grads = [[None] * (3 * heads) for _ in (0, 1)]
    for head in range(2 * heads):
        side, at = head // heads, head % heads
        firsts = [side * 3 * cols + kind * cols + at * DK for kind in range(3)]
        uq, slope_q = parts(firsts[0])
        uk, slope_k = parts(firsts[1])
        uv, slope_v = parts(firsts[2])
        norm_q = lax.rsqrt(jnp.sum(uq * uq, axis=-1, keepdims=True) + 1e-06)
        norm_k = lax.rsqrt(jnp.sum(uk * uk, axis=-1, keepdims=True) + 1e-06)
        q = (uq * norm_q).astype(BF16)
        k = (uk * norm_k).astype(BF16)
        v = uv.astype(BF16).astype(F32)
        beta = beta_all[:, head : head + 1]
        o = o_ref[0, head]
        don = dons[side][:, at * DK : (at + 1) * DK]
        r = lax.rsqrt(jnp.mean(o * o, axis=-1, keepdims=True) + 1e-05)
        scaled = don * gain
        dgain_ref[...] += jnp.sum(don * o * r, axis=0, keepdims=True)
        do = r * scaled - o * (r * r * r * jnp.mean(o * scaled, axis=-1, keepdims=True))
        u = u_ref[0, head]
        inner = dot(k, k, NT)
        scores = jnp.where(causal, dot(q, k, NT), 0.0)
        du = fine(scores, do, TN)
        dscores = jnp.where(causal, fine(do, u, NT), 0.0)
        dq = semi(dscores, k)
        dk = semi(dscores, q, TN)
        w = fine(t_ref[0, head], du, TN)
        dv = beta * w
        dlower = jnp.where(strict, fine(w, u, NT), 0.0)
        dbeta = jnp.sum(w * v, axis=-1, keepdims=True) - jnp.sum(dlower * inner, axis=-1, keepdims=True)
        dinner = dlower * beta
        dk = dk - semi(dinner, k) - semi(dinner, k, TN)
        dbl_total = jnp.where(lane == head, dbeta * beta * (1.0 - beta), dbl_total)
        grads[side][at] = conv_back(firsts[0], unit_back(uq, norm_q, dq) * slope_q).astype(BF16)
        grads[side][heads + at] = conv_back(firsts[1], unit_back(uk, norm_k, dk) * slope_k).astype(BF16)
        grads[side][2 * heads + at] = conv_back(firsts[2], dv * slope_v).astype(BF16)
    dbl = dbl_total.astype(BF16)
    dbl_ref[0] = dbl
    dact = dot(dbl, wbeta_ref[...])
    for side in (0, 1):
        dqkv = jnp.concatenate(grads[side], axis=1)
        dqkv_ref[0, :, side * 3 * cols : (side + 1) * 3 * cols] = dqkv
        dact = dact + dot(dqkv, flat(held[side][:, :, :, : 3 * cols]), NT)
    hand_out(seq, out_refs, dact.astype(BF16))


def feed_forward(where_ref, *rest):
    acts, dys, wgu_ref, wd_refs = rest[:4], rest[4:8], rest[8], (rest[9:13], rest[13:17])
    out_refs, dact_refs, rest = rest[17:22], rest[22:27], rest[27:]
    hid_refs, dgu_refs, wgu, wd, sems = rest[:2], rest[2:4], rest[4:6], rest[6:8], rest[8]
    step = pl.program_id(0)

    @pl.when(step == 0)
    def _():
        core = where_ref[4]
        groups = [load_side(wgu_ref, at, wgu[side], sems.at[side]) for side, at in enumerate((core, 1 - core))]
        groups += [load(wd_refs[side], wd[side], sems.at[2 + side], where_ref) for side in (0, 1)]
        wait_all(groups)

    hidden = hid_refs[0].shape[1]
    act = jnp.concatenate([chosen(acts[0], acts[2]), chosen(acts[1], acts[3])])
    dy = jnp.concatenate([chosen(dys[0], dys[2]), chosen(dys[1], dys[3])])
    rows = acts[0].shape[0]
    for side in (0, 1):
        gu = dot(act, flat(wgu[side][...]))
        gt, up = gu[:, :hidden], gu[:, hidden:]
        sigma = jax.nn.sigmoid(gt)
        swish = gt * sigma
        hid_refs[side][...] = (swish * up).astype(BF16)
        dhid = dot(dy, flat(wd[side][...]), NT)
        dgt = (dhid * up * sigma * (1.0 + gt * (1.0 - sigma))).astype(BF16)
        dup = (dhid * swish).astype(BF16)
        dgu_refs[side][...] = jnp.concatenate([dgt, dup], axis=1)
    for part in (0, 1):
        here = pl.ds(part * rows, rows)
        dact = sum([dot(dgu_refs[side][here], flat(wgu[side][...]), NT) for side in (0, 1)])
        hand_out(2 * step + part, dact_refs, dact.astype(BF16))
        out = sum([dot(hid_refs[side][here], flat(wd[side][...])) for side in (0, 1)])
        hand_out(2 * step + part, out_refs, out.astype(BF16))


def rows_out(where_ref, out_ref, held, value, index):
    held[...] = value.astype(BF16)
    rows = held.shape[0] // 4
    for n in range(4):
        out_ref[(n,) + index] = held[pl.ds(pl.multiple_of(where_ref[n] * rows, rows), rows)]


def gate_up_grads(where_ref, *rest):
    acts, dgus, out = rest[:4], (rest[4], rest[5]), rest[6]
    act = jnp.concatenate([ref[...] for ref in acts])
    rows = act.shape[1] // 4
    core = where_ref[4]
    for at, side in ((core, 0), (1 - core, 1)):
        value = dot(act, dgus[side][...], TN).astype(BF16)
        for n in range(4):
            out[n, at, 0] = value[n * rows : (n + 1) * rows]


def down_grads(where_ref, *rest):
    hids, dys, out = (rest[0], rest[1]), rest[2:6], rest[6]
    dy = jnp.concatenate([ref[...] for ref in dys])
    rows = hids[0].shape[1] // 4
    core = where_ref[4]
    for at, side in ((core, 0), (1 - core, 1)):
        value = dot(hids[side][...], dy, TN).astype(BF16)
        for n in range(4):
            out[n, at] = value[n * rows : (n + 1) * rows]


def mixer_grads(where_ref, act_ref, dqkv_ref, on_ref, dbl_ref, *rest):
    dys, outs, beta_ref, held = rest[:4], rest[4:6], rest[6], rest[7]
    act = act_ref[...]
    beta_ref[...] = dot(dbl_ref[...], act, TN)
    dy = jnp.concatenate([ref[...] for ref in dys])
    three, cols = dqkv_ref.shape[1] // 2, on_ref.shape[1] // 2
    for side in (0, 1):
        qkv = dot(act, dqkv_ref[:, side * three : (side + 1) * three], TN)
        out = dot(on_ref[:, side * cols : (side + 1) * cols], dy, TN)
        rows_out(where_ref, outs[side], held, jnp.concatenate([qkv, out], axis=1), (0,))


def whole(shape):
    return pl.BlockSpec(shape, lambda i: (0,) * len(shape), pipeline_mode=pl.Buffered(1))


def each(shape):
    return pl.BlockSpec((1,) + shape, lambda i: (i,) + (0,) * len(shape))


PARAMS = pltpu.CompilerParams(vmem_limit_bytes=60 * 1024 * 1024, dimension_semantics=("arbitrary",))


def tie(*values):
    return lax.optimization_barrier(values)


def gather_group(own):
    return [own, lax.ppermute(own, "x", SWAP), lax.ppermute(own, "y", SWAP), lax.ppermute(own, ("y", "x"), ACROSS)]


def joined(left, right):
    return left.astype(F32) + right.astype(F32)


def sum_group(parts, *later):
    own, by_x, by_y, x_low, y_top = parts
    half = x_low.shape[0]
    got_x = lax.ppermute(by_x, "x", SWAP)
    got_y = lax.ppermute(by_y, "y", SWAP)
    if later:
        got_x, got_y, *later = tie(got_x, got_y, *later)
    y_top = lax.ppermute(joined(y_top, got_x[1]).astype(BF16), "y", SWAP)
    x_low = lax.ppermute(joined(x_low, got_y[1]).astype(BF16), "x", SWAP)
    top = joined(own[:half], got_x[0]) + y_top.astype(F32)
    low = joined(own[half:], got_y[0]) + x_low.astype(F32)
    total = jnp.concatenate([top, low])
    return (total, *later) if later else total


def by_hand():
    return lax.axis_size("far") == 1 and lax.axis_size("narrow") == 4


def with_partner(pieces):
    return pieces, [lax.ppermute(piece, "c", SWAP) for piece in pieces]


def spread_first(mine):
    return [mine, lax.ppermute(mine, "narrow", NEAR), lax.ppermute(mine, "narrow", SKIP)]


def spread_last(mine, near, skip):
    return [mine, near, skip, lax.ppermute(mine, "narrow", MIDDLE), lax.ppermute(skip, "narrow", [(2, 3), (1, 0)])]


def all_four(mine, near, skip, middle, end):
    z = lax.axis_index("narrow")
    return [mine, near, skip, jnp.where((z == 1) | (z == 2), middle, end)]


def spread_columns(mine):
    far, narrow = lax.axis_size("far"), lax.axis_size("narrow")
    _, rows, columns = mine.shape
    full = lax.all_gather(mine, REST, axis=0).reshape(far, narrow, GROUP, rows, columns).transpose(0, 2, 1, 3, 4)
    return full.reshape(GROUP, 4, -1, columns)


def spread_rows(weight):
    full = lax.all_gather(weight, ALL, axis=0, tiled=True)
    total = full.shape[0] // GROUP
    return lax.dynamic_slice_in_dim(full, lax.axis_index(SLICES) * total, total, 0).reshape(4, -1, full.shape[1])


def collect(own, other, *early):
    got = lax.ppermute(other, "c", SWAP)
    own, near, skip, last = [joined(own[n], got[n]) for n in range(4)]
    last = last.astype(BF16)
    ends = lax.ppermute(last, "narrow", [(3, 2), (0, 1)])
    middle = lax.ppermute(last, "narrow", MIDDLE)
    near, ends, middle, *early = tie(near.astype(BF16), ends, middle, *early)
    skip = (skip + ends.astype(F32)).astype(BF16)
    near = lax.ppermute(near, "narrow", NEAR)
    skip = lax.ppermute(skip, "narrow", SKIP)
    return own + near.astype(F32) + joined(skip, middle), *early


def collect_columns(own, other):
    full = joined(own, lax.ppermute(other, "c", SWAP)).astype(BF16)
    columns = full.shape[-1]
    far, narrow = lax.axis_size("far"), lax.axis_size("narrow")
    full = full.transpose(1, 0, 2, 3).reshape(far, GROUP, narrow, -1, columns).transpose(0, 2, 1, 3, 4)
    full = lax.psum_scatter(full.reshape(-1, columns), REST, scatter_dimension=0, tiled=True)
    return full.reshape(GROUP, -1, columns).astype(F32)


def collect_rows(own, other):
    full = joined(own, lax.ppermute(other, "c", SWAP)).astype(BF16)
    full = full.reshape(1, -1, full.shape[-1])
    full = jnp.where((jnp.arange(GROUP) == lax.axis_index(SLICES))[:, None, None], full, 0)
    return lax.psum_scatter(full.reshape(-1, full.shape[-1]), ALL, scatter_dimension=0, tiled=True).astype(F32)


def to_owners(mine):
    return lax.all_to_all(mine.astype(BF16), SLICES, 0, 0, tiled=True).transpose(1, 0, 2).astype(F32)


def doubled(values, axis, pairs, bit):
    other = lax.ppermute(values, axis, pairs)
    return jnp.where(bit == 0, jnp.stack([values, other]), jnp.stack([other, values]))


def gather_small(values, *later):
    if not by_hand():
        shape = tuple(lax.axis_size(axis) for axis in ALL)
        return lax.all_gather(values, ALL, axis=0).reshape(shape + values.shape), *later
    z = lax.axis_index("narrow")
    values = doubled(values, "narrow", NEAR, z % 2)
    values = doubled(values, "narrow", SKIP, z // 2)
    values, *later = tie(values, *later)
    values = values.reshape((4,) + values.shape[2:])
    for axis in ("c", "x", "y"):
        values = doubled(values, axis, SWAP, lax.axis_index(axis))
    return values[None], *later


def sum_small(values):
    if not by_hand():
        return lax.psum_scatter(values, ALL, scatter_dimension=0, tiled=False)
    z = lax.axis_index("narrow")
    values = values.reshape((2, 2, 2, 2, 2) + values.shape[1:])
    bits = [("c", SWAP, lax.axis_index("c"), 2), ("x", SWAP, lax.axis_index("x"), 1), ("y", SWAP, lax.axis_index("y"), 0), ("narrow", NEAR, z % 2, 1), ("narrow", SKIP, z // 2, 0)]
    for axis, pairs, bit, dim in bits:
        keep = lax.dynamic_index_in_dim(values, bit, dim, keepdims=False)
        send = lax.dynamic_index_in_dim(values, 1 - bit, dim, keepdims=False)
        values = keep + lax.ppermute(send, axis, pairs)
    return values


def anywhere():
    return pl.BlockSpec(memory_space=pl.ANY)


def scalars():
    return pl.BlockSpec(memory_space=pltpu.SMEM)


def once(shape):
    return pl.BlockSpec(shape, lambda i: (0,) * len(shape), pipeline_mode=pl.Buffered(1))


def held_like(piece):
    return pltpu.VMEM((piece.shape[0], 4) + piece.shape[1:], BF16)


def call(kernel, name, grid, inputs, in_specs, outs, scratch, microseconds):
    results = pl.pallas_call(
        kernel,
        grid=(grid,),
        in_specs=in_specs,
        out_specs=[spec for spec, _, _ in outs],
        out_shape=[jax.ShapeDtypeStruct(shape, kind) for _, shape, kind in outs],
        scratch_shapes=scratch,
        compiler_params=PARAMS,
        cost_estimate=pl.CostEstimate(flops=int(microseconds * 1e9), bytes_accessed=20_000_000, transcendentals=0),
        name=name,
    )(*inputs)
    return list(results)


def local(tokens, doc_lengths, gain_attn, w_query, w_key, w_value, w_beta, conv_query, conv_key, conv_value, gain_head, w_out, gain_ffn, w_gate, w_up, w_down, cotangent):
    x_low = tokens[0]
    dy_low = cotangent[0]
    length, width = x_low.shape
    heads = w_beta.shape[1]
    mine = heads // GROUP
    cols = mine * DK
    three = 3 * cols
    count = conv_query.shape[0]
    total = 4 * length
    y_at, x_at, c_at, z_at = [lax.axis_index(axis) for axis in ("y", "x", "c", "narrow")]
    me = lax.axis_index(SLICES)
    where = jnp.stack([z_at, z_at ^ 1, z_at ^ 2, z_at ^ 3] if by_hand() else [0, 1, 2, 3])
    where = jnp.append(where, c_at)

    lengths = jnp.pad(doc_lengths.astype(BF16), ((0, 0), (0, gain_attn.shape[0] - doc_lengths.shape[1])))
    small = jnp.concatenate([gain_attn[None], gain_ffn[None], conv_query, conv_key, conv_value, w_beta.T, lengths])
    small, w_down, w_query = gather_small(small, w_down, w_query)

    def across(weights):
        rows = weights[0].shape[0]
        parts = jnp.concatenate([w.reshape(rows, GROUP, -1) for w in weights], axis=2)
        return lax.all_to_all(parts.transpose(1, 0, 2), SLICES, 0, 0, tiled=True)

    def blocked(weight):
        return jnp.moveaxis(weight.reshape(weight.shape[:-1] + (GROUP, -1)), -2, 0)

    x_low, small = tie(x_low, small)
    xs = gather_group(x_low)
    mixer_mine = across((w_query, w_key, w_value))
    hidden_mine = across((w_gate, w_up))
    if by_hand():
        down_w = spread_first(w_down[None])
        mixer_mine, *down_w = tie(mixer_mine, *down_w)
        mixer_w = spread_first(jnp.concatenate([mixer_mine, blocked(w_out)], axis=2))
        *mixer_w, xs[1], xs[2], xs[3] = tie(*mixer_w, *xs[1:])
        mixer_w = all_four(*spread_last(*mixer_w))
        hidden_mine, *rest = tie(hidden_mine, *mixer_w, *down_w)
        mixer_w, down_w = rest[:4], spread_last(*rest[4:])
        hidden_w = lax.all_gather(hidden_mine, ("c", "narrow"), axis=0).reshape((2, 4) + hidden_mine.shape)
    else:
        full = jnp.concatenate([spread_columns(mixer_mine), blocked(spread_rows(w_out))], axis=3)
        mixer_w = [full[:, n] for n in range(4)]
        full = spread_columns(hidden_mine).transpose(1, 0, 2, 3)
        other = lax.ppermute(full, "c", SWAP)
        hidden_w = jnp.stack([jnp.where(c_at == 0, full, other), jnp.where(c_at == 0, other, full)])
        full = spread_rows(w_down)[None]
        down_w = [full[:, n] for n in range(4)]
    mixer_w = with_partner(mixer_w)

    lengths = small[..., -1, : doc_lengths.shape[1]].astype(jnp.int32)
    lengths = lax.dynamic_index_in_dim(lengths, lax.axis_index("far"), 0, keepdims=False)
    lengths = lax.dynamic_index_in_dim(lengths, c_at, 2, keepdims=False)
    lengths = lax.dynamic_index_in_dim(lengths, z_at, 2, keepdims=False).reshape(4, -1)
    order = [(y_at ^ dy) * 2 + (x_at ^ dx) for dy in (0, 1) for dx in (0, 1)]
    ends = jnp.cumsum(jnp.take(lengths, jnp.stack(order), axis=0), axis=1)[:, :-1]
    wide = small.reshape((-1,) + small.shape[-2:]).transpose(1, 0, 2).reshape(small.shape[-2], width)
    gain_one = wide[0:1].astype(F32)
    gain_two = wide[1:2].astype(F32)
    pair = jnp.stack([me, me ^ 1])
    taps = jnp.take(wide[2 : 2 + 3 * count].reshape(3, count, GROUP, cols), pair, axis=2)
    taps = taps.transpose(1, 2, 0, 3).reshape(count, 2 * three).astype(F32)
    wbeta = jnp.take(wide[2 + 3 * count : -1].reshape(GROUP, mine, width), pair, axis=0).reshape(2 * mine, width)
    wbeta = jnp.pad(wbeta, ((0, DK - 2 * mine), (0, 0)))
    gain_h = gain_head.astype(F32)[None]

    dy_low, mixer_w[1][3] = tie(dy_low, mixer_w[1][3])
    dys = gather_group(dy_low)
    half = length // 2
    row_spec = whole((length, width))
    sums = [(once(shape), shape, BF16) for shape in ((length, width), (2, half, width), (2, half, width), (half, width), (half, width))]
    kept = [((length, 2 * three), F32), ((length, DK), F32), ((2 * mine, length, length), F32), ((2 * mine, length, DK), F32), ((2 * mine, length, DK), F32)]
    constants = [whole((DK, width)), whole((count, 2 * three)), whole((1, DK))]
    mixer_held = [held_like(mixer_w[0][0]), held_like(mixer_w[0][0]), pltpu.SemaphoreType.DMA((2, 4))]
    shapes = [((length, width), BF16)] + kept + [((length, 2 * cols), BF16)]
    results = call(
        mixer_forward,
        "mixer_forward",
        4,
        [ends, where] + xs + [gain_one, wbeta, taps, gain_h] + mixer_w[0] + mixer_w[1],
        [scalars(), scalars()] + [row_spec] * 4 + [whole((1, width))] + constants + [anywhere()] * 8,
        sums + [(each(shape), (4,) + shape, kind) for shape, kind in shapes],
        mixer_held,
        60,
    )
    y_parts, act, saved, on = results[:5], results[5], results[6:-1], results[-1]

    x = x_low.astype(F32)
    *y_parts, dys[1], dys[2], dys[3], down_w[-2], down_w[-1] = tie(*y_parts, *dys[1:], *down_w[-2:])
    down_w = with_partner(all_four(*down_w) if by_hand() else down_w)
    h1 = x + sum_group(y_parts)
    r2 = lax.rsqrt(jnp.mean(h1 * h1, axis=-1, keepdims=True) + 1e-06)
    act2 = (h1 * r2 * gain_two).astype(BF16)
    act2s = gather_group(act2)

    hidden = down_w[0][0].shape[1] * 4
    row_pairs = [(pl.BlockSpec((2 * length, n), lambda i: (i, 0)), (total, n), BF16) for n in (hidden, hidden, 2 * hidden, 2 * hidden)]
    results = call(
        feed_forward,
        "feed_forward",
        2,
        [where] + act2s + dys + [hidden_w] + down_w[0] + down_w[1],
        [scalars()] + [row_spec] * 8 + [anywhere()] * 9,
        sums + sums + row_pairs,
        [held_like(hidden_w[0, 0])] * 2 + [held_like(down_w[0][0])] * 2 + [pltpu.SemaphoreType.DMA((4, 4))],
        60,
    )
    out_parts, dact2_parts, hids, dgus = results[:5], results[5:10], results[10:12], results[12:14]

    block = width // GROUP
    columns_spec = pl.BlockSpec((length, block), lambda i: (0, i))
    grad_gu = call(
        gate_up_grads,
        "gate_up_grads",
        GROUP,
        [where] + act2s + dgus,
        [scalars()] + [columns_spec] * 4 + [whole(dgu.shape) for dgu in dgus],
        [(pl.BlockSpec((4, 2, 1, block // 4, 2 * hidden), lambda i: (0, 0, i, 0, 0)), (4, 2, GROUP, block // 4, 2 * hidden), BF16)],
        [],
        16,
    )[0]
    grad_second, grad_gu = sum_group(dact2_parts, grad_gu)
    scaled = grad_second * gain_two
    dh1 = dy_low.astype(F32) + r2 * scaled - h1 * (r2 * r2 * r2 * jnp.mean(h1 * scaled, axis=-1, keepdims=True))
    grad_gain_ffn = jnp.sum(grad_second * h1 * r2, axis=0)
    dy1 = dh1.astype(BF16)
    dy1s = gather_group(dy1)

    grad_down = call(
        down_grads,
        "down_grads",
        GROUP,
        [where] + hids + dys,
        [scalars()] + [whole(hid.shape) for hid in hids] + [columns_spec] * 4,
        [(pl.BlockSpec((4, 2, hidden // 4, block), lambda i: (0, 0, 0, i)), (4, 2, hidden // 4, width), BF16)],
        [],
        8,
    )[0]
    *out_parts, grad_down, dy1s[1], dy1s[2], dy1s[3] = tie(*out_parts, grad_down, *dy1s[1:])
    if by_hand():
        grad_gu = lax.psum_scatter(grad_gu.reshape(-1, 2 * hidden), ("narrow", "c"), scatter_dimension=0, tiled=True)
        grad_gu = to_owners(grad_gu.reshape(GROUP, -1, 2 * hidden))
        grad_down = lax.psum_scatter(grad_down.reshape(-1, width), ("narrow", "c"), scatter_dimension=0, tiled=True)
    else:
        grad_gu = [lax.dynamic_index_in_dim(grad_gu, at, 1, keepdims=False) for at in (c_at, 1 - c_at)]
        grad_gu = to_owners(collect_columns(*grad_gu))
        grad_down = collect_rows(*[lax.dynamic_index_in_dim(grad_down, at, 1, keepdims=False) for at in (c_at, 1 - c_at)])

    shapes = [((length, 2 * three), BF16), ((length, DK), BF16)]
    results = call(
        mixer_backward,
        "mixer_backward",
        4,
        [ends, where] + dy1s + saved + [wbeta, taps, gain_h] + mixer_w[0] + mixer_w[1],
        [scalars(), scalars()] + [row_spec] * 4 + [each(shape) for shape, _ in kept] + constants + [anywhere()] * 8,
        sums
        + [(each(shape), (4,) + shape, kind) for shape, kind in shapes]
        + [(once((count, 2 * three)), (count, 2 * three), F32), (once((1, DK)), (1, DK), F32)],
        mixer_held,
        60,
    )
    (dqkv, dbl, dtaps, dgain) = results[5:]
    total_out, *dact_parts = sum_group(out_parts, *results[:5])
    result = (h1 + total_out).astype(BF16)
    *grad_mixer, grad_wbeta = call(
        mixer_grads,
        "mixer_grads",
        GROUP,
        [where, act.reshape(total, width), dqkv.reshape(total, 2 * three), on.reshape(total, 2 * cols), dbl.reshape(total, DK)] + dy1s,
        [scalars(), pl.BlockSpec((total, block), lambda i: (0, i)), whole((total, 2 * three)), whole((total, 2 * cols)), whole((total, DK))] + [columns_spec] * 4,
        [(pl.BlockSpec((4, 1, block // 4, three + block), lambda i: (0, i, 0, 0)), (4, GROUP, block // 4, three + block), BF16)] * 2
        + [(pl.BlockSpec((DK, block), lambda i: (0, i)), (DK, width), F32)],
        [pltpu.VMEM((block, three + block), BF16)],
        15,
    )
    if by_hand():
        grad_mixer, grad_gu = collect(*grad_mixer, grad_gu)
        grad_out = grad_mixer[:, :, three:].transpose(1, 0, 2).reshape(-1, width)
        grad_qkv = to_owners(grad_mixer[:, :, :three])
    else:
        grad_out = [part[..., three:].transpose(0, 2, 1, 3).reshape(4, -1, width) for part in grad_mixer]
        grad_out = collect_rows(*grad_out)
        grad_qkv = to_owners(collect_columns(*[part[..., :three] for part in grad_mixer]))
    grad_qkv = grad_qkv.reshape(-1, GROUP, 3, cols)

    grad_act = sum_group(dact_parts)
    r1 = lax.rsqrt(jnp.mean(x * x, axis=-1, keepdims=True) + 1e-06)
    scaled = grad_act * gain_one
    grad_input = (dh1 + r1 * scaled - x * (r1 * r1 * r1 * jnp.mean(x * scaled, axis=-1, keepdims=True))).astype(BF16)
    grad_gain_attn = jnp.sum(grad_act * x * r1, axis=0)

    at = (jnp.arange(GROUP)[:, None] == pair[None, :]).astype(F32)
    dtaps = dtaps.reshape(count, 2, 3, cols)
    dtaps = (at[:, 0, None, None, None] * dtaps[None, :, 0] + at[:, 1, None, None, None] * dtaps[None, :, 1]).transpose(2, 1, 0, 3)
    dbeta = grad_wbeta[: 2 * mine].reshape(2, mine, width)
    dbeta = at[:, 0, None, None] * dbeta[None, 0] + at[:, 1, None, None] * dbeta[None, 1]
    smalls = jnp.concatenate([grad_gain_attn[None], grad_gain_ffn[None], dtaps.reshape(3 * count, width), dbeta.reshape(heads, width)])
    smalls = smalls.reshape(smalls.shape[0], lax.axis_size(ALL), -1).transpose(1, 0, 2)
    dgain = jnp.broadcast_to(dgain.reshape(1, -1, smalls.shape[2]), (smalls.shape[0], DK // smalls.shape[2], smalls.shape[2]))
    smalls = sum_small(jnp.concatenate([smalls, dgain], axis=1))
    last = 2 + 3 * count + heads

    return (
        result[None],
        grad_input[None],
        smalls[0],
        grad_qkv[:, :, 0].reshape(-1, width),
        grad_qkv[:, :, 1].reshape(-1, width),
        grad_qkv[:, :, 2].reshape(-1, width),
        smalls[2 + 3 * count : last].T,
        smalls[2 : 2 + count],
        smalls[2 + count : 2 + 2 * count],
        smalls[2 + 2 * count : 2 + 3 * count],
        smalls[last:].reshape(-1),
        grad_out,
        smalls[1],
        grad_gu[:, :, :hidden].reshape(grad_gu.shape[0], -1),
        grad_gu[:, :, hidden:].reshape(grad_gu.shape[0], -1),
        grad_down.astype(F32),
    )


def solution(mesh):
    wide, narrow = mesh.shape["wide"], mesh.shape["narrow"]
    inner = Mesh(mesh.devices.reshape(wide // GROUP, 2, 2, 2, narrow), ALL)
    rows = P(ALL, None)
    columns = P(None, ALL)
    vector = P(ALL)
    cube = P(ALL, None, None)
    return jax.shard_map(
        local,
        mesh=inner,
        in_specs=(cube, rows, vector, rows, rows, rows, rows, columns, columns, columns, P(), rows, vector, rows, rows, rows, cube),
        out_specs=(cube, cube, vector, rows, rows, rows, rows, columns, columns, columns, P(), rows, vector, rows, rows, rows),
        check_vma=False,
    )
```

```python
from functools import partial

import jax
import jax.numpy as jnp
from jax import lax
from jax.experimental import pallas as pl
from jax.experimental.pallas import tpu as pltpu
from jax.sharding import Mesh
from jax.sharding import PartitionSpec as P

F32 = jnp.float32
BF16 = jnp.bfloat16
DK = 128
GROUP = 8
SLICES = ("y", "x", "c")
REST = ("far", "narrow")
ALL = ("far", "y", "x", "c", "narrow")
SWAP = [(0, 1), (1, 0)]
NEAR = [(0, 1), (1, 0), (2, 3), (3, 2)]
SKIP = [(0, 2), (2, 0), (1, 3), (3, 1)]
MIDDLE = [(1, 2), (2, 1)]
ACROSS = [(0, 3), (3, 0), (1, 2), (2, 1)]

NN = (((1,), (0,)), ((), ()))
NT = (((1,), (1,)), ((), ()))
TN = (((0,), (0,)), ((), ()))


def dot(left, right, dims=NN):
    return lax.dot_general(left, right, dims, preferred_element_type=F32)


def halves(value):
    high = value.astype(BF16)
    return high, (value - high.astype(F32)).astype(BF16)


def fine(left, right, dims=NN):
    left_high, left_low = halves(left)
    right_high, right_low = halves(right)
    return dot(left_high, right_high, dims) + (dot(left_high, right_low, dims) + dot(left_low, right_high, dims))


def semi(left, right, dims=NN):
    left_high, left_low = halves(left)
    return dot(left_high, right, dims) + dot(left_low, right, dims)


def plain(left, right, dims=NN):
    return dot(left.astype(BF16), right.astype(BF16), dims)


def documents(ends_ref, seq, shape, axis):
    place = lax.broadcasted_iota(jnp.int32, shape, axis)
    doc = jnp.zeros(shape, jnp.int32)
    first = jnp.zeros(shape, jnp.int32)
    for j in range(ends_ref.shape[1]):
        end = ends_ref[seq, j]
        past = place >= end
        doc = doc + past.astype(jnp.int32)
        first = jnp.where(past, end, first)
    return doc, place - first


def inverses(lowers, size):
    row = lax.broadcasted_iota(jnp.int32, (size, size), 0)
    col = lax.broadcasted_iota(jnp.int32, (size, size), 1)
    apart = row ^ col
    eye = (row == col).astype(F32)
    results = [eye - jnp.where(apart == 1, lower, 0.0) for lower in lowers]
    half = 2
    while half < size:
        pair = jnp.logical_and(apart >= half, apart < 2 * half)
        parts = [jnp.where(pair, lower, 0.0) for lower in lowers]
        middles = [fine(part, result) for part, result in zip(parts, results)]
        results = [result - fine(result, middle) for middle, result in zip(middles, results)]
        half *= 2
    return results


def conv(values, taps, keeps):
    total = values * taps[0]
    for j in range(1, len(taps)):
        total = total + jnp.where(keeps[j], pltpu.roll(values, j, 0), 0.0) * taps[j]
    return total


def pieces_of(refs, held, sems, where_ref):
    return [pltpu.make_async_copy(ref, held.at[:, where_ref[n]], sems.at[n]) for n, ref in enumerate(refs)]


def side_of(ref, side, held, sems):
    return [pltpu.make_async_copy(ref.at[side, n], held.at[:, n], sems.at[n]) for n in range(4)]


def start_all(groups):
    for copies in groups:
        for copy in copies:
            copy.start()


def wait_all(groups):
    for copies in groups:
        for copy in copies:
            copy.wait()


def at_first(action, groups):
    pl.when(pl.program_id(0) == 0)(lambda: action(groups))


def flat(value):
    return value.reshape(-1, value.shape[-1])


def chosen(*refs):
    value = refs[0][...]
    for n, ref in enumerate(refs[1:], 1):
        value = jnp.where(pl.program_id(0) == n, ref[...], value)
    return value


def hand_out(step, refs, value):
    own_ref, by_x_ref, by_y_ref, x_low_ref, y_top_ref = refs
    half = value.shape[0] // 2

    @pl.when(step == 0)
    def _():
        own_ref[...] = value

    @pl.when(step == 1)
    def _():
        by_x_ref[0] = value[:half]
        x_low_ref[...] = value[half:]

    @pl.when(step == 2)
    def _():
        y_top_ref[...] = value[:half]
        by_y_ref[0] = value[half:]

    @pl.when(step == 3)
    def _():
        by_x_ref[1] = value[:half]
        by_y_ref[1] = value[half:]


def masks(ends_ref, seq, rows, taps):
    _, pos = documents(ends_ref, seq, (rows, DK), 0)
    doc_r, _ = documents(ends_ref, seq, (rows, rows), 0)
    doc_c, _ = documents(ends_ref, seq, (rows, rows), 1)
    row = lax.broadcasted_iota(jnp.int32, (rows, rows), 0)
    col = lax.broadcasted_iota(jnp.int32, (rows, rows), 1)
    same = doc_r == doc_c
    return [pos >= j for j in range(taps)], jnp.logical_and(same, row > col), jnp.logical_and(same, row >= col)


def mixer_forward(ends_ref, where_ref, x0_ref, x1_ref, x2_ref, x3_ref, gain_one_ref, wbeta_ref, taps_ref, gain_ref, *rest):
    w_refs = rest[:4], rest[4:8]
    out_refs, rest = rest[8:13], rest[13:]
    act_ref, p_ref, bl_ref, t_ref, u_ref, o_ref, on_ref, w0, w1, sems = rest
    held = (w0, w1)
    seq = pl.program_id(0)

    loads = [pieces_of(w_refs[side], held[side], sems.at[side], where_ref) for side in (0, 1)]
    at_first(start_all, loads)
    rows = x0_ref.shape[0]
    cols = on_ref.shape[2] // 2
    heads = cols // DK
    half = rows // 2
    count = taps_ref.shape[0]
    x = chosen(x0_ref, x1_ref, x2_ref, x3_ref).astype(F32)
    act = (x * lax.rsqrt(jnp.mean(x * x, axis=-1, keepdims=True) + 1e-06) * gain_one_ref[...]).astype(BF16)
    act_ref[0] = act
    projs = []
    for side in (0, 1):
        at_first(wait_all, loads[side : side + 1])
        proj = dot(act, flat(held[side][:, :, :, : 3 * cols]))
        p_ref[0, :, side * 3 * cols : (side + 1) * 3 * cols] = proj
        projs.append(proj)
    logit = dot(act, wbeta_ref[...], NT)
    bl_ref[0] = logit
    beta_all = jax.nn.sigmoid(logit)
    keeps, strict, causal = masks(ends_ref, seq, rows, count)
    gain = gain_ref[...]
    every = range(2 * heads)

    def part(kind, head):
        side, first = head // heads, kind * cols + (head % heads) * DK
        at = side * 3 * cols + first
        taps = [taps_ref[j : j + 1, at : at + DK] for j in range(count)]
        c = conv(projs[side][:, first : first + DK], taps, keeps)
        return c * jax.nn.sigmoid(c)

    def unit(u):
        return u * lax.rsqrt(jnp.sum(u * u, axis=-1, keepdims=True) + 1e-06)

    qs = [unit(part(0, head)).astype(BF16) for head in every]
    ks = [unit(part(1, head)).astype(BF16) for head in every]
    lowers = [jnp.where(strict, dot(ks[head], ks[head], NT), 0.0) * beta_all[:, head : head + 1] for head in every]
    blocks = inverses([block for lower in lowers for block in (lower[:half, :half], lower[half:, half:])], half)
    ons = []
    for head in every:
        v = part(2, head).astype(BF16)
        beta = beta_all[:, head : head + 1]
        top, low = blocks[2 * head], blocks[2 * head + 1]
        cross = -fine(low, fine(lowers[head][half:, :half], top))
        t_ref[0, head, :half, :half] = top
        t_ref[0, head, :half, half:] = jnp.zeros((half, half), F32)
        t_ref[0, head, half:, :half] = cross
        t_ref[0, head, half:, half:] = low
        target = v.astype(F32) * beta
        u_top = fine(top, target[:half])
        u_low = fine(cross, target[:half]) + fine(low, target[half:])
        u = jnp.concatenate([u_top, u_low], axis=0)
        u_ref[0, head] = u
        o = fine(jnp.where(causal, dot(qs[head], ks[head], NT), 0.0), u)
        o_ref[0, head] = o
        on = o * lax.rsqrt(jnp.mean(o * o, axis=-1, keepdims=True) + 1e-05) * gain
        ons.append(on.astype(BF16))
    on = jnp.concatenate(ons, axis=1)
    on_ref[0] = on
    y = []
    for block in range(w0.shape[0]):
        parts = [dot(on[:, side * cols : (side + 1) * cols], flat(held[side][block, :, :, 3 * cols :])) for side in (0, 1)]
        y.append((parts[0] + parts[1]).astype(BF16))
    hand_out(seq, out_refs, jnp.concatenate(y, axis=1))


def mixer_backward(ends_ref, where_ref, dy0_ref, dy1_ref, dy2_ref, dy3_ref, p_ref, bl_ref, t_ref, u_ref, o_ref, wbeta_ref, taps_ref, gain_ref, *rest):
    w_refs = rest[:4], rest[4:8]
    out_refs, rest = rest[8:13], rest[13:]
    dqkv_ref, dbl_ref, dtaps_ref, dgain_ref, w0, w1, sems = rest
    held = (w0, w1)
    seq = pl.program_id(0)
    rows = dy0_ref.shape[0]
    cols = p_ref.shape[2] // 6
    heads = cols // DK
    count = taps_ref.shape[0]

    loads = [pieces_of(w_refs[side], held[side], sems.at[side], where_ref) for side in (0, 1)]
    at_first(start_all, loads)

    @pl.when(seq == 0)
    def _():
        dtaps_ref[...] = jnp.zeros_like(dtaps_ref)
        dgain_ref[...] = jnp.zeros_like(dgain_ref)

    dy = chosen(dy0_ref, dy1_ref, dy2_ref, dy3_ref)
    dons = []
    for side in (0, 1):
        at_first(wait_all, loads[side : side + 1])
        don = 0.0
        for block in range(w0.shape[0]):
            weight = flat(held[side][block, :, :, 3 * cols :])
            don = don + dot(dy[:, block * weight.shape[1] : (block + 1) * weight.shape[1]], weight, NT)
        dons.append(don)
    beta_all = jax.nn.sigmoid(bl_ref[0])
    keeps, strict, causal = masks(ends_ref, seq, rows, count)
    gain = gain_ref[...]
    lane = lax.broadcasted_iota(jnp.int32, (rows, DK), 1)
    dbl_total = jnp.zeros((rows, DK), F32)

    def taps_of(first):
        return [taps_ref[j : j + 1, first : first + DK] for j in range(count)]

    def conv_back(first, dc):
        p = p_ref[0, :, first : first + DK]
        taps = taps_of(first)
        dp = dc * taps[0]
        dtaps_ref[0:1, first : first + DK] += jnp.sum(dc * p, axis=0, keepdims=True)
        for j in range(1, count):
            kept = jnp.where(keeps[j], dc, 0.0)
            dp = dp + pltpu.roll(kept, rows - j, 0) * taps[j]
            dtaps_ref[j : j + 1, first : first + DK] += jnp.sum(kept * pltpu.roll(p, j, 0), axis=0, keepdims=True)
        return dp

    def parts(first):
        c = conv(p_ref[0, :, first : first + DK], taps_of(first), keeps)
        sigma = jax.nn.sigmoid(c)
        return c * sigma, sigma * (1.0 + c * (1.0 - sigma))

    def unit_back(u, norm, grad):
        return norm * grad - u * (norm * norm * norm * jnp.sum(u * grad, axis=-1, keepdims=True))

    grads = [[None] * (3 * heads) for _ in (0, 1)]
    for head in range(2 * heads):
        side, at = head // heads, head % heads
        firsts = [side * 3 * cols + kind * cols + at * DK for kind in range(3)]
        uq, slope_q = parts(firsts[0])
        uk, slope_k = parts(firsts[1])
        uv, slope_v = parts(firsts[2])
        norm_q = lax.rsqrt(jnp.sum(uq * uq, axis=-1, keepdims=True) + 1e-06)
        norm_k = lax.rsqrt(jnp.sum(uk * uk, axis=-1, keepdims=True) + 1e-06)
        q = (uq * norm_q).astype(BF16)
        k = (uk * norm_k).astype(BF16)
        v = uv.astype(BF16).astype(F32)
        beta = beta_all[:, head : head + 1]
        o = o_ref[0, head]
        don = dons[side][:, at * DK : (at + 1) * DK]
        r = lax.rsqrt(jnp.mean(o * o, axis=-1, keepdims=True) + 1e-05)
        scaled = don * gain
        dgain_ref[...] += jnp.sum(don * o * r, axis=0, keepdims=True)
        do = r * scaled - o * (r * r * r * jnp.mean(o * scaled, axis=-1, keepdims=True))
        u = u_ref[0, head]
        inner = dot(k, k, NT)
        scores = jnp.where(causal, dot(q, k, NT), 0.0)
        du = fine(scores, do, TN)
        dscores = jnp.where(causal, fine(do, u, NT), 0.0)
        dq = semi(dscores, k)
        dk = semi(dscores, q, TN)
        w = fine(t_ref[0, head], du, TN)
        dv = beta * w
        dlower = jnp.where(strict, fine(w, u, NT), 0.0)
        dbeta = jnp.sum(w * v, axis=-1, keepdims=True) - jnp.sum(dlower * inner, axis=-1, keepdims=True)
        dinner = dlower * beta
        dk = dk - semi(dinner, k) - semi(dinner, k, TN)
        dbl_total = jnp.where(lane == head, dbeta * beta * (1.0 - beta), dbl_total)
        grads[side][at] = conv_back(firsts[0], unit_back(uq, norm_q, dq) * slope_q).astype(BF16)
        grads[side][heads + at] = conv_back(firsts[1], unit_back(uk, norm_k, dk) * slope_k).astype(BF16)
        grads[side][2 * heads + at] = conv_back(firsts[2], dv * slope_v).astype(BF16)
    dbl = dbl_total.astype(BF16)
    dbl_ref[0] = dbl
    dact = dot(dbl, wbeta_ref[...])
    for side in (0, 1):
        dqkv = jnp.concatenate(grads[side], axis=1)
        dqkv_ref[0, :, side * 3 * cols : (side + 1) * 3 * cols] = dqkv
        dact = dact + dot(dqkv, flat(held[side][:, :, :, : 3 * cols]), NT)
    hand_out(seq, out_refs, dact.astype(BF16))


def hidden_units(where_ref, *rest):
    acts, dys, wgu_ref, wd_refs = rest[:4], rest[4:8], rest[8], (rest[9:13], rest[13:17])
    hid_refs, dgu_refs, wgu, wd, sems = rest[17:19], rest[19:21], rest[21:23], rest[23:25], rest[25]
    core = where_ref[4]
    loads = []
    for side, at in enumerate((core, 1 - core)):
        loads.append(pieces_of(wd_refs[side], wd[side], sems.at[2 + side], where_ref))
        loads.append(side_of(wgu_ref, at, wgu[side], sems.at[side]))
    at_first(start_all, loads)
    hidden = hid_refs[0].shape[1]
    act = jnp.concatenate([chosen(acts[0], acts[2]), chosen(acts[1], acts[3])])
    dy = jnp.concatenate([chosen(dys[0], dys[2]), chosen(dys[1], dys[3])])
    for side in (0, 1):
        at_first(wait_all, loads[2 * side : 2 * side + 1])
        dhid = dot(dy, flat(wd[side][...]), NT)
        at_first(wait_all, loads[2 * side + 1 : 2 * side + 2])
        gu = dot(act, flat(wgu[side][...]))
        gt, up = gu[:, :hidden], gu[:, hidden:]
        sigma = jax.nn.sigmoid(gt)
        swish = gt * sigma
        hid_refs[side][...] = (swish * up).astype(BF16)
        dgt = (dhid * up * sigma * (1.0 + gt * (1.0 - sigma))).astype(BF16)
        dup = (dhid * swish).astype(BF16)
        dgu_refs[side][...] = jnp.concatenate([dgt, dup], axis=1)


def hidden_back(where_ref, dgu0_ref, dgu1_ref, wgu_ref, *rest):
    dact_refs, wgu, sems = rest[:5], rest[5:7], rest[7]
    step = pl.program_id(0)
    core = where_ref[4]
    loads = [side_of(wgu_ref, at, wgu[side], sems.at[side]) for side, at in enumerate((core, 1 - core))]
    at_first(start_all, loads)
    dact = 0.0
    for side, dgu_ref in enumerate((dgu0_ref, dgu1_ref)):
        at_first(wait_all, loads[side : side + 1])
        dact = dact + dot(dgu_ref[...], flat(wgu[side][...]), NT)
    rows = dact.shape[0] // 2
    for part in (0, 1):
        hand_out(2 * step + part, dact_refs, dact[part * rows : (part + 1) * rows].astype(BF16))


def hidden_out(where_ref, hid0_ref, hid1_ref, *rest):
    wd_refs, out_refs, wd, sems = (rest[:4], rest[4:8]), rest[8:13], rest[13:15], rest[15]
    step = pl.program_id(0)
    loads = [pieces_of(wd_refs[side], wd[side], sems.at[side], where_ref) for side in (0, 1)]
    at_first(start_all, loads)
    out = 0.0
    for side, hid_ref in enumerate((hid0_ref, hid1_ref)):
        at_first(wait_all, loads[side : side + 1])
        out = out + dot(hid_ref[...], flat(wd[side][...]))
    rows = out.shape[0] // 2
    for part in (0, 1):
        hand_out(2 * step + part, out_refs, out[part * rows : (part + 1) * rows].astype(BF16))


def gate_up_grads(where_ref, *rest):
    acts, dgus, out = rest[:4], (rest[4], rest[5]), rest[6]
    act = jnp.concatenate([ref[...] for ref in acts])
    rows = act.shape[1] // 4
    core = where_ref[4]
    for at, side in ((core, 0), (1 - core, 1)):
        value = dot(act, dgus[side][...], TN).astype(BF16)
        for n in range(4):
            out[n, at, 0] = value[n * rows : (n + 1) * rows]


def down_grads(where_ref, *rest):
    hids, dys, out = (rest[0], rest[1]), rest[2:6], rest[6]
    dy = jnp.concatenate([ref[...] for ref in dys])
    rows = hids[0].shape[1] // 4
    core = where_ref[4]
    for at, side in ((core, 0), (1 - core, 1)):
        value = dot(hids[side][...], dy, TN).astype(BF16)
        for n in range(4):
            out[n, at] = value[n * rows : (n + 1) * rows]


def mixer_grads(where_ref, act_ref, dqkv_ref, on_ref, dbl_ref, *rest):
    dys, out_ref, beta_ref = rest[:4], rest[4], rest[5]
    act = act_ref[...]
    beta_ref[...] = dot(dbl_ref[...], act, TN)
    dy = jnp.concatenate([ref[...] for ref in dys])
    three, cols = dqkv_ref.shape[1] // 2, on_ref.shape[1] // 2
    rows = act.shape[1] // 4
    core = where_ref[4]
    for at, side in ((core, 0), (1 - core, 1)):
        qkv = dot(act, dqkv_ref[:, side * three : (side + 1) * three], TN)
        out = dot(on_ref[:, side * cols : (side + 1) * cols], dy, TN)
        value = jnp.concatenate([qkv, out], axis=1).astype(BF16)
        for n in range(4):
            out_ref[n, at, 0] = value[n * rows : (n + 1) * rows]


def in_order(*refs):
    value, outs = refs[0], refs[1:]
    width = value.shape[2] // len(outs)
    for n, out in enumerate(outs):
        parts = [value[block, :, n * width : (n + 1) * width].astype(F32) for block in range(value.shape[0])]
        out[...] = jnp.concatenate(parts, axis=1)


def whole(shape):
    return pl.BlockSpec(shape, lambda i: (0,) * len(shape), pipeline_mode=pl.Buffered(1))


def each(shape):
    return pl.BlockSpec((1,) + shape, lambda i: (i,) + (0,) * len(shape))


PARAMS = pltpu.CompilerParams(vmem_limit_bytes=60 * 1024 * 1024, dimension_semantics=("arbitrary",))


def tie(*values):
    return lax.optimization_barrier(values)


def gather_group(own):
    return [own, lax.ppermute(own, "x", SWAP), lax.ppermute(own, "y", SWAP), lax.ppermute(own, ("y", "x"), ACROSS)]


def joined(left, right):
    return left.astype(F32) + right.astype(F32)


def sum_first(parts):
    own, by_x, by_y, x_low, y_top = parts
    return [lax.ppermute(by_x, "x", SWAP), lax.ppermute(by_y, "y", SWAP), own, x_low, y_top]


def sum_second(got_x, got_y, own, x_low, y_top):
    y_top = lax.ppermute(joined(y_top, got_x[1]).astype(BF16), "y", SWAP)
    x_low = lax.ppermute(joined(x_low, got_y[1]).astype(BF16), "x", SWAP)
    return [x_low, y_top, own, got_x, got_y]


def sum_last(x_low, y_top, own, got_x, got_y):
    half = x_low.shape[0]
    top = joined(own[:half], got_x[0]) + y_top.astype(F32)
    low = joined(own[half:], got_y[0]) + x_low.astype(F32)
    return jnp.concatenate([top, low])


def by_hand():
    return lax.axis_size("far") == 1 and lax.axis_size("narrow") == 4


def with_partner(pieces):
    return pieces, [lax.ppermute(piece, "c", SWAP) for piece in pieces]


def spread_first(mine):
    return [mine, lax.ppermute(mine, "narrow", NEAR), lax.ppermute(mine, "narrow", SKIP)]


def spread_last(mine, near, skip):
    return [mine, near, skip, lax.ppermute(mine, "narrow", MIDDLE), lax.ppermute(skip, "narrow", [(2, 3), (1, 0)])]


def all_four(mine, near, skip, middle, end):
    z = lax.axis_index("narrow")
    return [mine, near, skip, jnp.where((z == 1) | (z == 2), middle, end)]


def spread_columns(mine):
    far, narrow = lax.axis_size("far"), lax.axis_size("narrow")
    _, rows, columns = mine.shape
    full = lax.all_gather(mine, REST, axis=0).reshape(far, narrow, GROUP, rows, columns).transpose(0, 2, 1, 3, 4)
    return full.reshape(GROUP, 4, -1, columns)


def spread_rows(weight):
    full = lax.all_gather(weight, ALL, axis=0, tiled=True)
    total = full.shape[0] // GROUP
    return lax.dynamic_slice_in_dim(full, lax.axis_index(SLICES) * total, total, 0).reshape(4, -1, full.shape[1])


def collect_columns(own, other):
    full = joined(own, lax.ppermute(other, "c", SWAP)).astype(BF16)
    columns = full.shape[-1]
    far, narrow = lax.axis_size("far"), lax.axis_size("narrow")
    full = full.transpose(1, 0, 2, 3).reshape(far, GROUP, narrow, -1, columns).transpose(0, 2, 1, 3, 4)
    full = lax.psum_scatter(full.reshape(-1, columns), REST, scatter_dimension=0, tiled=True)
    return full.reshape(GROUP, -1, columns).astype(F32)


def collect_rows(own, other):
    full = joined(own, lax.ppermute(other, "c", SWAP)).astype(BF16)
    full = full.reshape(1, -1, full.shape[-1])
    full = jnp.where((jnp.arange(GROUP) == lax.axis_index(SLICES))[:, None, None], full, 0)
    return lax.psum_scatter(full.reshape(-1, full.shape[-1]), ALL, scatter_dimension=0, tiled=True).astype(F32)


def to_owners(mine):
    return lax.all_to_all(mine.astype(BF16), SLICES, 0, 0, tiled=True)


def gather_small(values, late):
    if not by_hand():
        shape = tuple(lax.axis_size(axis) for axis in ALL)
        return lax.all_gather(values, ALL, axis=0).reshape(shape + values.shape), late
    values = jnp.stack([values] + [lax.ppermute(values, "narrow", pairs) for pairs in (NEAR, SKIP, ACROSS)])
    values = jnp.stack([values, lax.ppermute(values, "c", SWAP)])
    values, late = tie(values, late)
    values = jnp.stack(gather_group(values))
    here = lax.axis_index(SLICES) * 4 + lax.axis_index("narrow")
    values = jnp.take(values.reshape((-1,) + values.shape[3:]), jnp.arange(32) ^ here, axis=0)
    return values.reshape((1, 2, 2, 2, 4) + values.shape[1:]), late


def sum_small(values):
    if not by_hand():
        return lax.psum_scatter(values, ALL, scatter_dimension=0, tiled=False)
    z = lax.axis_index("narrow")
    values = values.reshape((2, 2, 2, 2, 2) + values.shape[1:])
    bits = [("c", SWAP, lax.axis_index("c"), 2), ("x", SWAP, lax.axis_index("x"), 1), ("y", SWAP, lax.axis_index("y"), 0), ("narrow", NEAR, z % 2, 1), ("narrow", SKIP, z // 2, 0)]
    for axis, pairs, bit, dim in bits:
        keep = lax.dynamic_index_in_dim(values, bit, dim, keepdims=False)
        send = lax.dynamic_index_in_dim(values, 1 - bit, dim, keepdims=False)
        values = keep + lax.ppermute(send, axis, pairs)
    return values


def anywhere():
    return pl.BlockSpec(memory_space=pl.ANY)


def scalars():
    return pl.BlockSpec(memory_space=pltpu.SMEM)


def once(shape):
    return pl.BlockSpec(shape, lambda i: (0,) * len(shape), pipeline_mode=pl.Buffered(1))


def held_like(piece):
    return pltpu.VMEM((piece.shape[0], 4) + piece.shape[1:], BF16)


def call(kernel, name, grid, inputs, in_specs, outs, scratch, microseconds):
    results = pl.pallas_call(
        kernel,
        grid=(grid,),
        in_specs=in_specs,
        out_specs=[spec for spec, _, _ in outs],
        out_shape=[jax.ShapeDtypeStruct(shape, kind) for _, shape, kind in outs],
        scratch_shapes=scratch,
        compiler_params=PARAMS,
        cost_estimate=pl.CostEstimate(flops=int(microseconds * 1e9), bytes_accessed=20_000_000, transcendentals=0),
        name=name,
    )(*inputs)
    return list(results)


def local(tokens, doc_lengths, gain_attn, w_query, w_key, w_value, w_beta, conv_query, conv_key, conv_value, gain_head, w_out, gain_ffn, w_gate, w_up, w_down, cotangent):
    x_low = tokens[0]
    dy_low = cotangent[0]
    length, width = x_low.shape
    heads = w_beta.shape[1]
    mine = heads // GROUP
    cols = mine * DK
    three = 3 * cols
    count = conv_query.shape[0]
    total = 4 * length
    y_at, x_at, c_at, z_at = [lax.axis_index(axis) for axis in ("y", "x", "c", "narrow")]
    me = lax.axis_index(SLICES)
    where = jnp.stack([z_at, z_at ^ 1, z_at ^ 2, z_at ^ 3] if by_hand() else [0, 1, 2, 3])
    chips = [(y_at ^ dy) * 2 + (x_at ^ dx) for dy in (0, 1) for dx in (0, 1)]
    where = jnp.append(where, c_at)

    def across(weights):
        rows = weights[0].shape[0]
        return jnp.concatenate([w.reshape(rows, GROUP, -1) for w in weights], axis=2).transpose(1, 0, 2)

    def to_slices(parts):
        return lax.all_to_all(parts, SLICES, 0, 0, tiled=True)

    def blocked(weight):
        return jnp.moveaxis(weight.reshape(weight.shape[:-1] + (GROUP, -1)), -2, 0)

    mixer_parts, gain_attn, gain_ffn, conv_query, conv_key, conv_value, w_beta, doc_lengths = tie(
        across((w_query, w_key, w_value)), gain_attn, gain_ffn, conv_query, conv_key, conv_value, w_beta, doc_lengths
    )
    lengths = jnp.pad(doc_lengths.astype(BF16), ((0, 0), (0, gain_attn.shape[0] - doc_lengths.shape[1])))
    small = jnp.concatenate([gain_attn[None], gain_ffn[None], conv_query, conv_key, conv_value, w_beta.T, lengths])
    mixer_mine = to_slices(mixer_parts)
    small, mixer_mine = gather_small(small, mixer_mine)
    x_low, small = tie(x_low, small)
    xs = gather_group(x_low)
    lengths = small[..., -1, : doc_lengths.shape[1]].astype(jnp.int32)
    lengths = lax.dynamic_index_in_dim(lengths, lax.axis_index("far"), 0, keepdims=False)
    lengths = lax.dynamic_index_in_dim(lengths, c_at, 2, keepdims=False)
    lengths = lax.dynamic_index_in_dim(lengths, z_at, 2, keepdims=False).reshape(4, -1)
    ends = jnp.cumsum(jnp.take(lengths, jnp.stack(chips), axis=0), axis=1)[:, :-1]
    wide = small.reshape((-1,) + small.shape[-2:]).transpose(1, 0, 2).reshape(small.shape[-2], width)
    gain_one = wide[0:1].astype(F32)
    gain_two = wide[1:2].astype(F32)
    pair = jnp.stack([me, me ^ 1])
    taps = jnp.take(wide[2 : 2 + 3 * count].reshape(3, count, GROUP, cols), pair, axis=2)
    taps = taps.transpose(1, 2, 0, 3).reshape(count, 2 * three).astype(F32)
    wbeta = jnp.take(wide[2 + 3 * count : -1].reshape(GROUP, mine, width), pair, axis=0).reshape(2 * mine, width)
    wbeta = jnp.pad(wbeta, ((0, DK - 2 * mine), (0, 0)))
    gain_h = gain_head.astype(F32)[None]

    hidden_mine = to_slices(across((w_gate, w_up)))
    if by_hand():
        mixer_w = spread_first(jnp.concatenate([mixer_mine, blocked(w_out)], axis=2))
        *mixer_w, xs[1], xs[2], xs[3], ends, gain_one, taps, wbeta = tie(*mixer_w, *xs[1:], ends, gain_one, taps, wbeta)
        mixer_w = all_four(*spread_last(*mixer_w))
        hidden_mine, w_down, *mixer_w = tie(hidden_mine, w_down, *mixer_w)
        down_w = spread_first(w_down[None])
        hidden_w = lax.all_gather(hidden_mine, ("c", "narrow"), axis=0).reshape((2, 4) + hidden_mine.shape)
    else:
        full = jnp.concatenate([spread_columns(mixer_mine), blocked(spread_rows(w_out))], axis=3)
        mixer_w = [full[:, n] for n in range(4)]
        full = spread_columns(hidden_mine).transpose(1, 0, 2, 3)
        other = lax.ppermute(full, "c", SWAP)
        hidden_w = jnp.stack([jnp.where(c_at == 0, full, other), jnp.where(c_at == 0, other, full)])
        full = spread_rows(w_down)[None]
        down_w = [full[:, n] for n in range(4)]
    mixer_w = with_partner(mixer_w)

    dy_low, mixer_w[1][3] = tie(dy_low, mixer_w[1][3])
    dys = gather_group(dy_low)
    half = length // 2
    row_spec = whole((length, width))
    sums = [(once(shape), shape, BF16) for shape in ((length, width), (2, half, width), (2, half, width), (half, width), (half, width))]
    kept = [((length, 2 * three), F32), ((length, DK), F32), ((2 * mine, length, length), F32), ((2 * mine, length, DK), F32), ((2 * mine, length, DK), F32)]
    constants = [whole((DK, width)), whole((count, 2 * three)), whole((1, DK))]
    mixer_held = [held_like(mixer_w[0][0]), held_like(mixer_w[0][0]), pltpu.SemaphoreType.DMA((2, 4))]
    shapes = [((length, width), BF16)] + kept + [((length, 2 * cols), BF16)]
    results = call(
        mixer_forward,
        "mixer_forward",
        4,
        [ends, where] + xs + [gain_one, wbeta, taps, gain_h] + mixer_w[0] + mixer_w[1],
        [scalars(), scalars()] + [row_spec] * 4 + [whole((1, width))] + constants + [anywhere()] * 8,
        sums + [(each(shape), (4,) + shape, kind) for shape, kind in shapes],
        mixer_held,
        60,
    )
    y_parts, act, saved, on = results[:5], results[5], results[6:-1], results[-1]

    x = x_low.astype(F32)
    *rest, dys[1], dys[2], dys[3] = tie(*y_parts, *down_w, *dys[1:])
    y_parts, down_w = rest[:5], rest[5:]
    y_sum = sum_last(*sum_second(*sum_first(y_parts)))
    h1 = x + y_sum
    r2 = lax.rsqrt(jnp.mean(h1 * h1, axis=-1, keepdims=True) + 1e-06)
    act2 = (h1 * r2 * gain_two).astype(BF16)
    act2s = gather_group(act2)
    if by_hand():
        act2s[1], *down_w = tie(act2s[1], *spread_last(*down_w))
        down_w = all_four(*down_w)
    down_w = with_partner(down_w)

    hidden = down_w[0][0].shape[1] * 4
    def row_pairs(n):
        return pl.BlockSpec((2 * length, n), lambda i: (i, 0))

    held_gu, held_down = [held_like(hidden_w[0, 0])] * 2, [held_like(down_w[0][0])] * 2
    results = call(
        hidden_units,
        "hidden_units",
        2,
        [where] + act2s + dys + [hidden_w] + down_w[0] + down_w[1],
        [scalars()] + [row_spec] * 8 + [anywhere()] * 9,
        [(row_pairs(n), (total, n), BF16) for n in (hidden, hidden, 2 * hidden, 2 * hidden)],
        held_gu + held_down + [pltpu.SemaphoreType.DMA((4, 4))],
        30,
    )
    hids, dgus = results[:2], results[2:]

    block = width // GROUP
    columns_spec = pl.BlockSpec((length, block), lambda i: (0, i))
    def gate_up_half(at, turn):
        return call(
            gate_up_grads,
            "gate_up_grads",
            GROUP // 2,
            [turn] + act2s + dgus,
            [scalars()] + [pl.BlockSpec((length, block), lambda i: (0, i + at))] * 4 + [whole(dgu.shape) for dgu in dgus],
            [(pl.BlockSpec((4, 2, 1, block // 4, 2 * hidden), lambda i: (0, 0, i, 0, 0)), (4, 2, GROUP // 2, block // 4, 2 * hidden), BF16)],
            [],
            10,
        )[0]

    grad_gu = [gate_up_half(0, where)]
    grad_gu[0], where = tie(grad_gu[0], where)
    grad_gu.append(gate_up_half(GROUP // 2, where))
    *dgus, grad_gu[0], grad_gu[1] = tie(*dgus, *grad_gu)
    dact2_parts = call(
        hidden_back,
        "hidden_back",
        2,
        [where] + dgus + [hidden_w],
        [scalars(), row_pairs(2 * hidden), row_pairs(2 * hidden), anywhere()],
        sums,
        held_gu + [pltpu.SemaphoreType.DMA((2, 4))],
        15,
    )
    sums2 = sum_first(dact2_parts)
    out_parts = call(
        hidden_out,
        "hidden_out",
        2,
        [where] + hids + down_w[0] + down_w[1],
        [scalars(), row_pairs(hidden), row_pairs(hidden)] + [anywhere()] * 8,
        sums,
        held_down + [pltpu.SemaphoreType.DMA((2, 4))],
        8,
    )
    sums2[0], sums2[1], *out_parts = tie(sums2[0], sums2[1], *out_parts)
    grad_second = sum_last(*sum_second(*sums2))
    scaled = grad_second * gain_two
    dh1 = dy_low.astype(F32) + r2 * scaled - h1 * (r2 * r2 * r2 * jnp.mean(h1 * scaled, axis=-1, keepdims=True))
    grad_gain_ffn = jnp.sum(grad_second * h1 * r2, axis=0)
    dy1 = dh1.astype(BF16)
    dy1s = gather_group(dy1)

    grad_down = call(
        down_grads,
        "down_grads",
        GROUP,
        [where] + hids + dys,
        [scalars()] + [whole(hid.shape) for hid in hids] + [columns_spec] * 4,
        [(pl.BlockSpec((4, 2, hidden // 4, block), lambda i: (0, 0, 0, i)), (4, 2, hidden // 4, width), BF16)],
        [],
        8,
    )[0]
    if by_hand():
        grad_gu = [lax.psum_scatter(part.reshape(-1, 2 * hidden), ("narrow", "c"), scatter_dimension=0, tiled=True) for part in grad_gu]
    *out_parts, grad_gu[0], grad_down, dy1s[1], dy1s[2], dy1s[3] = tie(*out_parts, grad_gu[0], grad_down, *dy1s[1:])
    if by_hand():
        grad_down = lax.psum_scatter(grad_down.reshape(-1, width), ("narrow", "c"), scatter_dimension=0, tiled=True)
    else:
        grad_gu = jnp.concatenate(grad_gu, axis=2)
        grad_gu = [lax.dynamic_index_in_dim(grad_gu, at, 1, keepdims=False) for at in (c_at, 1 - c_at)]
        grad_gu = to_owners(collect_columns(*grad_gu))
        grad_down = collect_rows(*[lax.dynamic_index_in_dim(grad_down, at, 1, keepdims=False) for at in (c_at, 1 - c_at)])

    shapes = [((length, 2 * three), BF16), ((length, DK), BF16)]
    results = call(
        mixer_backward,
        "mixer_backward",
        4,
        [ends, where] + dy1s + saved + [wbeta, taps, gain_h] + mixer_w[0] + mixer_w[1],
        [scalars(), scalars()] + [row_spec] * 4 + [each(shape) for shape, _ in kept] + constants + [anywhere()] * 8,
        sums
        + [(each(shape), (4,) + shape, kind) for shape, kind in shapes]
        + [(once((count, 2 * three)), (count, 2 * three), F32), (once((1, DK)), (1, DK), F32)],
        mixer_held,
        60,
    )
    out_sums = sum_first(out_parts)
    if by_hand():
        out_sums[0], out_sums[1], grad_gu[1], *results = tie(out_sums[0], out_sums[1], grad_gu[1], *results)
        grad_gu = to_owners(jnp.concatenate(grad_gu).reshape(GROUP, -1, 2 * hidden))
    dact_parts, (dqkv, dbl, dtaps, dgain) = results[:5], results[5:]
    grad_mixer, grad_wbeta = call(
        mixer_grads,
        "mixer_grads",
        GROUP,
        [where, act.reshape(total, width), dqkv.reshape(total, 2 * three), on.reshape(total, 2 * cols), dbl.reshape(total, DK)] + dy1s,
        [scalars(), pl.BlockSpec((total, block), lambda i: (0, i)), whole((total, 2 * three)), whole((total, 2 * cols)), whole((total, DK))] + [columns_spec] * 4,
        [(pl.BlockSpec((4, 2, 1, block // 4, three + block), lambda i: (0, 0, i, 0, 0)), (4, 2, GROUP, block // 4, three + block), BF16)]
        + [(pl.BlockSpec((DK, block), lambda i: (0, i)), (DK, width), F32)],
        [],
        15,
    )
    grad_act, grad_down = tie(sum_last(*sum_second(*sum_first(dact_parts))), grad_down)
    if by_hand():
        grad_mixer = lax.psum_scatter(grad_mixer.reshape(-1, three + block), ("narrow", "c"), scatter_dimension=0, tiled=True)
        grad_mixer = grad_mixer.reshape(GROUP, -1, three + block)
        grad_qkv, grad_out = grad_mixer[:, :, :three], grad_mixer[:, :, three:].transpose(1, 0, 2).reshape(-1, width).astype(F32)
    else:
        own, other = [lax.dynamic_index_in_dim(grad_mixer, at, 1, keepdims=False) for at in (c_at, 1 - c_at)]
        grad_qkv = collect_columns(own[..., :three], other[..., :three])
        grad_out = collect_rows(*[part[..., three:].transpose(0, 2, 1, 3).reshape(4, -1, width) for part in (own, other)])
    result = (h1 + sum_last(*sum_second(*out_sums))).astype(BF16)
    grad_qkv = to_owners(grad_qkv)

    r1 = lax.rsqrt(jnp.mean(x * x, axis=-1, keepdims=True) + 1e-06)
    scaled = grad_act * gain_one
    grad_input = (dh1 + r1 * scaled - x * (r1 * r1 * r1 * jnp.mean(x * scaled, axis=-1, keepdims=True))).astype(BF16)
    grad_gain_attn = jnp.sum(grad_act * x * r1, axis=0)

    at = (jnp.arange(GROUP)[:, None] == pair[None, :]).astype(F32)
    dtaps = dtaps.reshape(count, 2, 3, cols)
    dtaps = (at[:, 0, None, None, None] * dtaps[None, :, 0] + at[:, 1, None, None, None] * dtaps[None, :, 1]).transpose(2, 1, 0, 3)
    dbeta = grad_wbeta[: 2 * mine].reshape(2, mine, width)
    dbeta = at[:, 0, None, None] * dbeta[None, 0] + at[:, 1, None, None] * dbeta[None, 1]
    smalls = jnp.concatenate([grad_gain_attn[None], grad_gain_ffn[None], dtaps.reshape(3 * count, width), dbeta.reshape(heads, width)])
    smalls = smalls.reshape(smalls.shape[0], lax.axis_size(ALL), -1).transpose(1, 0, 2)
    dgain = jnp.broadcast_to(dgain.reshape(1, -1, smalls.shape[2]), (smalls.shape[0], DK // smalls.shape[2], smalls.shape[2]))
    smalls = sum_small(jnp.concatenate([smalls, dgain], axis=1))
    last_small = 2 + 3 * count + heads

    def columns(value, parts):
        outs = [(whole((value.shape[1], width_of)), (value.shape[1], width_of), F32) for width_of in [GROUP * value.shape[2] // parts] * parts]
        return call(in_order, "in_order", 1, [value], [whole(value.shape)], outs, [], 2)

    grad_query, grad_key, grad_value = columns(grad_qkv, 3)
    grad_gate, grad_up = columns(grad_gu, 2)
    return (
        result[None],
        grad_input[None],
        smalls[0],
        grad_query,
        grad_key,
        grad_value,
        smalls[2 + 3 * count : last_small].T,
        smalls[2 : 2 + count],
        smalls[2 + count : 2 + 2 * count],
        smalls[2 + 2 * count : 2 + 3 * count],
        smalls[last_small:].reshape(-1),
        grad_out,
        smalls[1],
        grad_gate,
        grad_up,
        grad_down.astype(F32),
    )


def solution(mesh):
    wide, narrow = mesh.shape["wide"], mesh.shape["narrow"]
    inner = Mesh(mesh.devices.reshape(wide // GROUP, 2, 2, 2, narrow), ALL)
    rows = P(ALL, None)
    columns = P(None, ALL)
    vector = P(ALL)
    cube = P(ALL, None, None)
    return jax.shard_map(
        local,
        mesh=inner,
        in_specs=(cube, rows, vector, rows, rows, rows, rows, columns, columns, columns, P(), rows, vector, rows, rows, rows, cube),
        out_specs=(cube, cube, vector, rows, rows, rows, rows, columns, columns, columns, P(), rows, vector, rows, rows, rows),
        check_vma=False,
    )
```

```python
from functools import partial

import jax
import jax.numpy as jnp
from jax import lax
from jax.experimental import pallas as pl
from jax.experimental.pallas import tpu as pltpu
from jax.sharding import Mesh
from jax.sharding import PartitionSpec as P

F32 = jnp.float32
BF16 = jnp.bfloat16
DK = 128
GROUP = 8
SLICES = ("y", "x", "c")
REST = ("far", "narrow")
ALL = ("far", "y", "x", "c", "narrow")
SWAP = [(0, 1), (1, 0)]
NEAR = [(0, 1), (1, 0), (2, 3), (3, 2)]
SKIP = [(0, 2), (2, 0), (1, 3), (3, 1)]
MIDDLE = [(1, 2), (2, 1)]
ACROSS = [(0, 3), (3, 0), (1, 2), (2, 1)]

NN = (((1,), (0,)), ((), ()))
NT = (((1,), (1,)), ((), ()))
TN = (((0,), (0,)), ((), ()))


def dot(left, right, dims=NN):
    return lax.dot_general(left, right, dims, preferred_element_type=F32)


def halves(value):
    high = value.astype(BF16)
    return high, (value - high.astype(F32)).astype(BF16)


def fine(left, right, dims=NN):
    left_high, left_low = halves(left)
    right_high, right_low = halves(right)
    return dot(left_high, right_high, dims) + (dot(left_high, right_low, dims) + dot(left_low, right_high, dims))


def semi(left, right, dims=NN):
    left_high, left_low = halves(left)
    return dot(left_high, right, dims) + dot(left_low, right, dims)


def plain(left, right, dims=NN):
    return dot(left.astype(BF16), right.astype(BF16), dims)


def documents(ends_ref, seq, shape, axis):
    place = lax.broadcasted_iota(jnp.int32, shape, axis)
    doc = jnp.zeros(shape, jnp.int32)
    first = jnp.zeros(shape, jnp.int32)
    for j in range(ends_ref.shape[1]):
        end = ends_ref[seq, j]
        past = place >= end
        doc = doc + past.astype(jnp.int32)
        first = jnp.where(past, end, first)
    return doc, place - first


def inverses(lowers, size):
    row = lax.broadcasted_iota(jnp.int32, (size, size), 0)
    col = lax.broadcasted_iota(jnp.int32, (size, size), 1)
    apart = row ^ col
    eye = (row == col).astype(F32)
    results = [eye - jnp.where(apart == 1, lower, 0.0) for lower in lowers]
    half = 2
    while half < size:
        pair = jnp.logical_and(apart >= half, apart < 2 * half)
        parts = [jnp.where(pair, lower, 0.0) for lower in lowers]
        middles = [fine(part, result) for part, result in zip(parts, results)]
        results = [result - fine(result, middle) for middle, result in zip(middles, results)]
        half *= 2
    return results


def conv(values, taps, keeps):
    total = values * taps[0]
    for j in range(1, len(taps)):
        total = total + jnp.where(keeps[j], pltpu.roll(values, j, 0), 0.0) * taps[j]
    return total


def pieces_of(refs, held, sems, where_ref):
    return [pltpu.make_async_copy(ref, held.at[:, where_ref[n]], sems.at[n]) for n, ref in enumerate(refs)]


def side_of(ref, side, held, sems):
    return [pltpu.make_async_copy(ref.at[side, n], held.at[:, n], sems.at[n]) for n in range(4)]


def start_all(groups):
    for copies in groups:
        for copy in copies:
            copy.start()


def wait_all(groups):
    for copies in groups:
        for copy in copies:
            copy.wait()


def at_first(action, groups):
    pl.when(pl.program_id(0) == 0)(lambda: action(groups))


def flat(value):
    return value.reshape(-1, value.shape[-1])


def chosen(*refs):
    value = refs[0][...]
    for n, ref in enumerate(refs[1:], 1):
        value = jnp.where(pl.program_id(0) == n, ref[...], value)
    return value


def hand_out(step, refs, value):
    own_ref, by_x_ref, by_y_ref, x_low_ref, y_top_ref = refs
    half = value.shape[0] // 2

    @pl.when(step == 0)
    def _():
        own_ref[...] = value

    @pl.when(step == 1)
    def _():
        by_x_ref[0] = value[:half]
        x_low_ref[...] = value[half:]

    @pl.when(step == 2)
    def _():
        y_top_ref[...] = value[:half]
        by_y_ref[0] = value[half:]

    @pl.when(step == 3)
    def _():
        by_x_ref[1] = value[:half]
        by_y_ref[1] = value[half:]


def masks(ends_ref, seq, rows, taps):
    _, pos = documents(ends_ref, seq, (rows, DK), 0)
    doc_r, _ = documents(ends_ref, seq, (rows, rows), 0)
    doc_c, _ = documents(ends_ref, seq, (rows, rows), 1)
    row = lax.broadcasted_iota(jnp.int32, (rows, rows), 0)
    col = lax.broadcasted_iota(jnp.int32, (rows, rows), 1)
    same = doc_r == doc_c
    return [pos >= j for j in range(taps)], jnp.logical_and(same, row > col), jnp.logical_and(same, row >= col)


def mixer_forward(ends_ref, where_ref, x0_ref, x1_ref, x2_ref, x3_ref, gain_one_ref, wbeta_ref, taps_ref, gain_ref, *rest):
    w_refs = rest[:4], rest[4:8]
    out_refs, rest = rest[8:13], rest[13:]
    act_ref, p_ref, bl_ref, t_ref, u_ref, o_ref, on0_ref, on1_ref, w0, w1, sems = rest
    held = (w0, w1)
    seq = pl.program_id(0)

    loads = [pieces_of(w_refs[side], held[side], sems.at[side], where_ref) for side in (0, 1)]
    at_first(start_all, loads)
    rows = x0_ref.shape[0]
    cols = on0_ref.shape[2]
    heads = cols // DK
    half = rows // 2
    count = taps_ref.shape[0]
    x = chosen(x0_ref, x1_ref, x2_ref, x3_ref).astype(F32)
    act = (x * lax.rsqrt(jnp.mean(x * x, axis=-1, keepdims=True) + 1e-06) * gain_one_ref[...]).astype(BF16)
    act_ref[0] = act
    projs = []
    for side in (0, 1):
        at_first(wait_all, loads[side : side + 1])
        proj = dot(act, flat(held[side][:, :, :, : 3 * cols]))
        p_ref[0, :, side * 3 * cols : (side + 1) * 3 * cols] = proj
        projs.append(proj)
    logit = dot(act, wbeta_ref[...], NT)
    bl_ref[0] = logit
    beta_all = jax.nn.sigmoid(logit)
    keeps, strict, causal = masks(ends_ref, seq, rows, count)
    gain = gain_ref[...]
    every = range(2 * heads)

    def part(kind, head):
        side, first = head // heads, kind * cols + (head % heads) * DK
        at = side * 3 * cols + first
        taps = [taps_ref[j : j + 1, at : at + DK] for j in range(count)]
        c = conv(projs[side][:, first : first + DK], taps, keeps)
        return c * jax.nn.sigmoid(c)

    def unit(u):
        return u * lax.rsqrt(jnp.sum(u * u, axis=-1, keepdims=True) + 1e-06)

    qs = [unit(part(0, head)).astype(BF16) for head in every]
    ks = [unit(part(1, head)).astype(BF16) for head in every]
    lowers = [jnp.where(strict, dot(ks[head], ks[head], NT), 0.0) * beta_all[:, head : head + 1] for head in every]
    blocks = inverses([block for lower in lowers for block in (lower[:half, :half], lower[half:, half:])], half)
    ons = []
    for head in every:
        v = part(2, head).astype(BF16)
        beta = beta_all[:, head : head + 1]
        top, low = blocks[2 * head], blocks[2 * head + 1]
        cross = -fine(low, fine(lowers[head][half:, :half], top))
        t_ref[0, head, :half, :half] = top
        t_ref[0, head, :half, half:] = jnp.zeros((half, half), F32)
        t_ref[0, head, half:, :half] = cross
        t_ref[0, head, half:, half:] = low
        target = v.astype(F32) * beta
        u_top = fine(top, target[:half])
        u_low = fine(cross, target[:half]) + fine(low, target[half:])
        u = jnp.concatenate([u_top, u_low], axis=0)
        u_ref[0, head] = u
        o = fine(jnp.where(causal, dot(qs[head], ks[head], NT), 0.0), u)
        o_ref[0, head] = o
        on = o * lax.rsqrt(jnp.mean(o * o, axis=-1, keepdims=True) + 1e-05) * gain
        ons.append(on.astype(BF16))
    on = jnp.concatenate(ons, axis=1)
    on0_ref[0] = on[:, :cols]
    on1_ref[0] = on[:, cols:]
    y = []
    for block in range(w0.shape[0]):
        parts = [dot(on[:, side * cols : (side + 1) * cols], flat(held[side][block, :, :, 3 * cols :])) for side in (0, 1)]
        y.append((parts[0] + parts[1]).astype(BF16))
    hand_out(seq, out_refs, jnp.concatenate(y, axis=1))


def mixer_backward(base, ends_ref, where_ref, dy0_ref, dy1_ref, x0_ref, x1_ref, p_ref, bl_ref, t_ref, u_ref, o_ref, wbeta_ref, taps_ref, gain_ref, *rest):
    w_refs = rest[:4], rest[4:8]
    refs = rest[8 : 11 + base // 2]
    rest = rest[8 + len(refs) :]
    dqkv0_ref, dqkv1_ref, dbl_ref, dtaps_ref, dgain_ref, dgain_one_ref, w0, w1, sems = rest
    held = (w0, w1)
    seq = pl.program_id(0)
    rows = dy0_ref.shape[0]
    cols = p_ref.shape[2] // 6
    heads = cols // DK
    count = taps_ref.shape[0]

    loads = [pieces_of(w_refs[side], held[side], sems.at[side], where_ref) for side in (0, 1)]
    at_first(start_all, loads)

    @pl.when(seq == 0)
    def _():
        dtaps_ref[...] = jnp.zeros_like(dtaps_ref)
        dgain_ref[...] = jnp.zeros_like(dgain_ref)
        dgain_one_ref[...] = jnp.zeros_like(dgain_one_ref)

    dy = chosen(dy0_ref, dy1_ref)
    dons = []
    for side in (0, 1):
        at_first(wait_all, loads[side : side + 1])
        don = 0.0
        for block in range(w0.shape[0]):
            weight = flat(held[side][block, :, :, 3 * cols :])
            don = don + dot(dy[:, block * weight.shape[1] : (block + 1) * weight.shape[1]], weight, NT)
        dons.append(don)
    beta_all = jax.nn.sigmoid(bl_ref[0])
    keeps, strict, causal = masks(ends_ref, base + seq, rows, count)
    gain = gain_ref[...]
    lane = lax.broadcasted_iota(jnp.int32, (rows, DK), 1)
    dbl_total = jnp.zeros((rows, DK), F32)

    def taps_of(first):
        return [taps_ref[j : j + 1, first : first + DK] for j in range(count)]

    def conv_back(first, dc):
        p = p_ref[0, :, first : first + DK]
        taps = taps_of(first)
        dp = dc * taps[0]
        dtaps_ref[0:1, first : first + DK] += jnp.sum(dc * p, axis=0, keepdims=True)
        for j in range(1, count):
            kept = jnp.where(keeps[j], dc, 0.0)
            dp = dp + pltpu.roll(kept, rows - j, 0) * taps[j]
            dtaps_ref[j : j + 1, first : first + DK] += jnp.sum(kept * pltpu.roll(p, j, 0), axis=0, keepdims=True)
        return dp

    def parts(first):
        c = conv(p_ref[0, :, first : first + DK], taps_of(first), keeps)
        sigma = jax.nn.sigmoid(c)
        return c * sigma, sigma * (1.0 + c * (1.0 - sigma))

    def unit_back(u, norm, grad):
        return norm * grad - u * (norm * norm * norm * jnp.sum(u * grad, axis=-1, keepdims=True))

    grads = [[None] * (3 * heads) for _ in (0, 1)]
    for head in range(2 * heads):
        side, at = head // heads, head % heads
        firsts = [side * 3 * cols + kind * cols + at * DK for kind in range(3)]
        uq, slope_q = parts(firsts[0])
        uk, slope_k = parts(firsts[1])
        uv, slope_v = parts(firsts[2])
        norm_q = lax.rsqrt(jnp.sum(uq * uq, axis=-1, keepdims=True) + 1e-06)
        norm_k = lax.rsqrt(jnp.sum(uk * uk, axis=-1, keepdims=True) + 1e-06)
        q = (uq * norm_q).astype(BF16)
        k = (uk * norm_k).astype(BF16)
        v = uv.astype(BF16).astype(F32)
        beta = beta_all[:, head : head + 1]
        o = o_ref[0, head]
        don = dons[side][:, at * DK : (at + 1) * DK]
        r = lax.rsqrt(jnp.mean(o * o, axis=-1, keepdims=True) + 1e-05)
        scaled = don * gain
        dgain_ref[...] += jnp.sum(don * o * r, axis=0, keepdims=True)
        do = r * scaled - o * (r * r * r * jnp.mean(o * scaled, axis=-1, keepdims=True))
        u = u_ref[0, head]
        inner = dot(k, k, NT)
        scores = jnp.where(causal, dot(q, k, NT), 0.0)
        du = fine(scores, do, TN)
        dscores = jnp.where(causal, fine(do, u, NT), 0.0)
        dq = semi(dscores, k)
        dk = semi(dscores, q, TN)
        w = fine(t_ref[0, head], du, TN)
        dv = beta * w
        dlower = jnp.where(strict, fine(w, u, NT), 0.0)
        dbeta = jnp.sum(w * v, axis=-1, keepdims=True) - jnp.sum(dlower * inner, axis=-1, keepdims=True)
        dinner = dlower * beta
        dk = dk - semi(dinner, k) - semi(dinner, k, TN)
        dbl_total = jnp.where(lane == head, dbeta * beta * (1.0 - beta), dbl_total)
        grads[side][at] = conv_back(firsts[0], unit_back(uq, norm_q, dq) * slope_q).astype(BF16)
        grads[side][heads + at] = conv_back(firsts[1], unit_back(uk, norm_k, dk) * slope_k).astype(BF16)
        grads[side][2 * heads + at] = conv_back(firsts[2], dv * slope_v).astype(BF16)
    dbl = dbl_total.astype(BF16)
    dbl_ref[0] = dbl
    dact = dot(dbl, wbeta_ref[...])
    for side in (0, 1):
        dqkv = jnp.concatenate(grads[side], axis=1)
        (dqkv0_ref, dqkv1_ref)[side][0] = dqkv
        dact = dact + dot(dqkv, flat(held[side][:, :, :, : 3 * cols]), NT)
    x = chosen(x0_ref, x1_ref).astype(F32)
    normed = x * lax.rsqrt(jnp.mean(x * x, axis=-1, keepdims=True) + 1e-06)
    dgain_one_ref[...] += jnp.sum(dact * normed, axis=0, keepdims=True)
    dact = dact.astype(BF16)
    half = rows // 2

    @pl.when(seq == 0)
    def _():
        if base == 0:
            refs[0][...] = dact
        else:
            refs[0][...] = dact[:half]
            refs[1][...] = dact[half:]

    @pl.when(seq == 1)
    def _():
        refs[-2][...] = dact[:half]
        refs[-1][...] = dact[half:]


def hidden_units(where_ref, *rest):
    acts, dys, wgu_ref, wd_refs = rest[:4], rest[4:8], rest[8], (rest[9:13], rest[13:17])
    hid_refs, dgu_refs, wgu, wd, sems = rest[17:19], rest[19:21], rest[21:23], rest[23:25], rest[25]
    core = where_ref[4]
    loads = []
    for side, at in enumerate((core, 1 - core)):
        loads.append(pieces_of(wd_refs[side], wd[side], sems.at[2 + side], where_ref))
        loads.append(side_of(wgu_ref, at, wgu[side], sems.at[side]))
    at_first(start_all, loads)
    hidden = hid_refs[0].shape[1]
    act = jnp.concatenate([chosen(acts[0], acts[2]), chosen(acts[1], acts[3])])
    dy = jnp.concatenate([chosen(dys[0], dys[2]), chosen(dys[1], dys[3])])
    for side in (0, 1):
        at_first(wait_all, loads[2 * side : 2 * side + 1])
        dhid = dot(dy, flat(wd[side][...]), NT)
        at_first(wait_all, loads[2 * side + 1 : 2 * side + 2])
        gu = dot(act, flat(wgu[side][...]))
        gt, up = gu[:, :hidden], gu[:, hidden:]
        sigma = jax.nn.sigmoid(gt)
        swish = gt * sigma
        hid_refs[side][...] = (swish * up).astype(BF16)
        dgt = (dhid * up * sigma * (1.0 + gt * (1.0 - sigma))).astype(BF16)
        dup = (dhid * swish).astype(BF16)
        dgu_refs[side][...] = jnp.concatenate([dgt, dup], axis=1)


def hidden_back(where_ref, dgu0_ref, dgu1_ref, wgu_ref, *rest):
    dact_refs, wgu, sems = rest[:5], rest[5:7], rest[7]
    step = pl.program_id(0)
    core = where_ref[4]
    loads = [side_of(wgu_ref, at, wgu[side], sems.at[side]) for side, at in enumerate((core, 1 - core))]
    at_first(start_all, loads)
    dact = 0.0
    for side, dgu_ref in enumerate((dgu0_ref, dgu1_ref)):
        at_first(wait_all, loads[side : side + 1])
        dact = dact + dot(dgu_ref[...], flat(wgu[side][...]), NT)
    rows = dact.shape[0] // 2
    for part in (0, 1):
        hand_out(2 * step + part, dact_refs, dact[part * rows : (part + 1) * rows].astype(BF16))


def hidden_out(where_ref, hid0_ref, hid1_ref, *rest):
    wd_refs, out_refs, wd, sems = (rest[:4], rest[4:8]), rest[8:13], rest[13:15], rest[15]
    step = pl.program_id(0)
    loads = [pieces_of(wd_refs[side], wd[side], sems.at[side], where_ref) for side in (0, 1)]
    at_first(start_all, loads)
    out = 0.0
    for side, hid_ref in enumerate((hid0_ref, hid1_ref)):
        at_first(wait_all, loads[side : side + 1])
        out = out + dot(hid_ref[...], flat(wd[side][...]))
    rows = out.shape[0] // 2
    for part in (0, 1):
        hand_out(2 * step + part, out_refs, out[part * rows : (part + 1) * rows].astype(BF16))


def gate_up_grads(where_ref, *rest):
    acts, dgus, out = rest[:4], (rest[4], rest[5]), rest[6]
    act = jnp.concatenate([ref[...] for ref in acts])
    rows = act.shape[1] // 4
    core = where_ref[4]
    for at, side in ((core, 0), (1 - core, 1)):
        value = dot(act, dgus[side][...], TN).astype(BF16)
        for n in range(4):
            out[n, at, 0] = value[n * rows : (n + 1) * rows]


def down_grads(where_ref, *rest):
    hids, dys, out = (rest[0], rest[1]), rest[2:6], rest[6]
    dy = jnp.concatenate([ref[...] for ref in dys])
    rows = hids[0].shape[1] // 4
    core = where_ref[4]
    for at, side in ((core, 0), (1 - core, 1)):
        value = dot(hids[side][...], dy, TN).astype(BF16)
        for n in range(4):
            out[n, at] = value[n * rows : (n + 1) * rows]


def mixer_grads(where_ref, act_ref, act2_ref, on_ref, on2_ref, dbl0_ref, dbl1_ref, *rest):
    dqkvs, dys, out_ref, beta_ref = rest[:4], rest[4:12], rest[12], rest[13]
    acts = act_ref[...], act2_ref[...]
    beta_ref[...] = dot(jnp.concatenate([dbl0_ref[...], dbl1_ref[...]]), acts[0], TN)
    tokens = dqkvs[0].shape[0]
    qkv = out = 0.0
    for core in (0, 1):
        for part in (0, 1):
            qkv = qkv + dot(acts[core][part * tokens : (part + 1) * tokens], dqkvs[2 * core + part][...], TN)
        dy = jnp.concatenate([ref[...] for ref in dys[4 * core : 4 * core + 4]])
        out = out + dot((on_ref, on2_ref)[core][...], dy, TN)
    value = jnp.concatenate([qkv, out], axis=1).astype(BF16)
    rows = value.shape[0] // 4
    for n in range(4):
        out_ref[n, 0] = value[n * rows : (n + 1) * rows]


def in_order(*refs):
    value, outs = refs[0], refs[1:]
    width = value.shape[2] // len(outs)
    for n, out in enumerate(outs):
        parts = [value[block, :, n * width : (n + 1) * width].astype(F32) for block in range(value.shape[0])]
        out[...] = jnp.concatenate(parts, axis=1)


def whole(shape):
    return pl.BlockSpec(shape, lambda i: (0,) * len(shape), pipeline_mode=pl.Buffered(1))


def each(shape):
    return pl.BlockSpec((1,) + shape, lambda i: (i,) + (0,) * len(shape))


PARAMS = pltpu.CompilerParams(vmem_limit_bytes=60 * 1024 * 1024, dimension_semantics=("arbitrary",))


def tie(*values):
    return lax.optimization_barrier(values)


def gather_group(own):
    return [own, lax.ppermute(own, "x", SWAP), lax.ppermute(own, "y", SWAP), lax.ppermute(own, ("y", "x"), ACROSS)]


def joined(left, right):
    return left.astype(F32) + right.astype(F32)


def sum_first(parts):
    own, by_x, by_y, x_low, y_top = parts
    return [lax.ppermute(by_x, "x", SWAP), lax.ppermute(by_y, "y", SWAP), own, x_low, y_top]


def sum_second(got_x, got_y, own, x_low, y_top):
    y_top = lax.ppermute(joined(y_top, got_x[1]).astype(BF16), "y", SWAP)
    x_low = lax.ppermute(joined(x_low, got_y[1]).astype(BF16), "x", SWAP)
    return [x_low, y_top, own, got_x, got_y]


def sum_last(x_low, y_top, own, got_x, got_y):
    half = x_low.shape[0]
    top = joined(own[:half], got_x[0]) + y_top.astype(F32)
    low = joined(own[half:], got_y[0]) + x_low.astype(F32)
    return jnp.concatenate([top, low])


def by_hand():
    return lax.axis_size("far") == 1 and lax.axis_size("narrow") == 4


def with_partner(pieces):
    return pieces, [lax.ppermute(piece, "c", SWAP) for piece in pieces]


def spread_first(mine):
    return [mine, lax.ppermute(mine, "narrow", NEAR), lax.ppermute(mine, "narrow", SKIP)]


def spread_last(mine, near, skip):
    return [mine, near, skip, lax.ppermute(mine, "narrow", MIDDLE), lax.ppermute(skip, "narrow", [(2, 3), (1, 0)])]


def all_four(mine, near, skip, middle, end):
    z = lax.axis_index("narrow")
    return [mine, near, skip, jnp.where((z == 1) | (z == 2), middle, end)]


def spread_columns(mine):
    far, narrow = lax.axis_size("far"), lax.axis_size("narrow")
    _, rows, columns = mine.shape
    full = lax.all_gather(mine, REST, axis=0).reshape(far, narrow, GROUP, rows, columns).transpose(0, 2, 1, 3, 4)
    return full.reshape(GROUP, 4, -1, columns)


def spread_rows(weight):
    full = lax.all_gather(weight, ALL, axis=0, tiled=True)
    total = full.shape[0] // GROUP
    return lax.dynamic_slice_in_dim(full, lax.axis_index(SLICES) * total, total, 0).reshape(4, -1, full.shape[1])


def collect_columns(full):
    columns = full.shape[-1]
    far, narrow = lax.axis_size("far"), lax.axis_size("narrow")
    full = full.transpose(1, 0, 2, 3).reshape(far, GROUP, narrow, -1, columns).transpose(0, 2, 1, 3, 4)
    full = lax.psum_scatter(full.reshape(-1, columns), REST, scatter_dimension=0, tiled=True)
    return full.reshape(GROUP, -1, columns).astype(F32)


def collect_rows(full):
    full = full.reshape(1, -1, full.shape[-1])
    full = jnp.where((jnp.arange(GROUP) == lax.axis_index(SLICES))[:, None, None], full, 0)
    return lax.psum_scatter(full.reshape(-1, full.shape[-1]), ALL, scatter_dimension=0, tiled=True).astype(F32)


def to_owners(mine):
    return lax.all_to_all(mine.astype(BF16), SLICES, 0, 0, tiled=True)


def gather_small(values, late):
    if not by_hand():
        shape = tuple(lax.axis_size(axis) for axis in ALL)
        return lax.all_gather(values, ALL, axis=0).reshape(shape + values.shape), late
    values = jnp.stack([values] + [lax.ppermute(values, "narrow", pairs) for pairs in (NEAR, SKIP, ACROSS)])
    values = jnp.stack([values, lax.ppermute(values, "c", SWAP)])
    values, late = tie(values, late)
    values = jnp.stack(gather_group(values))
    here = lax.axis_index(SLICES) * 4 + lax.axis_index("narrow")
    values = jnp.take(values.reshape((-1,) + values.shape[3:]), jnp.arange(32) ^ here, axis=0)
    return values.reshape((1, 2, 2, 2, 4) + values.shape[1:]), late


def sum_small(values, *others):
    if not by_hand():
        return lax.psum_scatter(values, ALL, scatter_dimension=0, tiled=False), *others
    later = list(others)
    z = lax.axis_index("narrow")
    values = values.reshape((2, 2, 2, 2, 2) + values.shape[1:])
    bits = [("c", SWAP, lax.axis_index("c"), 2), ("x", SWAP, lax.axis_index("x"), 1), ("y", SWAP, lax.axis_index("y"), 0), ("narrow", NEAR, z % 2, 1), ("narrow", SKIP, z // 2, 0)]
    for axis, pairs, bit, dim in bits:
        keep = lax.dynamic_index_in_dim(values, bit, dim, keepdims=False)
        send = lax.dynamic_index_in_dim(values, 1 - bit, dim, keepdims=False)
        values = keep + lax.ppermute(send, axis, pairs)
        if axis == "x":
            values, later[0], later[1] = tie(values, later[0], later[1])
        if axis == "y":
            values, *later = tie(values, *later)
    return values, *later


def anywhere():
    return pl.BlockSpec(memory_space=pl.ANY)


def scalars():
    return pl.BlockSpec(memory_space=pltpu.SMEM)


def once(shape):
    return pl.BlockSpec(shape, lambda i: (0,) * len(shape), pipeline_mode=pl.Buffered(1))


def held_like(piece):
    return pltpu.VMEM((piece.shape[0], 4) + piece.shape[1:], BF16)


def call(kernel, name, grid, inputs, in_specs, outs, scratch, microseconds):
    results = pl.pallas_call(
        kernel,
        grid=(grid,),
        in_specs=in_specs,
        out_specs=[spec for spec, _, _ in outs],
        out_shape=[jax.ShapeDtypeStruct(shape, kind) for _, shape, kind in outs],
        scratch_shapes=scratch,
        compiler_params=PARAMS,
        cost_estimate=pl.CostEstimate(flops=int(microseconds * 1e9), bytes_accessed=20_000_000, transcendentals=0),
        name=name,
    )(*inputs)
    return list(results)


def local(tokens, doc_lengths, gain_attn, w_query, w_key, w_value, w_beta, conv_query, conv_key, conv_value, gain_head, w_out, gain_ffn, w_gate, w_up, w_down, cotangent):
    x_low = tokens[0]
    dy_low = cotangent[0]
    length, width = x_low.shape
    heads = w_beta.shape[1]
    mine = heads // GROUP
    cols = mine * DK
    three = 3 * cols
    count = conv_query.shape[0]
    total = 4 * length
    y_at, x_at, c_at, z_at = [lax.axis_index(axis) for axis in ("y", "x", "c", "narrow")]
    me = lax.axis_index(SLICES)
    where = jnp.stack([z_at, z_at ^ 1, z_at ^ 2, z_at ^ 3] if by_hand() else [0, 1, 2, 3])
    chips = [(y_at ^ dy) * 2 + (x_at ^ dx) for dy in (0, 1) for dx in (0, 1)]
    where = jnp.append(where, c_at)

    def across(weights):
        rows = weights[0].shape[0]
        return jnp.concatenate([w.reshape(rows, GROUP, -1) for w in weights], axis=2).transpose(1, 0, 2)

    def to_slices(parts):
        return lax.all_to_all(parts, SLICES, 0, 0, tiled=True)

    def blocked(weight):
        return jnp.moveaxis(weight.reshape(weight.shape[:-1] + (GROUP, -1)), -2, 0)

    mixer_parts, gain_attn, gain_ffn, conv_query, conv_key, conv_value, w_beta, doc_lengths = tie(
        across((w_query, w_key, w_value)), gain_attn, gain_ffn, conv_query, conv_key, conv_value, w_beta, doc_lengths
    )
    lengths = jnp.pad(doc_lengths.astype(BF16), ((0, 0), (0, gain_attn.shape[0] - doc_lengths.shape[1])))
    small = jnp.concatenate([gain_attn[None], gain_ffn[None], conv_query, conv_key, conv_value, w_beta.T, lengths])
    mixer_mine = to_slices(mixer_parts)
    small, mixer_mine = gather_small(small, mixer_mine)
    x_low, small = tie(x_low, small)
    xs = gather_group(x_low)
    lengths = small[..., -1, : doc_lengths.shape[1]].astype(jnp.int32)
    lengths = lax.dynamic_index_in_dim(lengths, lax.axis_index("far"), 0, keepdims=False)
    lengths = lax.dynamic_index_in_dim(lengths, c_at, 2, keepdims=False)
    lengths = lax.dynamic_index_in_dim(lengths, z_at, 2, keepdims=False).reshape(4, -1)
    ends = jnp.cumsum(jnp.take(lengths, jnp.stack(chips), axis=0), axis=1)[:, :-1]
    wide = small.reshape((-1,) + small.shape[-2:]).transpose(1, 0, 2).reshape(small.shape[-2], width)
    gain_one = wide[0:1].astype(F32)
    gain_two = wide[1:2].astype(F32)
    pair = jnp.stack([me, me ^ 1])
    taps = jnp.take(wide[2 : 2 + 3 * count].reshape(3, count, GROUP, cols), pair, axis=2)
    taps = taps.transpose(1, 2, 0, 3).reshape(count, 2 * three).astype(F32)
    wbeta = jnp.take(wide[2 + 3 * count : -1].reshape(GROUP, mine, width), pair, axis=0).reshape(2 * mine, width)
    wbeta = jnp.pad(wbeta, ((0, DK - 2 * mine), (0, 0)))
    gain_h = gain_head.astype(F32)[None]

    hidden_mine = to_slices(across((w_gate, w_up)))
    if by_hand():
        mixer_w = spread_first(jnp.concatenate([mixer_mine, blocked(w_out)], axis=2))
        *mixer_w, xs[1], xs[2], xs[3], ends, gain_one, taps, wbeta = tie(*mixer_w, *xs[1:], ends, gain_one, taps, wbeta)
        mixer_w = all_four(*spread_last(*mixer_w))
        hidden_mine, w_down, *mixer_w = tie(hidden_mine, w_down, *mixer_w)
        down_w = spread_first(w_down[None])
        hidden_w = lax.all_gather(hidden_mine, ("c", "narrow"), axis=0).reshape((2, 4) + hidden_mine.shape)
    else:
        full = jnp.concatenate([spread_columns(mixer_mine), blocked(spread_rows(w_out))], axis=3)
        mixer_w = [full[:, n] for n in range(4)]
        full = spread_columns(hidden_mine).transpose(1, 0, 2, 3)
        other = lax.ppermute(full, "c", SWAP)
        hidden_w = jnp.stack([jnp.where(c_at == 0, full, other), jnp.where(c_at == 0, other, full)])
        full = spread_rows(w_down)[None]
        down_w = [full[:, n] for n in range(4)]
    mixer_w = with_partner(mixer_w)

    dy_low, mixer_w[1][3] = tie(dy_low, mixer_w[1][3])
    dys = gather_group(dy_low)
    half = length // 2
    row_spec = whole((length, width))
    sums = [(once(shape), shape, BF16) for shape in ((length, width), (2, half, width), (2, half, width), (half, width), (half, width))]
    kept = [((length, 2 * three), F32), ((length, DK), F32), ((2 * mine, length, length), F32), ((2 * mine, length, DK), F32), ((2 * mine, length, DK), F32)]
    constants = [whole((DK, width)), whole((count, 2 * three)), whole((1, DK))]
    mixer_held = [held_like(mixer_w[0][0]), held_like(mixer_w[0][0]), pltpu.SemaphoreType.DMA((2, 4))]
    shapes = [((length, width), BF16)] + kept + [((length, cols), BF16)] * 2
    results = call(
        mixer_forward,
        "mixer_forward",
        4,
        [ends, where] + xs + [gain_one, wbeta, taps, gain_h] + mixer_w[0] + mixer_w[1],
        [scalars(), scalars()] + [row_spec] * 4 + [whole((1, width))] + constants + [anywhere()] * 8,
        sums + [(each(shape), (4,) + shape, kind) for shape, kind in shapes],
        mixer_held,
        60,
    )
    y_parts, act, saved, ons = results[:5], results[5], results[6:-2], results[-2:]

    x = x_low.astype(F32)
    *rest, dys[1], dys[2], dys[3] = tie(*y_parts, *down_w, *dys[1:])
    y_parts, down_w = rest[:5], rest[5:]
    y_sum = sum_last(*sum_second(*sum_first(y_parts)))
    h1 = x + y_sum
    r2 = lax.rsqrt(jnp.mean(h1 * h1, axis=-1, keepdims=True) + 1e-06)
    act2 = (h1 * r2 * gain_two).astype(BF16)
    act2s = gather_group(act2)
    if by_hand():
        act2s[1], *down_w = tie(act2s[1], *spread_last(*down_w))
        down_w = all_four(*down_w)
    down_w = with_partner(down_w)

    hidden = down_w[0][0].shape[1] * 4
    def row_pairs(n):
        return pl.BlockSpec((2 * length, n), lambda i: (i, 0))

    held_gu, held_down = [held_like(hidden_w[0, 0])] * 2, [held_like(down_w[0][0])] * 2
    results = call(
        hidden_units,
        "hidden_units",
        2,
        [where] + act2s + dys + [hidden_w] + down_w[0] + down_w[1],
        [scalars()] + [row_spec] * 8 + [anywhere()] * 9,
        [(row_pairs(n), (total, n), BF16) for n in (hidden, hidden, 2 * hidden, 2 * hidden)],
        held_gu + held_down + [pltpu.SemaphoreType.DMA((4, 4))],
        30,
    )
    hids, dgus = results[:2], results[2:]

    block = width // GROUP
    columns_spec = pl.BlockSpec((length, block), lambda i: (0, i))
    def gate_up_half(at, turn):
        return call(
            gate_up_grads,
            "gate_up_grads",
            GROUP // 2,
            [turn] + act2s + dgus,
            [scalars()] + [pl.BlockSpec((length, block), lambda i: (0, i + at))] * 4 + [whole(dgu.shape) for dgu in dgus],
            [(pl.BlockSpec((4, 2, 1, block // 4, 2 * hidden), lambda i: (0, 0, i, 0, 0)), (4, 2, GROUP // 2, block // 4, 2 * hidden), BF16)],
            [],
            10,
        )[0]

    grad_gu = [gate_up_half(0, where)]
    *dgus, grad_gu[0] = tie(*dgus, grad_gu[0])
    dact2_parts = call(
        hidden_back,
        "hidden_back",
        2,
        [where] + dgus + [hidden_w],
        [scalars(), row_pairs(2 * hidden), row_pairs(2 * hidden), anywhere()],
        sums,
        held_gu + [pltpu.SemaphoreType.DMA((2, 4))],
        15,
    )
    sums2 = sum_first(dact2_parts)
    where, dact2_parts[0] = tie(where, dact2_parts[0])
    grad_gu.append(gate_up_half(GROUP // 2, where))
    sums2[0], sums2[1], grad_gu[1], where = tie(sums2[0], sums2[1], grad_gu[1], where)
    def down_part(at, blocks):
        spec = pl.BlockSpec((length, block), lambda i: (0, i + at))
        return call(
            down_grads,
            "down_grads",
            blocks,
            [where] + hids + dys,
            [scalars()] + [whole(hid.shape) for hid in hids] + [spec] * 4,
            [(pl.BlockSpec((4, 2, hidden // 4, block), lambda i: (0, 0, 0, i)), (4, 2, hidden // 4, blocks * block), BF16)],
            [],
            5,
        )[0]

    grad_second = sum_last(*sum_second(*sums2))
    scaled = grad_second * gain_two
    dh1 = dy_low.astype(F32) + r2 * scaled - h1 * (r2 * r2 * r2 * jnp.mean(h1 * scaled, axis=-1, keepdims=True))
    grad_gain_ffn = jnp.sum(grad_second * h1 * r2, axis=0)
    dy1 = dh1.astype(BF16)
    *dy1s, dy1_partner = tie(dy1, lax.ppermute(dy1, "x", SWAP), lax.ppermute(dy1, "y", SWAP), lax.ppermute(dy1, "c", SWAP))
    dy1s.append(lax.ppermute(dy1s[0], ("y", "x"), ACROSS))

    out_parts = call(
        hidden_out,
        "hidden_out",
        2,
        [where] + hids + down_w[0] + down_w[1],
        [scalars(), row_pairs(hidden), row_pairs(hidden)] + [anywhere()] * 8,
        sums,
        held_down + [pltpu.SemaphoreType.DMA((2, 4))],
        8,
    )
    where, out_parts[0] = tie(where, out_parts[0])
    grad_down = down_part(0, GROUP)
    if by_hand():
        grad_gu = [lax.psum_scatter(part.reshape(-1, 2 * hidden), ("narrow", "c"), scatter_dimension=0, tiled=True) for part in grad_gu]
    dy1s[0], dy1s[1], dy1s[2], grad_gu[0], grad_down = tie(*dy1s[:3], grad_gu[0], grad_down)
    if by_hand():
        grad_down = lax.psum_scatter(grad_down.reshape(-1, width), ("narrow", "c"), scatter_dimension=0, tiled=True)
    else:
        grad_gu = jnp.concatenate(grad_gu, axis=2)
        grad_gu = [lax.dynamic_index_in_dim(grad_gu, at, 1, keepdims=False) for at in (c_at, 1 - c_at)]
        grad_gu = joined(grad_gu[0], lax.ppermute(grad_gu[1], "c", SWAP)).astype(BF16)
        grad_gu = to_owners(collect_columns(grad_gu))

    def mixer_half(base, dys, xs, turn):
        def part(shape):
            return pl.BlockSpec((1,) + shape, lambda i: (i + base,) + (0,) * len(shape))

        whole_piece = [(once((length, width)), (length, width), BF16)]
        half_piece = [(once((half, width)), (half, width), BF16)]
        shapes = [((length, three), BF16)] * 2 + [((length, DK), BF16)]
        return call(
            partial(mixer_backward, base),
            "mixer_backward",
            2,
            [ends, turn] + dys + xs + saved + [wbeta, taps, gain_h] + mixer_w[0] + mixer_w[1],
            [scalars(), scalars()] + [row_spec] * 4 + [part(shape) for shape, _ in kept] + constants + [anywhere()] * 8,
            (half_piece * 4 if base else whole_piece + half_piece * 2)
            + [(each(shape), (2,) + shape, kind) for shape, kind in shapes]
            + [(once(shape), shape, F32) for shape in ((count, 2 * three), (1, DK), (1, width))],
            mixer_held,
            30,
        )

    act_partner, on_partner = [lax.ppermute(value, "c", SWAP) for value in (act, ons[1])]
    own, x_top, x_low, *first_half = mixer_half(0, dy1s[:2], xs[:2], where)
    partners = [dy1_partner] + [lax.ppermute(piece, "c", SWAP) for piece in dy1s[1:3]]
    *out_parts, partners[1], partners[2], act_partner, on_partner, dy1s[3], own, where = tie(
        *out_parts, *partners[1:], act_partner, on_partner, dy1s[3], own, where
    )
    partners.append(lax.ppermute(dy1s[3], "c", SWAP))
    dqkv_partner = [lax.ppermute(first_half[1], "c", SWAP)]
    y_top, y_low, far_top, far_low, *second_half = mixer_half(2, dy1s[2:], xs[2:], where)
    out_sums = sum_first(out_parts)
    if by_hand():
        rest = tie(out_sums[0], out_sums[1], grad_gu[1], far_top, partners[3], dqkv_partner[0], *second_half)
        out_sums[0], out_sums[1], grad_gu[1], far_top, partners[3], dqkv_partner[0], *second_half = rest
    dqkv_partner.append(lax.ppermute(second_half[1], "c", SWAP))
    far_top, far_low = lax.ppermute(far_top, "x", SWAP), lax.ppermute(far_low, "y", SWAP)
    dqkvs = [part.reshape(total // 2, three) for part in (first_half[0], second_half[0], *dqkv_partner)]
    dbls = [part[2].reshape(total // 2, DK) for part in (first_half, second_half)]
    dtaps, dgain, dgain_one = [first + second for first, second in zip(first_half[3:], second_half[3:])]
    grad_mixer, grad_wbeta = call(
        mixer_grads,
        "mixer_grads",
        GROUP,
        [where, act.reshape(total, width), act_partner.reshape(total, width)]
        + [ons[0].reshape(total, cols), on_partner.reshape(total, cols)]
        + dbls
        + dqkvs
        + dy1s
        + partners,
        [scalars()]
        + [pl.BlockSpec((total, block), lambda i: (0, i))] * 2
        + [whole((total, cols))] * 2
        + [whole((total // 2, DK))] * 2
        + [whole((total // 2, three))] * 4
        + [columns_spec] * 8,
        [(pl.BlockSpec((4, 1, block // 4, three + block), lambda i: (0, i, 0, 0)), (4, GROUP, block // 4, three + block), BF16)]
        + [(pl.BlockSpec((DK, block), lambda i: (0, i)), (DK, width), F32)],
        [],
        15,
    )
    if by_hand():
        grad_gu = to_owners(jnp.concatenate(grad_gu).reshape(GROUP, -1, 2 * hidden))
    far_top, far_low, x_top, y_low = tie(far_top, far_low, x_top, y_low)
    x_top, y_low, x_low, y_top = tie(lax.ppermute(x_top, "x", SWAP), lax.ppermute(y_low, "y", SWAP), x_low, y_top)
    total_out = sum_last(*sum_second(*out_sums))
    grad_act = sum_last(*sum_second([x_top, far_top], [y_low, far_low], own, x_low, y_top))
    if by_hand():
        grad_mixer = lax.psum_scatter(grad_mixer.reshape(-1, three + block), "narrow", scatter_dimension=0, tiled=True)
        grad_mixer = grad_mixer.reshape(GROUP, -1, three + block)
        grad_qkv, grad_out = grad_mixer[:, :, :three], grad_mixer[:, :, three:].transpose(1, 0, 2).reshape(-1, width).astype(F32)
    else:
        grad_qkv = collect_columns(grad_mixer[..., :three])
        grad_out = collect_rows(grad_mixer[..., three:].transpose(0, 2, 1, 3).reshape(4, -1, width))
        own, other = [lax.dynamic_index_in_dim(grad_down, at, 1, keepdims=False) for at in (c_at, 1 - c_at)]
        grad_down = collect_rows(joined(own, lax.ppermute(other, "c", SWAP)).astype(BF16))
    at = (jnp.arange(GROUP)[:, None] == pair[None, :]).astype(F32)
    dtaps = dtaps.reshape(count, 2, 3, cols)
    dtaps = (at[:, 0, None, None, None] * dtaps[None, :, 0] + at[:, 1, None, None, None] * dtaps[None, :, 1]).transpose(2, 1, 0, 3)
    dbeta = grad_wbeta[: 2 * mine].reshape(2, mine, width)
    dbeta = at[:, 0, None, None] * dbeta[None, 0] + at[:, 1, None, None] * dbeta[None, 1]
    smalls = jnp.concatenate([dgain_one, grad_gain_ffn[None], dtaps.reshape(3 * count, width), dbeta.reshape(heads, width)])
    smalls = smalls.reshape(smalls.shape[0], lax.axis_size(ALL), -1).transpose(1, 0, 2)
    dgain = jnp.broadcast_to(dgain.reshape(1, -1, smalls.shape[2]), (smalls.shape[0], DK // smalls.shape[2], smalls.shape[2]))
    smalls, grad_gu, grad_down, grad_act, total_out, grad_qkv = sum_small(
        jnp.concatenate([smalls, dgain], axis=1), grad_gu, grad_down, grad_act, total_out, grad_qkv
    )
    grad_qkv = to_owners(grad_qkv)
    r1 = lax.rsqrt(jnp.mean(x * x, axis=-1, keepdims=True) + 1e-06)
    scaled = grad_act * gain_one
    grad_input = (dh1 + r1 * scaled - x * (r1 * r1 * r1 * jnp.mean(x * scaled, axis=-1, keepdims=True))).astype(BF16)
    result = (h1 + total_out).astype(BF16)
    last_small = 2 + 3 * count + heads

    def columns(value, parts):
        outs = [(whole((value.shape[1], width_of)), (value.shape[1], width_of), F32) for width_of in [GROUP * value.shape[2] // parts] * parts]
        return call(in_order, "in_order", 1, [value], [whole(value.shape)], outs, [], 2)

    grad_query, grad_key, grad_value = columns(grad_qkv, 3)
    grad_gate, grad_up = columns(grad_gu, 2)
    return (
        result[None],
        grad_input[None],
        smalls[0],
        grad_query,
        grad_key,
        grad_value,
        smalls[2 + 3 * count : last_small].T,
        smalls[2 : 2 + count],
        smalls[2 + count : 2 + 2 * count],
        smalls[2 + 2 * count : 2 + 3 * count],
        smalls[last_small:].reshape(-1),
        grad_out,
        smalls[1],
        grad_gate,
        grad_up,
        grad_down.astype(F32),
    )


def solution(mesh):
    wide, narrow = mesh.shape["wide"], mesh.shape["narrow"]
    inner = Mesh(mesh.devices.reshape(wide // GROUP, 2, 2, 2, narrow), ALL)
    rows = P(ALL, None)
    columns = P(None, ALL)
    vector = P(ALL)
    cube = P(ALL, None, None)
    return jax.shard_map(
        local,
        mesh=inner,
        in_specs=(cube, rows, vector, rows, rows, rows, rows, columns, columns, columns, P(), rows, vector, rows, rows, rows, cube),
        out_specs=(cube, cube, vector, rows, rows, rows, rows, columns, columns, columns, P(), rows, vector, rows, rows, rows),
        check_vma=False,
    )
```

```python
from functools import partial

import jax
import jax.numpy as jnp
from jax import lax
from jax.experimental import pallas as pl
from jax.experimental.pallas import tpu as pltpu
from jax.sharding import Mesh
from jax.sharding import PartitionSpec as P

F32 = jnp.float32
BF16 = jnp.bfloat16
DK = 128
GROUP = 8
SLICES = ("y", "x", "c")
REST = ("far", "narrow")
ALL = ("far", "y", "x", "c", "narrow")
SWAP = [(0, 1), (1, 0)]
NEAR = [(0, 1), (1, 0), (2, 3), (3, 2)]
SKIP = [(0, 2), (2, 0), (1, 3), (3, 1)]
MIDDLE = [(1, 2), (2, 1)]
ACROSS = [(0, 3), (3, 0), (1, 2), (2, 1)]

NN = (((1,), (0,)), ((), ()))
NT = (((1,), (1,)), ((), ()))
TN = (((0,), (0,)), ((), ()))


def dot(left, right, dims=NN):
    return lax.dot_general(left, right, dims, preferred_element_type=F32)


def halves(value):
    high = value.astype(BF16)
    return high, (value - high.astype(F32)).astype(BF16)


def fine(left, right, dims=NN):
    left_high, left_low = halves(left)
    right_high, right_low = halves(right)
    return dot(left_high, right_high, dims) + (dot(left_high, right_low, dims) + dot(left_low, right_high, dims))


def semi(left, right, dims=NN):
    left_high, left_low = halves(left)
    return dot(left_high, right, dims) + dot(left_low, right, dims)


def plain(left, right, dims=NN):
    return dot(left.astype(BF16), right.astype(BF16), dims)


def documents(ends_ref, seq, shape, axis):
    place = lax.broadcasted_iota(jnp.int32, shape, axis)
    doc = jnp.zeros(shape, jnp.int32)
    first = jnp.zeros(shape, jnp.int32)
    for j in range(ends_ref.shape[1]):
        end = ends_ref[seq, j]
        past = place >= end
        doc = doc + past.astype(jnp.int32)
        first = jnp.where(past, end, first)
    return doc, place - first


def inverses(lowers, size):
    row = lax.broadcasted_iota(jnp.int32, (size, size), 0)
    col = lax.broadcasted_iota(jnp.int32, (size, size), 1)
    apart = row ^ col
    eye = (row == col).astype(F32)
    results = [eye - jnp.where(apart == 1, lower, 0.0) for lower in lowers]
    half = 2
    while half < size:
        pair = jnp.logical_and(apart >= half, apart < 2 * half)
        parts = [jnp.where(pair, lower, 0.0) for lower in lowers]
        middles = [fine(part, result) for part, result in zip(parts, results)]
        results = [result - fine(result, middle) for middle, result in zip(middles, results)]
        half *= 2
    return results


def conv(values, taps, keeps):
    total = values * taps[0]
    for j in range(1, len(taps)):
        total = total + jnp.where(keeps[j], pltpu.roll(values, j, 0), 0.0) * taps[j]
    return total


def pieces_of(refs, held, sems, where_ref):
    return [pltpu.make_async_copy(ref, held.at[:, where_ref[n]], sems.at[n]) for n, ref in enumerate(refs)]


def side_of(ref, side, held, sems):
    return [pltpu.make_async_copy(ref.at[side, n], held.at[:, n], sems.at[n]) for n in range(4)]


def start_all(groups):
    for copies in groups:
        for copy in copies:
            copy.start()


def wait_all(groups):
    for copies in groups:
        for copy in copies:
            copy.wait()


def at_first(action, groups):
    pl.when(pl.program_id(0) == 0)(lambda: action(groups))


def flat(value):
    return value.reshape(-1, value.shape[-1])


def chosen(*refs):
    value = refs[0][...]
    for n, ref in enumerate(refs[1:], 1):
        value = jnp.where(pl.program_id(0) == n, ref[...], value)
    return value


def hand_out(step, refs, value):
    own_ref, by_x_ref, by_y_ref, x_low_ref, y_top_ref = refs
    half = value.shape[0] // 2

    @pl.when(step == 0)
    def _():
        own_ref[...] = value

    @pl.when(step == 1)
    def _():
        by_x_ref[0] = value[:half]
        x_low_ref[...] = value[half:]

    @pl.when(step == 2)
    def _():
        y_top_ref[...] = value[:half]
        by_y_ref[0] = value[half:]

    @pl.when(step == 3)
    def _():
        by_x_ref[1] = value[:half]
        by_y_ref[1] = value[half:]


def masks(ends_ref, seq, rows, taps):
    _, pos = documents(ends_ref, seq, (rows, DK), 0)
    doc_r, _ = documents(ends_ref, seq, (rows, rows), 0)
    doc_c, _ = documents(ends_ref, seq, (rows, rows), 1)
    row = lax.broadcasted_iota(jnp.int32, (rows, rows), 0)
    col = lax.broadcasted_iota(jnp.int32, (rows, rows), 1)
    same = doc_r == doc_c
    return [pos >= j for j in range(taps)], jnp.logical_and(same, row > col), jnp.logical_and(same, row >= col)


def mixer_forward(ends_ref, where_ref, x0_ref, x1_ref, x2_ref, x3_ref, gain_one_ref, wbeta_ref, taps_ref, gain_ref, *rest):
    w_refs = rest[:4], rest[4:8]
    out_refs, rest = rest[8:13], rest[13:]
    act_ref, p_ref, bl_ref, t_ref, u_ref, o_ref, on0_ref, on1_ref, w0, w1, sems = rest
    held = (w0, w1)
    seq = pl.program_id(0)

    loads = [pieces_of(w_refs[side], held[side], sems.at[side], where_ref) for side in (0, 1)]
    at_first(start_all, loads[:1])
    rows = x0_ref.shape[0]
    cols = on0_ref.shape[2]
    heads = cols // DK
    half = rows // 2
    count = taps_ref.shape[0]
    x = chosen(x0_ref, x1_ref, x2_ref, x3_ref).astype(F32)
    act = (x * lax.rsqrt(jnp.mean(x * x, axis=-1, keepdims=True) + 1e-06) * gain_one_ref[...]).astype(BF16)
    act_ref[0] = act
    projs = []
    for side in (0, 1):
        at_first(wait_all, loads[side : side + 1])
        if side == 0:
            at_first(start_all, loads[1:])
        proj = dot(act, flat(held[side][:, :, :, : 3 * cols]))
        p_ref[0, :, side * 3 * cols : (side + 1) * 3 * cols] = proj
        projs.append(proj)
    logit = dot(act, wbeta_ref[...], NT)
    bl_ref[0] = logit
    beta_all = jax.nn.sigmoid(logit)
    keeps, strict, causal = masks(ends_ref, seq, rows, count)
    gain = gain_ref[...]
    every = range(2 * heads)

    def part(kind, head):
        side, first = head // heads, kind * cols + (head % heads) * DK
        at = side * 3 * cols + first
        taps = [taps_ref[j : j + 1, at : at + DK] for j in range(count)]
        c = conv(projs[side][:, first : first + DK], taps, keeps)
        return c * jax.nn.sigmoid(c)

    def unit(u):
        return u * lax.rsqrt(jnp.sum(u * u, axis=-1, keepdims=True) + 1e-06)

    qs = [unit(part(0, head)).astype(BF16) for head in every]
    ks = [unit(part(1, head)).astype(BF16) for head in every]
    lowers = [jnp.where(strict, dot(ks[head], ks[head], NT), 0.0) * beta_all[:, head : head + 1] for head in every]
    blocks = inverses([block for lower in lowers for block in (lower[:half, :half], lower[half:, half:])], half)
    ons = []
    for head in every:
        v = part(2, head).astype(BF16)
        beta = beta_all[:, head : head + 1]
        top, low = blocks[2 * head], blocks[2 * head + 1]
        cross = -fine(low, fine(lowers[head][half:, :half], top))
        t_ref[0, head, :half, :half] = top
        t_ref[0, head, :half, half:] = jnp.zeros((half, half), F32)
        t_ref[0, head, half:, :half] = cross
        t_ref[0, head, half:, half:] = low
        target = v.astype(F32) * beta
        u_top = fine(top, target[:half])
        u_low = fine(cross, target[:half]) + fine(low, target[half:])
        u = jnp.concatenate([u_top, u_low], axis=0)
        u_ref[0, head] = u
        o = fine(jnp.where(causal, dot(qs[head], ks[head], NT), 0.0), u)
        o_ref[0, head] = o
        on = o * lax.rsqrt(jnp.mean(o * o, axis=-1, keepdims=True) + 1e-05) * gain
        ons.append(on.astype(BF16))
    on = jnp.concatenate(ons, axis=1)
    on0_ref[0] = on[:, :cols]
    on1_ref[0] = on[:, cols:]
    y = []
    for block in range(w0.shape[0]):
        parts = [dot(on[:, side * cols : (side + 1) * cols], flat(held[side][block, :, :, 3 * cols :])) for side in (0, 1)]
        y.append((parts[0] + parts[1]).astype(BF16))
    hand_out(seq, out_refs, jnp.concatenate(y, axis=1))


def mixer_backward(base, ends_ref, where_ref, dy0_ref, dy1_ref, x0_ref, x1_ref, p_ref, bl_ref, t_ref, u_ref, o_ref, wbeta_ref, taps_ref, gain_ref, *rest):
    w_refs = rest[:4], rest[4:8]
    refs = rest[8 : 11 + base // 2]
    rest = rest[8 + len(refs) :]
    dqkv0_ref, dqkv1_ref, dbl_ref, dtaps_ref, dgain_ref, dgain_one_ref, w0, w1, sems = rest
    held = (w0, w1)
    seq = pl.program_id(0)
    rows = dy0_ref.shape[0]
    cols = p_ref.shape[2] // 6
    heads = cols // DK
    count = taps_ref.shape[0]

    loads = [pieces_of(w_refs[side], held[side], sems.at[side], where_ref) for side in (0, 1)]
    at_first(start_all, loads[:1])

    @pl.when(seq == 0)
    def _():
        dtaps_ref[...] = jnp.zeros_like(dtaps_ref)
        dgain_ref[...] = jnp.zeros_like(dgain_ref)
        dgain_one_ref[...] = jnp.zeros_like(dgain_one_ref)

    dy = chosen(dy0_ref, dy1_ref)
    dons = []
    for side in (0, 1):
        at_first(wait_all, loads[side : side + 1])
        if side == 0:
            at_first(start_all, loads[1:])
        don = 0.0
        for block in range(w0.shape[0]):
            weight = flat(held[side][block, :, :, 3 * cols :])
            don = don + dot(dy[:, block * weight.shape[1] : (block + 1) * weight.shape[1]], weight, NT)
        dons.append(don)
    beta_all = jax.nn.sigmoid(bl_ref[0])
    keeps, strict, causal = masks(ends_ref, base + seq, rows, count)
    gain = gain_ref[...]
    lane = lax.broadcasted_iota(jnp.int32, (rows, DK), 1)
    dbl_total = jnp.zeros((rows, DK), F32)

    def taps_of(first):
        return [taps_ref[j : j + 1, first : first + DK] for j in range(count)]

    def conv_back(first, dc):
        p = p_ref[0, :, first : first + DK]
        taps = taps_of(first)
        dp = dc * taps[0]
        dtaps_ref[0:1, first : first + DK] += jnp.sum(dc * p, axis=0, keepdims=True)
        for j in range(1, count):
            kept = jnp.where(keeps[j], dc, 0.0)
            dp = dp + pltpu.roll(kept, rows - j, 0) * taps[j]
            dtaps_ref[j : j + 1, first : first + DK] += jnp.sum(kept * pltpu.roll(p, j, 0), axis=0, keepdims=True)
        return dp

    def parts(first):
        c = conv(p_ref[0, :, first : first + DK], taps_of(first), keeps)
        sigma = jax.nn.sigmoid(c)
        return c * sigma, sigma * (1.0 + c * (1.0 - sigma))

    def unit_back(u, norm, grad):
        return norm * grad - u * (norm * norm * norm * jnp.sum(u * grad, axis=-1, keepdims=True))

    grads = [[None] * (3 * heads) for _ in (0, 1)]
    for head in range(2 * heads):
        side, at = head // heads, head % heads
        firsts = [side * 3 * cols + kind * cols + at * DK for kind in range(3)]
        uq, slope_q = parts(firsts[0])
        uk, slope_k = parts(firsts[1])
        uv, slope_v = parts(firsts[2])
        norm_q = lax.rsqrt(jnp.sum(uq * uq, axis=-1, keepdims=True) + 1e-06)
        norm_k = lax.rsqrt(jnp.sum(uk * uk, axis=-1, keepdims=True) + 1e-06)
        q = (uq * norm_q).astype(BF16)
        k = (uk * norm_k).astype(BF16)
        v = uv.astype(BF16).astype(F32)
        beta = beta_all[:, head : head + 1]
        o = o_ref[0, head]
        don = dons[side][:, at * DK : (at + 1) * DK]
        r = lax.rsqrt(jnp.mean(o * o, axis=-1, keepdims=True) + 1e-05)
        scaled = don * gain
        dgain_ref[...] += jnp.sum(don * o * r, axis=0, keepdims=True)
        do = r * scaled - o * (r * r * r * jnp.mean(o * scaled, axis=-1, keepdims=True))
        u = u_ref[0, head]
        inner = dot(k, k, NT)
        scores = jnp.where(causal, dot(q, k, NT), 0.0)
        du = fine(scores, do, TN)
        dscores = jnp.where(causal, fine(do, u, NT), 0.0)
        dq = semi(dscores, k)
        dk = semi(dscores, q, TN)
        w = fine(t_ref[0, head], du, TN)
        dv = beta * w
        dlower = jnp.where(strict, fine(w, u, NT), 0.0)
        dbeta = jnp.sum(w * v, axis=-1, keepdims=True) - jnp.sum(dlower * inner, axis=-1, keepdims=True)
        dinner = dlower * beta
        dk = dk - semi(dinner, k) - semi(dinner, k, TN)
        dbl_total = jnp.where(lane == head, dbeta * beta * (1.0 - beta), dbl_total)
        grads[side][at] = conv_back(firsts[0], unit_back(uq, norm_q, dq) * slope_q).astype(BF16)
        grads[side][heads + at] = conv_back(firsts[1], unit_back(uk, norm_k, dk) * slope_k).astype(BF16)
        grads[side][2 * heads + at] = conv_back(firsts[2], dv * slope_v).astype(BF16)
    dbl = dbl_total.astype(BF16)
    dbl_ref[0] = dbl
    dact = dot(dbl, wbeta_ref[...])
    for side in (0, 1):
        dqkv = jnp.concatenate(grads[side], axis=1)
        (dqkv0_ref, dqkv1_ref)[side][0] = dqkv
        dact = dact + dot(dqkv, flat(held[side][:, :, :, : 3 * cols]), NT)
    x = chosen(x0_ref, x1_ref).astype(F32)
    normed = x * lax.rsqrt(jnp.mean(x * x, axis=-1, keepdims=True) + 1e-06)
    dgain_one_ref[...] += jnp.sum(dact * normed, axis=0, keepdims=True)
    dact = dact.astype(BF16)
    half = rows // 2

    @pl.when(seq == 0)
    def _():
        if base == 0:
            refs[0][...] = dact
        else:
            refs[0][...] = dact[:half]
            refs[1][...] = dact[half:]

    @pl.when(seq == 1)
    def _():
        refs[-2][...] = dact[:half]
        refs[-1][...] = dact[half:]


def hidden_units(where_ref, *rest):
    acts, dys, wgu_ref, wd_refs = rest[:4], rest[4:8], rest[8], (rest[9:13], rest[13:17])
    hid_refs, dgu_refs, wgu, wd, sems = rest[17:19], rest[19:21], rest[21:23], rest[23:25], rest[25]
    core = where_ref[4]
    loads = []
    for side, at in enumerate((core, 1 - core)):
        loads.append(pieces_of(wd_refs[side], wd[side], sems.at[2 + side], where_ref))
        loads.append(side_of(wgu_ref, at, wgu[side], sems.at[side]))
    at_first(start_all, loads[:2])
    hidden = hid_refs[0].shape[1]
    act = jnp.concatenate([chosen(acts[0], acts[2]), chosen(acts[1], acts[3])])
    dy = jnp.concatenate([chosen(dys[0], dys[2]), chosen(dys[1], dys[3])])
    for side in (0, 1):
        at_first(wait_all, loads[2 * side : 2 * side + 1])
        dhid = dot(dy, flat(wd[side][...]), NT)
        at_first(wait_all, loads[2 * side + 1 : 2 * side + 2])
        if side == 0:
            at_first(start_all, loads[2:])
        gu = dot(act, flat(wgu[side][...]))
        gt, up = gu[:, :hidden], gu[:, hidden:]
        sigma = jax.nn.sigmoid(gt)
        swish = gt * sigma
        hid_refs[side][...] = (swish * up).astype(BF16)
        dgt = (dhid * up * sigma * (1.0 + gt * (1.0 - sigma))).astype(BF16)
        dup = (dhid * swish).astype(BF16)
        dgu_refs[side][...] = jnp.concatenate([dgt, dup], axis=1)


def hidden_back(where_ref, dgu0_ref, dgu1_ref, wgu_ref, *rest):
    dact_refs, wgu, sems = rest[:5], rest[5:7], rest[7]
    step = pl.program_id(0)
    core = where_ref[4]
    loads = [side_of(wgu_ref, at, wgu[side], sems.at[side]) for side, at in enumerate((core, 1 - core))]
    at_first(start_all, loads[:1])
    dact = 0.0
    for side, dgu_ref in enumerate((dgu0_ref, dgu1_ref)):
        at_first(wait_all, loads[side : side + 1])
        if side == 0:
            at_first(start_all, loads[1:])
        dact = dact + dot(dgu_ref[...], flat(wgu[side][...]), NT)
    rows = dact.shape[0] // 2
    for part in (0, 1):
        hand_out(2 * step + part, dact_refs, dact[part * rows : (part + 1) * rows].astype(BF16))


def hidden_out(where_ref, hid0_ref, hid1_ref, *rest):
    wd_refs, out_refs, wd, sems = (rest[:4], rest[4:8]), rest[8:13], rest[13:15], rest[15]
    step = pl.program_id(0)
    loads = [pieces_of(wd_refs[side], wd[side], sems.at[side], where_ref) for side in (0, 1)]
    at_first(start_all, loads[:1])
    out = 0.0
    for side, hid_ref in enumerate((hid0_ref, hid1_ref)):
        at_first(wait_all, loads[side : side + 1])
        if side == 0:
            at_first(start_all, loads[1:])
        out = out + dot(hid_ref[...], flat(wd[side][...]))
    rows = out.shape[0] // 2
    for part in (0, 1):
        hand_out(2 * step + part, out_refs, out[part * rows : (part + 1) * rows].astype(BF16))


def gate_up_grads(where_ref, *rest):
    acts, dgus, out = rest[:4], (rest[4], rest[5]), rest[6]
    act = jnp.concatenate([ref[...] for ref in acts])
    rows = act.shape[1] // 4
    core = where_ref[4]
    for at, side in ((core, 0), (1 - core, 1)):
        value = dot(act, dgus[side][...], TN).astype(BF16)
        for n in range(4):
            out[n, at, 0] = value[n * rows : (n + 1) * rows]


def down_grads(where_ref, *rest):
    hids, dys, out = (rest[0], rest[1]), rest[2:6], rest[6]
    dy = jnp.concatenate([ref[...] for ref in dys])
    rows = hids[0].shape[1] // 4
    core = where_ref[4]
    for at, side in ((core, 0), (1 - core, 1)):
        value = dot(hids[side][...], dy, TN).astype(BF16)
        for n in range(4):
            out[n, at] = value[n * rows : (n + 1) * rows]


def mixer_grads(where_ref, act_ref, act2_ref, on_ref, on2_ref, dbl0_ref, dbl1_ref, *rest):
    dqkvs, dys, out_ref, beta_ref = rest[:4], rest[4:12], rest[12], rest[13]
    acts = act_ref[...], act2_ref[...]
    beta_ref[...] = dot(jnp.concatenate([dbl0_ref[...], dbl1_ref[...]]), acts[0], TN)
    tokens = dqkvs[0].shape[0]
    qkv = out = 0.0
    for core in (0, 1):
        for part in (0, 1):
            qkv = qkv + dot(acts[core][part * tokens : (part + 1) * tokens], dqkvs[2 * core + part][...], TN)
        dy = jnp.concatenate([ref[...] for ref in dys[4 * core : 4 * core + 4]])
        out = out + dot((on_ref, on2_ref)[core][...], dy, TN)
    value = jnp.concatenate([qkv, out], axis=1).astype(BF16)
    rows = value.shape[0] // 4
    for n in range(4):
        out_ref[n, 0] = value[n * rows : (n + 1) * rows]


def in_order(*refs):
    value, outs = refs[0], refs[1:]
    width = value.shape[2] // len(outs)
    for n, out in enumerate(outs):
        parts = [value[block, :, n * width : (n + 1) * width].astype(F32) for block in range(value.shape[0])]
        out[...] = jnp.concatenate(parts, axis=1)


def whole(shape):
    return pl.BlockSpec(shape, lambda i: (0,) * len(shape), pipeline_mode=pl.Buffered(1))


def each(shape):
    return pl.BlockSpec((1,) + shape, lambda i: (i,) + (0,) * len(shape))


PARAMS = pltpu.CompilerParams(vmem_limit_bytes=60 * 1024 * 1024, dimension_semantics=("arbitrary",))


def tie(*values):
    return lax.optimization_barrier(values)


def gather_group(own):
    return [own, lax.ppermute(own, "x", SWAP), lax.ppermute(own, "y", SWAP), lax.ppermute(own, ("y", "x"), ACROSS)]


def joined(left, right):
    return left.astype(F32) + right.astype(F32)


def sum_first(parts):
    own, by_x, by_y, x_low, y_top = parts
    return [lax.ppermute(by_x, "x", SWAP), lax.ppermute(by_y, "y", SWAP), own, x_low, y_top]


def sum_second(got_x, got_y, own, x_low, y_top):
    y_top = lax.ppermute(joined(y_top, got_x[1]).astype(BF16), "y", SWAP)
    x_low = lax.ppermute(joined(x_low, got_y[1]).astype(BF16), "x", SWAP)
    return [x_low, y_top, own, got_x, got_y]


def sum_last(x_low, y_top, own, got_x, got_y):
    half = x_low.shape[0]
    top = joined(own[:half], got_x[0]) + y_top.astype(F32)
    low = joined(own[half:], got_y[0]) + x_low.astype(F32)
    return jnp.concatenate([top, low])


def by_hand():
    return lax.axis_size("far") == 1 and lax.axis_size("narrow") == 4


def with_partner(pieces):
    return pieces, [lax.ppermute(piece, "c", SWAP) for piece in pieces]


def spread_first(mine):
    return [mine, lax.ppermute(mine, "narrow", NEAR), lax.ppermute(mine, "narrow", SKIP)]


def spread_last(mine, near, skip):
    return [mine, near, skip, lax.ppermute(mine, "narrow", MIDDLE), lax.ppermute(skip, "narrow", [(2, 3), (1, 0)])]


def all_four(mine, near, skip, middle, end):
    z = lax.axis_index("narrow")
    return [mine, near, skip, jnp.where((z == 1) | (z == 2), middle, end)]


def spread_columns(mine):
    far, narrow = lax.axis_size("far"), lax.axis_size("narrow")
    _, rows, columns = mine.shape
    full = lax.all_gather(mine, REST, axis=0).reshape(far, narrow, GROUP, rows, columns).transpose(0, 2, 1, 3, 4)
    return full.reshape(GROUP, 4, -1, columns)


def spread_rows(weight):
    full = lax.all_gather(weight, ALL, axis=0, tiled=True)
    total = full.shape[0] // GROUP
    return lax.dynamic_slice_in_dim(full, lax.axis_index(SLICES) * total, total, 0).reshape(4, -1, full.shape[1])


def collect_columns(full):
    columns = full.shape[-1]
    far, narrow = lax.axis_size("far"), lax.axis_size("narrow")
    full = full.transpose(1, 0, 2, 3).reshape(far, GROUP, narrow, -1, columns).transpose(0, 2, 1, 3, 4)
    full = lax.psum_scatter(full.reshape(-1, columns), REST, scatter_dimension=0, tiled=True)
    return full.reshape(GROUP, -1, columns).astype(F32)


def collect_rows(full):
    full = full.reshape(1, -1, full.shape[-1])
    full = jnp.where((jnp.arange(GROUP) == lax.axis_index(SLICES))[:, None, None], full, 0)
    return lax.psum_scatter(full.reshape(-1, full.shape[-1]), ALL, scatter_dimension=0, tiled=True).astype(F32)


def to_owners(mine):
    return lax.all_to_all(mine.astype(BF16), SLICES, 0, 0, tiled=True)


def gather_small(values, late):
    if not by_hand():
        shape = tuple(lax.axis_size(axis) for axis in ALL)
        return lax.all_gather(values, ALL, axis=0).reshape(shape + values.shape), late
    values = jnp.stack([values] + [lax.ppermute(values, "narrow", pairs) for pairs in (NEAR, SKIP, ACROSS)])
    values = jnp.stack([values, lax.ppermute(values, "c", SWAP)])
    values, late = tie(values, late)
    values = jnp.stack(gather_group(values))
    here = lax.axis_index(SLICES) * 4 + lax.axis_index("narrow")
    values = jnp.take(values.reshape((-1,) + values.shape[3:]), jnp.arange(32) ^ here, axis=0)
    return values.reshape((1, 2, 2, 2, 4) + values.shape[1:]), late


def sum_small(values, *others):
    if not by_hand():
        return lax.psum_scatter(values, ALL, scatter_dimension=0, tiled=False), *others
    later = list(others)
    z = lax.axis_index("narrow")
    values = values.reshape((2, 2, 2, 2, 2) + values.shape[1:])
    bits = [("c", SWAP, lax.axis_index("c"), 2), ("x", SWAP, lax.axis_index("x"), 1), ("y", SWAP, lax.axis_index("y"), 0), ("narrow", NEAR, z % 2, 1), ("narrow", SKIP, z // 2, 0)]
    for axis, pairs, bit, dim in bits:
        keep = lax.dynamic_index_in_dim(values, bit, dim, keepdims=False)
        send = lax.dynamic_index_in_dim(values, 1 - bit, dim, keepdims=False)
        values = keep + lax.ppermute(send, axis, pairs)
        if axis == "x":
            values, later[0], later[1] = tie(values, later[0], later[1])
        if axis == "y":
            values, *later = tie(values, *later)
    return values, *later


def anywhere():
    return pl.BlockSpec(memory_space=pl.ANY)


def scalars():
    return pl.BlockSpec(memory_space=pltpu.SMEM)


def once(shape):
    return pl.BlockSpec(shape, lambda i: (0,) * len(shape), pipeline_mode=pl.Buffered(1))


def held_like(piece):
    return pltpu.VMEM((piece.shape[0], 4) + piece.shape[1:], BF16)


def call(kernel, name, grid, inputs, in_specs, outs, scratch, microseconds):
    results = pl.pallas_call(
        kernel,
        grid=(grid,),
        in_specs=in_specs,
        out_specs=[spec for spec, _, _ in outs],
        out_shape=[jax.ShapeDtypeStruct(shape, kind) for _, shape, kind in outs],
        scratch_shapes=scratch,
        compiler_params=PARAMS,
        cost_estimate=pl.CostEstimate(flops=int(microseconds * 1e9), bytes_accessed=20_000_000, transcendentals=0),
        name=name,
    )(*inputs)
    return list(results)


def local(tokens, doc_lengths, gain_attn, w_query, w_key, w_value, w_beta, conv_query, conv_key, conv_value, gain_head, w_out, gain_ffn, w_gate, w_up, w_down, cotangent):
    x_low = tokens[0]
    dy_low = cotangent[0]
    length, width = x_low.shape
    heads = w_beta.shape[1]
    mine = heads // GROUP
    cols = mine * DK
    three = 3 * cols
    count = conv_query.shape[0]
    total = 4 * length
    y_at, x_at, c_at, z_at = [lax.axis_index(axis) for axis in ("y", "x", "c", "narrow")]
    me = lax.axis_index(SLICES)
    where = jnp.stack([z_at, z_at ^ 1, z_at ^ 2, z_at ^ 3] if by_hand() else [0, 1, 2, 3])
    chips = [(y_at ^ dy) * 2 + (x_at ^ dx) for dy in (0, 1) for dx in (0, 1)]
    where = jnp.append(where, c_at)

    def across(weights):
        rows = weights[0].shape[0]
        return jnp.concatenate([w.reshape(rows, GROUP, -1) for w in weights], axis=2).transpose(1, 0, 2)

    def to_slices(parts):
        return lax.all_to_all(parts, SLICES, 0, 0, tiled=True)

    def blocked(weight):
        return jnp.moveaxis(weight.reshape(weight.shape[:-1] + (GROUP, -1)), -2, 0)

    mixer_parts, gain_attn, gain_ffn, conv_query, conv_key, conv_value, w_beta, doc_lengths = tie(
        across((w_query, w_key, w_value)), gain_attn, gain_ffn, conv_query, conv_key, conv_value, w_beta, doc_lengths
    )
    lengths = jnp.pad(doc_lengths.astype(BF16), ((0, 0), (0, gain_attn.shape[0] - doc_lengths.shape[1])))
    small = jnp.concatenate([gain_attn[None], gain_ffn[None], conv_query, conv_key, conv_value, w_beta.T, lengths])
    mixer_mine = to_slices(mixer_parts)
    small, mixer_mine = gather_small(small, mixer_mine)
    x_low, small = tie(x_low, small)
    xs = gather_group(x_low)
    lengths = small[..., -1, : doc_lengths.shape[1]].astype(jnp.int32)
    lengths = lax.dynamic_index_in_dim(lengths, lax.axis_index("far"), 0, keepdims=False)
    lengths = lax.dynamic_index_in_dim(lengths, c_at, 2, keepdims=False)
    lengths = lax.dynamic_index_in_dim(lengths, z_at, 2, keepdims=False).reshape(4, -1)
    ends = jnp.cumsum(jnp.take(lengths, jnp.stack(chips), axis=0), axis=1)[:, :-1]
    wide = small.reshape((-1,) + small.shape[-2:]).transpose(1, 0, 2).reshape(small.shape[-2], width)
    gain_one = wide[0:1].astype(F32)
    gain_two = wide[1:2].astype(F32)
    pair = jnp.stack([me, me ^ 1])
    taps = jnp.take(wide[2 : 2 + 3 * count].reshape(3, count, GROUP, cols), pair, axis=2)
    taps = taps.transpose(1, 2, 0, 3).reshape(count, 2 * three).astype(F32)
    wbeta = jnp.take(wide[2 + 3 * count : -1].reshape(GROUP, mine, width), pair, axis=0).reshape(2 * mine, width)
    wbeta = jnp.pad(wbeta, ((0, DK - 2 * mine), (0, 0)))
    gain_h = gain_head.astype(F32)[None]

    hidden_mine = to_slices(across((w_gate, w_up)))
    if by_hand():
        mixer_w = spread_first(jnp.concatenate([mixer_mine, blocked(w_out)], axis=2))
        *mixer_w, xs[1], xs[2], xs[3], ends, gain_one, taps, wbeta = tie(*mixer_w, *xs[1:], ends, gain_one, taps, wbeta)
        mixer_w = all_four(*spread_last(*mixer_w))
        hidden_mine, w_down, *mixer_w = tie(hidden_mine, w_down, *mixer_w)
        down_w = spread_first(w_down[None])
        hidden_w = lax.all_gather(hidden_mine, ("c", "narrow"), axis=0).reshape((2, 4) + hidden_mine.shape)
    else:
        full = jnp.concatenate([spread_columns(mixer_mine), blocked(spread_rows(w_out))], axis=3)
        mixer_w = [full[:, n] for n in range(4)]
        full = spread_columns(hidden_mine).transpose(1, 0, 2, 3)
        other = lax.ppermute(full, "c", SWAP)
        hidden_w = jnp.stack([jnp.where(c_at == 0, full, other), jnp.where(c_at == 0, other, full)])
        full = spread_rows(w_down)[None]
        down_w = [full[:, n] for n in range(4)]
    mixer_w = with_partner(mixer_w)

    dy_low, mixer_w[1][3] = tie(dy_low, mixer_w[1][3])
    dys = gather_group(dy_low)
    half = length // 2
    row_spec = whole((length, width))
    sums = [(once(shape), shape, BF16) for shape in ((length, width), (2, half, width), (2, half, width), (half, width), (half, width))]
    kept = [((length, 2 * three), F32), ((length, DK), F32), ((2 * mine, length, length), F32), ((2 * mine, length, DK), F32), ((2 * mine, length, DK), F32)]
    constants = [whole((DK, width)), whole((count, 2 * three)), whole((1, DK))]
    mixer_held = [held_like(mixer_w[0][0]), held_like(mixer_w[0][0]), pltpu.SemaphoreType.DMA((2, 4))]
    shapes = [((length, width), BF16)] + kept + [((length, cols), BF16)] * 2
    results = call(
        mixer_forward,
        "mixer_forward",
        4,
        [ends, where] + xs + [gain_one, wbeta, taps, gain_h] + mixer_w[0] + mixer_w[1],
        [scalars(), scalars()] + [row_spec] * 4 + [whole((1, width))] + constants + [anywhere()] * 8,
        sums + [(each(shape), (4,) + shape, kind) for shape, kind in shapes],
        mixer_held,
        60,
    )
    y_parts, act, saved, ons = results[:5], results[5], results[6:-2], results[-2:]

    x = x_low.astype(F32)
    *rest, dys[1], dys[2], dys[3] = tie(*y_parts, *down_w, *dys[1:])
    y_parts, down_w = rest[:5], rest[5:]
    y_sum = sum_last(*sum_second(*sum_first(y_parts)))
    h1 = x + y_sum
    r2 = lax.rsqrt(jnp.mean(h1 * h1, axis=-1, keepdims=True) + 1e-06)
    act2 = (h1 * r2 * gain_two).astype(BF16)
    act2s = gather_group(act2)
    if by_hand():
        act2s[1], *down_w = tie(act2s[1], *spread_last(*down_w))
        down_w = all_four(*down_w)
    down_w = with_partner(down_w)

    hidden = down_w[0][0].shape[1] * 4
    def row_pairs(n):
        return pl.BlockSpec((2 * length, n), lambda i: (i, 0))

    held_gu, held_down = [held_like(hidden_w[0, 0])] * 2, [held_like(down_w[0][0])] * 2
    results = call(
        hidden_units,
        "hidden_units",
        2,
        [where] + act2s + dys + [hidden_w] + down_w[0] + down_w[1],
        [scalars()] + [row_spec] * 8 + [anywhere()] * 9,
        [(row_pairs(n), (total, n), BF16) for n in (hidden, hidden, 2 * hidden, 2 * hidden)],
        held_gu + held_down + [pltpu.SemaphoreType.DMA((4, 4))],
        30,
    )
    hids, dgus = results[:2], results[2:]

    block = width // GROUP
    columns_spec = pl.BlockSpec((length, block), lambda i: (0, i))
    def gate_up_half(at, turn):
        return call(
            gate_up_grads,
            "gate_up_grads",
            GROUP // 2,
            [turn] + act2s + dgus,
            [scalars()] + [pl.BlockSpec((length, block), lambda i: (0, i + at))] * 4 + [whole(dgu.shape) for dgu in dgus],
            [(pl.BlockSpec((4, 2, 1, block // 4, 2 * hidden), lambda i: (0, 0, i, 0, 0)), (4, 2, GROUP // 2, block // 4, 2 * hidden), BF16)],
            [],
            10,
        )[0]

    grad_gu = [gate_up_half(0, where)]
    *dgus, grad_gu[0] = tie(*dgus, grad_gu[0])
    dact2_parts = call(
        hidden_back,
        "hidden_back",
        2,
        [where] + dgus + [hidden_w],
        [scalars(), row_pairs(2 * hidden), row_pairs(2 * hidden), anywhere()],
        sums,
        held_gu + [pltpu.SemaphoreType.DMA((2, 4))],
        15,
    )
    sums2 = sum_first(dact2_parts)
    where, dact2_parts[0] = tie(where, dact2_parts[0])
    grad_gu.append(gate_up_half(GROUP // 2, where))
    sums2[0], sums2[1], grad_gu[1], where = tie(sums2[0], sums2[1], grad_gu[1], where)
    def down_part(at, blocks):
        spec = pl.BlockSpec((length, block), lambda i: (0, i + at))
        return call(
            down_grads,
            "down_grads",
            blocks,
            [where] + hids + dys,
            [scalars()] + [whole(hid.shape) for hid in hids] + [spec] * 4,
            [(pl.BlockSpec((4, 2, hidden // 4, block), lambda i: (0, 0, 0, i)), (4, 2, hidden // 4, blocks * block), BF16)],
            [],
            5,
        )[0]

    grad_second = sum_last(*sum_second(*sums2))
    scaled = grad_second * gain_two
    dh1 = dy_low.astype(F32) + r2 * scaled - h1 * (r2 * r2 * r2 * jnp.mean(h1 * scaled, axis=-1, keepdims=True))
    grad_gain_ffn = jnp.sum(grad_second * h1 * r2, axis=0)
    dy1 = dh1.astype(BF16)
    *dy1s, dy1_partner = tie(dy1, lax.ppermute(dy1, "x", SWAP), lax.ppermute(dy1, "y", SWAP), lax.ppermute(dy1, "c", SWAP))
    dy1s.append(lax.ppermute(dy1s[0], ("y", "x"), ACROSS))

    out_parts = call(
        hidden_out,
        "hidden_out",
        2,
        [where] + hids + down_w[0] + down_w[1],
        [scalars(), row_pairs(hidden), row_pairs(hidden)] + [anywhere()] * 8,
        sums,
        held_down + [pltpu.SemaphoreType.DMA((2, 4))],
        8,
    )
    where, out_parts[0] = tie(where, out_parts[0])
    grad_down = down_part(0, GROUP)
    if by_hand():
        grad_gu = [lax.psum_scatter(part.reshape(-1, 2 * hidden), ("narrow", "c"), scatter_dimension=0, tiled=True) for part in grad_gu]
    dy1s[0], dy1s[1], dy1s[2], grad_gu[0], grad_down = tie(*dy1s[:3], grad_gu[0], grad_down)
    if by_hand():
        grad_down = lax.psum_scatter(grad_down.reshape(-1, width), ("narrow", "c"), scatter_dimension=0, tiled=True)
    else:
        grad_gu = jnp.concatenate(grad_gu, axis=2)
        grad_gu = [lax.dynamic_index_in_dim(grad_gu, at, 1, keepdims=False) for at in (c_at, 1 - c_at)]
        grad_gu = joined(grad_gu[0], lax.ppermute(grad_gu[1], "c", SWAP)).astype(BF16)
        grad_gu = to_owners(collect_columns(grad_gu))

    def mixer_half(base, dys, xs, turn):
        def part(shape):
            return pl.BlockSpec((1,) + shape, lambda i: (i + base,) + (0,) * len(shape))

        whole_piece = [(once((length, width)), (length, width), BF16)]
        half_piece = [(once((half, width)), (half, width), BF16)]
        shapes = [((length, three), BF16)] * 2 + [((length, DK), BF16)]
        return call(
            partial(mixer_backward, base),
            "mixer_backward",
            2,
            [ends, turn] + dys + xs + saved + [wbeta, taps, gain_h] + mixer_w[0] + mixer_w[1],
            [scalars(), scalars()] + [row_spec] * 4 + [part(shape) for shape, _ in kept] + constants + [anywhere()] * 8,
            (half_piece * 4 if base else whole_piece + half_piece * 2)
            + [(each(shape), (2,) + shape, kind) for shape, kind in shapes]
            + [(once(shape), shape, F32) for shape in ((count, 2 * three), (1, DK), (1, width))],
            mixer_held,
            30,
        )

    act_partner, on_partner = [lax.ppermute(value, "c", SWAP) for value in (act, ons[1])]
    own, x_top, x_low, *first_half = mixer_half(0, dy1s[:2], xs[:2], where)
    partners = [dy1_partner] + [lax.ppermute(piece, "c", SWAP) for piece in dy1s[1:3]]
    *out_parts, partners[1], partners[2], act_partner, on_partner, dy1s[3], own, where = tie(
        *out_parts, *partners[1:], act_partner, on_partner, dy1s[3], own, where
    )
    partners.append(lax.ppermute(dy1s[3], "c", SWAP))
    dqkv_partner = [lax.ppermute(first_half[1], "c", SWAP)]
    y_top, y_low, far_top, far_low, *second_half = mixer_half(2, dy1s[2:], xs[2:], where)
    out_sums = sum_first(out_parts)
    if by_hand():
        rest = tie(out_sums[0], out_sums[1], grad_gu[1], far_top, partners[3], dqkv_partner[0], *second_half)
        out_sums[0], out_sums[1], grad_gu[1], far_top, partners[3], dqkv_partner[0], *second_half = rest
    dqkv_partner.append(lax.ppermute(second_half[1], "c", SWAP))
    far_top, far_low = lax.ppermute(far_top, "x", SWAP), lax.ppermute(far_low, "y", SWAP)
    dqkvs = [part.reshape(total // 2, three) for part in (first_half[0], second_half[0], *dqkv_partner)]
    dbls = [part[2].reshape(total // 2, DK) for part in (first_half, second_half)]
    dtaps, dgain, dgain_one = [first + second for first, second in zip(first_half[3:], second_half[3:])]
    grad_mixer, grad_wbeta = call(
        mixer_grads,
        "mixer_grads",
        GROUP,
        [where, act.reshape(total, width), act_partner.reshape(total, width)]
        + [ons[0].reshape(total, cols), on_partner.reshape(total, cols)]
        + dbls
        + dqkvs
        + dy1s
        + partners,
        [scalars()]
        + [pl.BlockSpec((total, block), lambda i: (0, i))] * 2
        + [whole((total, cols))] * 2
        + [whole((total // 2, DK))] * 2
        + [whole((total // 2, three))] * 4
        + [columns_spec] * 8,
        [(pl.BlockSpec((4, 1, block // 4, three + block), lambda i: (0, i, 0, 0)), (4, GROUP, block // 4, three + block), BF16)]
        + [(pl.BlockSpec((DK, block), lambda i: (0, i)), (DK, width), F32)],
        [],
        15,
    )
    if by_hand():
        grad_gu = to_owners(jnp.concatenate(grad_gu).reshape(GROUP, -1, 2 * hidden))
    far_top, far_low, x_top, y_low = tie(far_top, far_low, x_top, y_low)
    x_top, y_low, x_low, y_top = tie(lax.ppermute(x_top, "x", SWAP), lax.ppermute(y_low, "y", SWAP), x_low, y_top)
    total_out = sum_last(*sum_second(*out_sums))
    grad_act = sum_last(*sum_second([x_top, far_top], [y_low, far_low], own, x_low, y_top))
    if by_hand():
        grad_mixer = lax.psum_scatter(grad_mixer.reshape(-1, three + block), "narrow", scatter_dimension=0, tiled=True)
        grad_mixer = grad_mixer.reshape(GROUP, -1, three + block)
        grad_qkv, grad_out = grad_mixer[:, :, :three], grad_mixer[:, :, three:].transpose(1, 0, 2).reshape(-1, width).astype(F32)
    else:
        grad_qkv = collect_columns(grad_mixer[..., :three])
        grad_out = collect_rows(grad_mixer[..., three:].transpose(0, 2, 1, 3).reshape(4, -1, width))
        own, other = [lax.dynamic_index_in_dim(grad_down, at, 1, keepdims=False) for at in (c_at, 1 - c_at)]
        grad_down = collect_rows(joined(own, lax.ppermute(other, "c", SWAP)).astype(BF16))
    at = (jnp.arange(GROUP)[:, None] == pair[None, :]).astype(F32)
    dtaps = dtaps.reshape(count, 2, 3, cols)
    dtaps = (at[:, 0, None, None, None] * dtaps[None, :, 0] + at[:, 1, None, None, None] * dtaps[None, :, 1]).transpose(2, 1, 0, 3)
    dbeta = grad_wbeta[: 2 * mine].reshape(2, mine, width)
    dbeta = at[:, 0, None, None] * dbeta[None, 0] + at[:, 1, None, None] * dbeta[None, 1]
    smalls = jnp.concatenate([dgain_one, grad_gain_ffn[None], dtaps.reshape(3 * count, width), dbeta.reshape(heads, width)])
    smalls = smalls.reshape(smalls.shape[0], lax.axis_size(ALL), -1).transpose(1, 0, 2)
    dgain = jnp.broadcast_to(dgain.reshape(1, -1, smalls.shape[2]), (smalls.shape[0], DK // smalls.shape[2], smalls.shape[2]))
    smalls, grad_gu, grad_down, grad_act, total_out, grad_qkv = sum_small(
        jnp.concatenate([smalls, dgain], axis=1), grad_gu, grad_down, grad_act, total_out, grad_qkv
    )
    grad_qkv = to_owners(grad_qkv)
    r1 = lax.rsqrt(jnp.mean(x * x, axis=-1, keepdims=True) + 1e-06)
    scaled = grad_act * gain_one
    grad_input = (dh1 + r1 * scaled - x * (r1 * r1 * r1 * jnp.mean(x * scaled, axis=-1, keepdims=True))).astype(BF16)
    result = (h1 + total_out).astype(BF16)
    last_small = 2 + 3 * count + heads

    def columns(value, parts):
        outs = [(whole((value.shape[1], width_of)), (value.shape[1], width_of), F32) for width_of in [GROUP * value.shape[2] // parts] * parts]
        return call(in_order, "in_order", 1, [value], [whole(value.shape)], outs, [], 2)

    grad_query, grad_key, grad_value = columns(grad_qkv, 3)
    grad_gate, grad_up = columns(grad_gu, 2)
    return (
        result[None],
        grad_input[None],
        smalls[0],
        grad_query,
        grad_key,
        grad_value,
        smalls[2 + 3 * count : last_small].T,
        smalls[2 : 2 + count],
        smalls[2 + count : 2 + 2 * count],
        smalls[2 + 2 * count : 2 + 3 * count],
        smalls[last_small:].reshape(-1),
        grad_out,
        smalls[1],
        grad_gate,
        grad_up,
        grad_down.astype(F32),
    )


def solution(mesh):
    wide, narrow = mesh.shape["wide"], mesh.shape["narrow"]
    inner = Mesh(mesh.devices.reshape(wide // GROUP, 2, 2, 2, narrow), ALL)
    rows = P(ALL, None)
    columns = P(None, ALL)
    vector = P(ALL)
    cube = P(ALL, None, None)
    return jax.shard_map(
        local,
        mesh=inner,
        in_specs=(cube, rows, vector, rows, rows, rows, rows, columns, columns, columns, P(), rows, vector, rows, rows, rows, cube),
        out_specs=(cube, cube, vector, rows, rows, rows, rows, columns, columns, columns, P(), rows, vector, rows, rows, rows),
        check_vma=False,
    )
```
